128 devices in a mesh: adapter: 32 (over x, z, core), head: 4 (over y).
Axes of the slice: x: 4, y: 4, z: 4, core: 2. Of those that a mesh axis runs over, the one named last changes fastest.
Arguments:
- call_token_inputs: bfloat16 [1024, 32, 4096], P('adapter', None, 'head'), may hold values from -6 to 6
- routed_group_index: int32 [1024], replicated, may hold values from 0 to 31, as said below
- call_adapter_index: int32 [1024, 1], replicated, may hold values from 0 to 63
- holder_table_row: int32 [64], replicated, may hold values from 0 to 63, each once
- channel_input_weight: bfloat16 [4096, 4096], P(None, 'head'), may hold values from -0.09375 to 0.09375
- input_state_weight: bfloat16 [4096, 512], P(None, 'head'), may hold values from -0.09375 to 0.09375
- output_state_weight: bfloat16 [4096, 512], P(None, 'head'), may hold values from -0.09375 to 0.09375
- step_size_weight: bfloat16 [4096, 64], P(None, 'head'), may hold values from -0.09375 to 0.09375
- channel_input_taps: bfloat16 [4, 4096], P(None, 'head'), may hold values from -3 to 3
- input_state_taps: bfloat16 [4, 512], P(None, 'head'), may hold values from -3 to 3
- output_state_taps: bfloat16 [4, 512], P(None, 'head'), may hold values from -3 to 3
- adapter_down_weight: bfloat16 [64, 4096, 64], P('adapter', None, 'head'), may hold values from -0.09375 to 0.09375
- adapter_up_weight: bfloat16 [64, 64, 4096], P('adapter', None, 'head'), may hold values from -0.75 to 0.75
- decay_logarithm: float32 [64], P('head'), may hold values from -2.5 to 1.5
- step_size_bias: float32 [64], P('head'), may hold values from -2 to 0
- head_skip_factor: float32 [64], P('head'), may hold values from 0.5 to 1.5
Outputs:
- replies: bfloat16 [2048, 32, 4096], P('adapter', None, 'head')
The draws below stay inside these ranges and needn't reach their ends.
Inputs may be any that keep to these rules, and one draw needn't show every extreme that they name: `routed_group_index`: among the 32 calls of one source no group is named more than 2 times, and one group is named exactly 2 times by every source. `call_adapter_index`: every adapter is named by some call. `holder_table_row`: A permutation of 0 to 63.
All inputs are finite; a program needn't handle non-finite values.
Results may differ from the reference program's by a relative error of at most 0.0035.
Values may be sent and summed in bfloat16 or wider, within the bound.
A program may use at most 192 MiB of HBM per device.

```python
import jax
import jax.numpy as jnp
from jax import lax

MODEL_WIDTH = 4096
HEADS = 64
HEAD_DIM = 64
NSTATE = 128
CONV = 4
ADAPTER_RANK = 64
CAP = 2
LEN = 32
GROUP_SLOTS = 64
CALLS_DEV = 32
CALLS = 1024
ADAPTER_TOTAL = 64
INPUT_CHANNELS = 4096
GN = 512


def draw_routed_group_index(key, part):
    sender_indices = CALLS // CALLS_DEV
    group_lookup = jnp.arange(GROUP_SLOTS, dtype=jnp.int32) // CAP
    group_extra_score = jax.random.randint(jax.random.fold_in(key, 11), (sender_indices,), 0, 1 << 16, dtype=jnp.int32)
    busiest_group = jax.random.randint(jax.random.fold_in(key, 12), (), 0, sender_indices, dtype=jnp.int32)
    slot_extra_score = group_extra_score[group_lookup] + jnp.where(group_lookup == busiest_group, 1 << 20, 0).astype(jnp.int32)
    noise_amounts = jax.random.randint(jax.random.fold_in(key, 13), (sender_indices, GROUP_SLOTS), 0, 1 << 16, dtype=jnp.int32)
    routing_marks = (noise_amounts + slot_extra_score[None, :]) * GROUP_SLOTS + jnp.arange(GROUP_SLOTS, dtype=jnp.int32)[None, :]
    unused, picked = lax.top_k(routing_marks, CALLS_DEV)
    order_keys = jax.random.randint(jax.random.fold_in(key, 14), (sender_indices, CALLS_DEV), 0, 1 << 16, dtype=jnp.int32)
    order_keys = order_keys * CALLS_DEV + jnp.arange(CALLS_DEV, dtype=jnp.int32)[None, :]
    unused_too, shuffled_idx = lax.top_k(order_keys, CALLS_DEV)
    chosen = jnp.take_along_axis(picked, shuffled_idx, axis=1)
    return group_lookup[chosen].reshape(-1).astype(jnp.int32)


def level_of(key, extent, shards, least, largest):
    def one(dim, parts):
        steps = jax.random.uniform(jax.random.fold_in(jax.random.fold_in(key, 6), dim), (parts,), jnp.float32, least / len(shards), largest / len(shards))
        return jnp.repeat(jnp.exp(steps), extent[dim] // parts).reshape((-1,) + (1,) * (len(extent) - dim - 1))

    factor_of = one(*shards[0])
    for cut in shards[1:]:
        factor_of = factor_of * one(*cut)
    return factor_of


def choose_distinct(own_key, rows, count, top, lift):
    ranking = jax.random.permutation(jax.random.fold_in(own_key, 1), count)
    favour = ranking
    for power in range(3):
        favour = favour * favour // count
    favour = favour * lift // count
    lots = jax.random.randint(jax.random.fold_in(own_key, 2), (rows, count), 0, 4096) + favour
    holders = jax.random.permutation(jax.random.fold_in(own_key, 3), rows)[jnp.arange(count) % rows]
    lots = jnp.where(jnp.arange(rows)[:, None] == holders[None, :], 1 << 14, lots)
    score = lots * count + jnp.arange(count)
    return lax.top_k(score.astype(jnp.int32), top)[1].astype(jnp.int32)


def noise(stream_key, extent, width, limit, pieces=(), kind=jnp.bfloat16):
    factor_of = level_of(stream_key, extent, pieces, -0.22, 0.18) if pieces else 1.0
    entries = jax.random.normal(stream_key, extent, jnp.float32) * width * factor_of
    return jnp.minimum(jnp.maximum(entries, -limit), limit).astype(kind)


def setup_inputs(seed: int = 0) -> dict:
    streams_of = jax.random.split(jax.random.key(seed), 17)
    call_token_inputs = noise(streams_of[0], (CALLS, LEN, MODEL_WIDTH), 1.0, 6.0, ((0, 32), (2, 4)))
    routed_group_index = draw_routed_group_index(jax.random.fold_in(streams_of[16], 71), 0)
    call_adapter_index = choose_distinct(streams_of[2], CALLS, ADAPTER_TOTAL, 1, 256)
    holder_table_row = jax.random.permutation(streams_of[3], ADAPTER_TOTAL).astype(jnp.int32)
    channel_input_weight = noise(streams_of[4], (MODEL_WIDTH, INPUT_CHANNELS), MODEL_WIDTH ** -0.5, 0.09375, ((1, 4),))
    input_state_weight = noise(streams_of[5], (MODEL_WIDTH, GN), MODEL_WIDTH ** -0.5, 0.09375, ((1, 4),))
    output_state_weight = noise(streams_of[6], (MODEL_WIDTH, GN), MODEL_WIDTH ** -0.5, 0.09375, ((1, 4),))
    step_size_weight = noise(streams_of[7], (MODEL_WIDTH, HEADS), MODEL_WIDTH ** -0.5, 0.09375, ((1, 4),))
    channel_input_taps = noise(streams_of[8], (CONV, INPUT_CHANNELS), CONV ** -0.5, 3.0, ((1, 4),))
    input_state_taps = noise(streams_of[9], (CONV, GN), CONV ** -0.5, 3.0, ((1, 4),))
    output_state_taps = noise(streams_of[10], (CONV, GN), CONV ** -0.5, 3.0, ((1, 4),))
    adapter_down_weight = noise(streams_of[11], (ADAPTER_TOTAL, MODEL_WIDTH, ADAPTER_RANK), MODEL_WIDTH ** -0.5, 0.09375, ((0, 32), (2, 4)))
    adapter_up_weight = noise(streams_of[12], (ADAPTER_TOTAL, ADAPTER_RANK, INPUT_CHANNELS), ADAPTER_RANK ** -0.5, 0.75, ((0, 32), (2, 4)))
    decay_logarithm = jnp.clip(-2.5 + 4.0 * jax.random.uniform(streams_of[13], (HEADS,), jnp.float32) ** level_of(streams_of[13], (HEADS,), ((0, 4),), -0.2, 0.2), -2.5, 1.5)
    step_size_bias = jnp.clip(-2.0 + 2.0 * jax.random.uniform(streams_of[14], (HEADS,), jnp.float32) ** level_of(streams_of[14], (HEADS,), ((0, 4),), -0.2, 0.2), -2.0, 0.0)
    head_skip_factor = jnp.clip(0.5 + 1.0 * jax.random.uniform(streams_of[15], (HEADS,), jnp.float32) ** level_of(streams_of[15], (HEADS,), ((0, 4),), -0.2, 0.2), 0.5, 1.5)
    return dict(call_token_inputs=call_token_inputs, routed_group_index=routed_group_index, call_adapter_index=call_adapter_index, holder_table_row=holder_table_row, channel_input_weight=channel_input_weight, input_state_weight=input_state_weight, output_state_weight=output_state_weight, step_size_weight=step_size_weight, channel_input_taps=channel_input_taps, input_state_taps=input_state_taps, output_state_taps=output_state_taps, adapter_down_weight=adapter_down_weight, adapter_up_weight=adapter_up_weight, decay_logarithm=decay_logarithm, step_size_bias=step_size_bias, head_skip_factor=head_skip_factor)


PRECISE = lax.Precision.HIGHEST


def call_ranks(group_grid):
    count = group_grid.shape[-1]
    same_group = group_grid[..., :, None] == group_grid[..., None, :]
    earlier = jnp.arange(count)[None, :] < jnp.arange(count)[:, None]
    return jnp.sum(jnp.where(same_group & earlier, 1, 0), axis=-1).astype(jnp.int32)


def causal_filter_apply(series, kernel):
    span = kernel.shape[0]
    length = series.shape[1]
    padded = jnp.pad(series, ((0, 0), (span - 1, 0), (0, 0)))
    summed = jnp.zeros(series.shape, jnp.float32)
    for offset in range(span):
        summed = summed + kernel[offset].astype(jnp.float32) * padded[:, offset:offset + length, :]
    return jax.nn.silu(summed)


def state_space(filtered_inputs, b_conv, c_conv, dt_vals, decay_logarithm, head_skip_factor, call_token_length):
    blocks = filtered_inputs.shape[0]
    block_rows = filtered_inputs.shape[1]
    head_count = decay_logarithm.shape[0]
    group_count = b_conv.shape[2] // NSTATE
    x_heads = filtered_inputs.reshape(blocks, block_rows, head_count, HEAD_DIM)
    b_groups = b_conv.reshape(blocks, block_rows, group_count, NSTATE)
    c_groups = c_conv.reshape(blocks, block_rows, group_count, NSTATE)
    step_vals = -jnp.exp(decay_logarithm) * dt_vals
    cumulated = jnp.cumsum(jnp.moveaxis(step_vals, 2, 1), axis=2)
    row_iota = jnp.arange(block_rows)
    causal = (row_iota[:, None] // call_token_length == row_iota[None, :] // call_token_length) & (row_iota[None, :] <= row_iota[:, None])
    segment = cumulated[:, :, :, None] - cumulated[:, :, None, :]
    decay = jnp.where(causal, jnp.exp(jnp.where(causal, segment, 0.0)), 0.0)
    routing_marks = jnp.einsum("ntgk,njgk->ngtj", c_groups, b_groups, precision=PRECISE)
    routing_marks = jnp.repeat(routing_marks, head_count // group_count, axis=1)
    mixing = routing_marks * decay * jnp.moveaxis(dt_vals, 2, 1)[:, :, None, :]
    output = jnp.einsum("nhtj,njhp->nthp", mixing, x_heads, precision=PRECISE) + head_skip_factor[:, None] * x_heads
    return output.reshape(blocks, block_rows, head_count * HEAD_DIM)


def reference(call_token_inputs, routed_group_index, call_adapter_index, holder_table_row, channel_input_weight, input_state_weight, output_state_weight, step_size_weight, channel_input_taps, input_state_taps, output_state_taps, adapter_down_weight, adapter_up_weight, decay_logarithm, step_size_bias, head_skip_factor):
    sender_indices = CALLS // CALLS_DEV

    def one_source(inputs):
        sender_call_rows, source_ids = inputs
        token_places = holder_table_row[source_ids]
        down_weight_table = adapter_down_weight[token_places].astype(jnp.float32)
        up_weight_table = adapter_up_weight[token_places].astype(jnp.float32)
        reduced_features = jnp.einsum("ikp,ipm->ikm", sender_call_rows.astype(jnp.float32), down_weight_table).astype(jnp.bfloat16)
        flat_rows = sender_call_rows.reshape(CALLS_DEV * LEN, MODEL_WIDTH)

        def apply_projection(weight):
            return jnp.dot(flat_rows, weight, preferred_element_type=jnp.float32).reshape(CALLS_DEV, LEN, weight.shape[1])

        projected_inputs = apply_projection(channel_input_weight) + jnp.einsum("fza,fau->fzu", reduced_features.astype(jnp.float32), up_weight_table)
        filtered_inputs = causal_filter_apply(projected_inputs, channel_input_taps)
        b_conv = causal_filter_apply(apply_projection(input_state_weight), input_state_taps)
        c_conv = causal_filter_apply(apply_projection(output_state_weight), output_state_taps)
        dt_vals = jax.nn.softplus(apply_projection(step_size_weight) + step_size_bias)
        output = state_space(filtered_inputs, b_conv, c_conv, dt_vals, decay_logarithm, head_skip_factor, LEN)
        return output.astype(jnp.bfloat16)

    per_call = lax.map(one_source, (call_token_inputs.reshape(sender_indices, CALLS_DEV, LEN, MODEL_WIDTH), call_adapter_index[:, 0].reshape(sender_indices, CALLS_DEV)))
    group_grid = routed_group_index.reshape(sender_indices, CALLS_DEV)
    rank_grid = call_ranks(group_grid)
    source_iota = jnp.arange(sender_indices, dtype=jnp.int32)[:, None]
    target = (group_grid * GROUP_SLOTS + source_iota * CAP + rank_grid).reshape(-1).astype(jnp.int32)
    replies = jnp.zeros((GROUP_SLOTS * sender_indices, LEN, INPUT_CHANNELS), jnp.bfloat16)
    return replies.at[target].set(per_call.reshape(CALLS, LEN, INPUT_CHANNELS))
```

```python
import functools

import jax
import jax.numpy as jnp
from jax import lax
from jax.experimental import pallas as pl
from jax.experimental.pallas import tpu as pltpu
from jax.sharding import PartitionSpec as P

HEAD_DIM = 64
NSTATE = 128
CAP = 2
CHUNK = 4
PAD = 8
RING = 4
MESH = pl.DeviceIdType.MESH
HIGH = lax.Precision.HIGHEST
F32 = jnp.float32
BF16 = jnp.bfloat16

OFFSETS = (0, -1, 1, 2)
N_TABLE = 4 + 16 + 16


def nt_dot(a, b):
    return lax.dot_general(a, b, (((1,), (1,)), ((), ())), preferred_element_type=F32)


class Table:
    def __init__(self, buf, send, recv, first, second, core, strides, axes_to_adapter):
        self.buf, self.send, self.recv = buf, send, recv
        self.first, self.second, self.core = first, second, core
        self.strides = strides
        self.to_adapter = axes_to_adapter

    def owner(self, df, ds, core=None):
        core = self.core if core is None else core
        a = lax.rem(self.first + (df + RING), RING)
        b = lax.rem(self.second + (ds + RING), RING)
        return a * self.strides[0] + b * self.strides[1] + core

    def unit(self, df, ds, part=None, core=None):
        ref = self.buf.at[self.owner(df, ds, core)]
        return ref if part is None else ref.at[part]

    def copy(self, ref, index, target):
        return pltpu.make_async_remote_copy(
            src_ref=ref,
            dst_ref=ref,
            send_sem=self.send.at[index],
            recv_sem=self.recv.at[index],
            device_id={"adapter": target},
            device_id_type=MESH,
        )

    def plain(self, df):
        return 0 if df is None else 4 + 4 * OFFSETS.index(df)

    def send_plain(self, df):
        base = self.plain(df)
        if df is None:
            self.copy(self.unit(0, 0), base, self.owner(1, 0)).start()
            self.copy(self.unit(0, 0), base + 1, self.owner(-1, 0)).start()
        else:
            self.copy(self.unit(df, 0), base, self.owner(0, 1)).start()
            self.copy(self.unit(df, 0), base + 1, self.owner(0, -1)).start()

    def got_plain(self, df):
        base = self.plain(df)
        here = self.owner(0, 0)
        if df is None:
            self.copy(self.unit(-1, 0), base, here).wait_recv()
            self.copy(self.unit(1, 0), base + 1, here).wait_recv()
        else:
            self.copy(self.unit(df, -1), base, here).wait_recv()
            self.copy(self.unit(df, 1), base + 1, here).wait_recv()

    def send_relay(self, df):
        base = self.plain(df) + 2
        if df is None:
            self.copy(self.unit(-1, 0, 0), base, self.owner(1, 0)).start()
            self.copy(self.unit(1, 0, 1), base + 1, self.owner(-1, 0)).start()
        else:
            self.copy(self.unit(df, -1, 0), base, self.owner(0, 1)).start()
            self.copy(self.unit(df, 1, 1), base + 1, self.owner(0, -1)).start()

    def got_relay(self, df):
        base = self.plain(df) + 2
        here = self.owner(0, 0)
        at = (2, 0) if df is None else (df, 2)
        self.copy(self.unit(*at, 0), base, here).wait_recv()
        self.copy(self.unit(*at, 1), base + 1, here).wait_recv()

    def twin_index(self, df, ds):
        return 20 + 4 * OFFSETS.index(df) + OFFSETS.index(ds)

    def send_twin(self, df, ds):
        self.copy(
            self.unit(df, ds), self.twin_index(df, ds), self.owner(0, 0, 1 - self.core)
        ).start()

    def got_twins(self):
        here = self.owner(0, 0)
        for df in OFFSETS:
            for ds in OFFSETS:
                self.copy(
                    self.unit(df, ds, core=1 - self.core), self.twin_index(df, ds), here
                ).wait_recv()

    def sent_all(self):
        here = self.owner(0, 0)
        for df in (None, *OFFSETS):
            base = self.plain(df)
            for i in (0, 1):
                self.copy(self.unit(0, 0), base + i, here).wait_send()
                self.copy(self.unit(0, 0, 0), base + 2 + i, here).wait_send()
        for i in range(16):
            self.copy(self.unit(0, 0), 20 + i, here).wait_send()

    def event(self, number):
        if number == 0:
            self.send_plain(None)
            self.send_plain(0)
            self.send_twin(0, 0)
        elif number == 1:
            self.got_plain(None)
            self.send_relay(None)
            self.send_plain(-1)
            self.send_plain(1)
            self.got_plain(0)
            self.send_relay(0)
            for at in ((-1, 0), (1, 0), (0, -1), (0, 1)):
                self.send_twin(*at)
        elif number == 2:
            self.got_relay(None)
            self.send_plain(2)
            self.send_twin(2, 0)
            self.got_relay(0)
            self.send_twin(0, 2)
        elif number == 3:
            for df in (-1, 1):
                self.got_plain(df)
                self.send_relay(df)
                self.send_twin(df, -1)
                self.send_twin(df, 1)
        elif number == 4:
            self.got_plain(2)
            self.send_relay(2)
            self.send_twin(2, -1)
            self.send_twin(2, 1)
            for df in (-1, 1):
                self.got_relay(df)
                self.send_twin(df, 2)
        elif number == 5:
            self.got_relay(2)
            self.send_twin(2, 2)


N_EVENTS = 6


def mixer_kernel(
    meta,
    params,
    taps,
    skip,
    wdt_in,
    x_hbm,
    wx_hbm,
    wb_hbm,
    wc_hbm,
    down_hbm,
    up_hbm,
    out_hbm,
    x_in,
    x_all,
    w_all,
    wdt,
    down,
    up,
    proj,
    proj_dt,
    low,
    gathered,
    done,
    slots,
    load_sem,
    y_send,
    y_recv,
    table_send,
    table_recv,
    low_send,
    low_recv,
    out_send,
    out_recv,
):
    sources = lax.axis_size("adapter")
    me = lax.axis_index("adapter")
    y = lax.axis_index("head")
    calls, length, width = x_in.shape
    chunks = calls // CHUNK
    rows = CHUNK * length
    cols = wx_hbm.shape[1]
    half = CHUNK // 2
    right, left = lax.rem(y + 1, RING), lax.rem(y + RING - 1, RING)
    across = lax.rem(y + 2, RING)
    core = lax.rem(me, 2)
    pos_z = lax.rem(lax.div(me, 2), RING)
    pos_x = lax.div(me, 2 * RING)

    loads = [
        pltpu.make_async_copy(x_hbm, x_in, load_sem.at[0]),
        pltpu.make_async_copy(down_hbm, down.at[me], load_sem.at[1]),
        pltpu.make_async_copy(up_hbm, up.at[me], load_sem.at[2]),
        pltpu.make_async_copy(wx_hbm, w_all.at[:, pl.ds(0, cols)], load_sem.at[3]),
        pltpu.make_async_copy(wb_hbm, w_all.at[:, pl.ds(cols, NSTATE)], load_sem.at[4]),
        pltpu.make_async_copy(
            wc_hbm, w_all.at[:, pl.ds(cols + NSTATE, NSTATE)], load_sem.at[5]
        ),
    ]
    for load in loads:
        load.start()

    barrier = pltpu.get_barrier_semaphore()

    def greet(i, carry):
        pl.semaphore_signal(
            barrier,
            inc=1,
            device_id={"adapter": lax.rem(me + i, sources)},
            device_id_type=MESH,
        )
        return carry

    lax.fori_loop(1, sources, greet, 0)
    for d in range(1, RING):
        pl.semaphore_signal(
            barrier,
            inc=1,
            device_id={"head": lax.rem(y + d, RING)},
            device_id_type=MESH,
        )
    pl.semaphore_wait(barrier, sources - 1 + RING - 1)

    table_down = Table(
        down, table_send.at[0], table_recv.at[0], pos_x, pos_z, core, (2 * RING, 2), None
    )
    table_up = Table(
        up, table_send.at[1], table_recv.at[1], pos_z, pos_x, core, (2, 2 * RING), None
    )
    tables = (table_down, table_up)

    loads[1].wait()
    loads[2].wait()
    for table in tables:
        table.event(0)

    loads[0].wait()

    def arrange(j, carry):
        x_all[y, j] = x_in[meta[0, j]]
        return carry

    lax.fori_loop(0, calls, arrange, 0)

    def y_copy(kind, owner, k, target):
        if kind < 2:
            ref = x_all.at[owner, pl.ds(k * CHUNK, CHUNK)]
        else:
            ref = x_all.at[owner, pl.ds(k * CHUNK + (kind - 2) * half, half)]
        return pltpu.make_async_remote_copy(
            src_ref=ref,
            dst_ref=ref,
            send_sem=y_send.at[kind, k],
            recv_sem=y_recv.at[kind, k],
            device_id={"head": target},
            device_id_type=MESH,
        )

    def send_own(k):
        y_copy(0, y, k, right).start()
        y_copy(1, y, k, left).start()

    send_own(0)
    send_own(1)

    for k in range(chunks):
        for c in range(CHUNK):
            proj[k, c, pl.ds(0, PAD), :] = jnp.zeros((PAD, proj.shape[3]), F32)
    wdt[...] = jnp.zeros(wdt.shape, BF16)
    wdt[:, pl.ds(0, wdt_in.shape[1])] = wdt_in[...]
    loads[3].wait()
    loads[4].wait()
    loads[5].wait()

    def chunk_tokens(owner, k):
        return x_all[owner, pl.ds(k * CHUNK, CHUNK)].reshape(rows, width)

    tile = 256 if (cols + 2 * NSTATE) % 256 == 0 else 128

    def first_loop(k, carry):
        y_copy(0, left, k, y).wait_recv()
        y_copy(2, left, k, right).start()
        y_copy(1, right, k, y).wait_recv()
        y_copy(3, right, k, left).start()

        @pl.when(k + 2 < chunks)
        def _():
            send_own(k + 2)

        for number in range(1, N_EVENTS):

            @pl.when(k == number)
            def _(number=number):
                for table in tables:
                    table.event(number)

        y_copy(2, across, k, y).wait_recv()
        y_copy(3, across, k, y).wait_recv()

        @pl.loop(0, w_all.shape[1] // tile)
        def _(n):
            at = pl.ds(pl.multiple_of(n * tile, tile), tile)
            total = jnp.zeros((rows, tile), F32)
            for owner in range(RING):
                total = total + jnp.dot(
                    chunk_tokens(owner, k),
                    w_all[pl.ds(owner * width, width), at],
                    preferred_element_type=F32,
                )
            proj[k, :, pl.ds(PAD, length), at] = total.reshape(CHUNK, length, tile)

        total = jnp.zeros((rows, wdt.shape[1]), F32)
        for owner in range(RING):
            total = total + jnp.dot(
                chunk_tokens(owner, k),
                wdt[pl.ds(owner * width, width), :],
                preferred_element_type=F32,
            )
        proj_dt[k] = total
        return carry

    lax.fori_loop(0, chunks, first_loop, 0)

    for table in tables:
        table.got_twins()

    rank = down.shape[2]

    def low_copy(owner, d, k, target):
        ref = low.at[owner, k]
        return pltpu.make_async_remote_copy(
            src_ref=ref,
            dst_ref=ref,
            send_sem=low_send.at[d - 1, k],
            recv_sem=low_recv.at[d - 1, k],
            device_id={"head": target},
            device_id_type=MESH,
        )

    def down_loop(k, carry):
        for c in range(CHUNK):
            row = meta[1, k * CHUNK + c]
            gathered[pl.ds(c * rank, rank), :] = down[lax.div(row, 2), lax.rem(row, 2)]
        total = jnp.zeros((rows, CHUNK * rank), F32)
        for owner in range(RING):
            total = total + nt_dot(
                chunk_tokens(owner, k), gathered[:, pl.ds(owner * width, width)]
            )
        row_call = lax.broadcasted_iota(jnp.int32, total.shape, 0) // length
        lane_call = lax.broadcasted_iota(jnp.int32, total.shape, 1) // rank
        kept = jnp.where(row_call == lane_call, total, 0.0).astype(BF16)
        shape = (CHUNK * rank, low.shape[3])
        from_rank = lax.broadcasted_iota(jnp.int32, shape, 0) % rank + y * rank
        fold = jnp.where(
            from_rank == lax.broadcasted_iota(jnp.int32, shape, 1), 1.0, 0.0
        ).astype(BF16)
        low[y, k] = jnp.dot(kept, fold, preferred_element_type=F32).astype(BF16)
        for d in range(1, RING):
            low_copy(y, d, k, lax.rem(y + d, RING)).start()
        return carry

    lax.fori_loop(0, chunks, down_loop, 0)

    def out_copy(i, target, source):
        return pltpu.make_async_remote_copy(
            src_ref=slots.at[pl.ds(i * CAP, CAP)],
            dst_ref=out_hbm.at[pl.ds(source * CAP, CAP)],
            send_sem=out_send.at[i],
            recv_sem=out_recv.at[i],
            device_id={"adapter": target},
            device_id_type=MESH,
        )

    def fill(i):
        for r in range(CAP):
            at = i * CAP + r
            block = done[meta[2, at]].astype(F32)
            slots[at] = jnp.where(meta[3, at] > 0, block, 0.0).astype(BF16)

    def send_slots(i):
        fill(i)
        out_copy(i, lax.rem(me + i, sources), me).start()

    own = pltpu.make_async_copy(
        slots.at[pl.ds(0, CAP)], out_hbm.at[pl.ds(me * CAP, CAP)], load_sem.at[6]
    )

    decay_rate = -jnp.exp(params[0:1, :])
    bias = params[1:2, :]
    rank_all = up.shape[2]

    def conv(k, at):
        total = jnp.zeros((CHUNK, length, 128), F32)
        for i in range(4):
            total = total + taps[pl.ds(i, 1), at].reshape(1, 1, 128) * proj[
                k, :, pl.ds(PAD - 3 + i, length), at
            ]
        total = total.reshape(rows, 128)
        return total / (1.0 + jnp.exp(-total))

    def mix_loop(k, carry):
        for d in range(1, RING):
            low_copy(lax.rem(y + RING - d, RING), d, k, y).wait_recv()
        low_rank = (
            low[0, k].astype(F32)
            + low[1, k].astype(F32)
            + low[2, k].astype(F32)
            + low[3, k].astype(F32)
        ).astype(BF16)
        for c in range(CHUNK):
            row = meta[1, k * CHUNK + c]
            weight = up[lax.div(row, 2), lax.rem(row, 2)]
            delta = jnp.dot(
                low_rank[c * length : (c + 1) * length, :rank_all],
                weight,
                preferred_element_type=F32,
            )
            proj[k, c, pl.ds(PAD, length), pl.ds(0, cols)] = (
                proj[k, c, pl.ds(PAD, length), pl.ds(0, cols)] + delta
            )
        t_iota = lax.broadcasted_iota(jnp.int32, (rows, rows), 0)
        j_iota = lax.broadcasted_iota(jnp.int32, (rows, rows), 1)
        causal = (t_iota // length == j_iota // length) & (j_iota <= t_iota)
        raw = proj_dt[k] + bias
        dt = jnp.maximum(raw, 0.0) + jnp.log1p(jnp.exp(-jnp.abs(raw)))
        cum = jnp.dot(
            jnp.where(causal, 1.0, 0.0),
            decay_rate * dt,
            preferred_element_type=F32,
            precision=HIGH,
        )
        cum_t = cum.T
        dt_t = dt.T
        b_conv = conv(k, pl.ds(cols, NSTATE))
        c_conv = conv(k, pl.ds(cols + NSTATE, NSTATE))
        marks = lax.dot_general(
            c_conv,
            b_conv,
            (((1,), (1,)), ((), ())),
            preferred_element_type=F32,
            precision=HIGH,
        )
        lane = lax.broadcasted_iota(jnp.int32, (rows, 128), 1)
        for pair in range(cols // 128):
            at = pl.ds(pair * 128, 128)
            x_conv = conv(k, at)
            mixing = []
            for h in (2 * pair, 2 * pair + 1):
                segment = cum[:, h : h + 1] - cum_t[h : h + 1, :]
                decay = jnp.exp(jnp.where(causal, segment, -1e30))
                mixing.append((marks * decay * dt_t[h : h + 1, :]).astype(BF16))
            x_low = jnp.where(lane < HEAD_DIM, x_conv, 0.0).astype(BF16)
            x_high = jnp.where(lane < HEAD_DIM, 0.0, x_conv).astype(BF16)
            mixed = jnp.dot(
                jnp.concatenate(mixing, axis=1),
                jnp.concatenate([x_low, x_high], axis=0),
                preferred_element_type=F32,
            )
            mixed = mixed + skip[0:1, at] * x_conv
            done[pl.ds(k * CHUNK, CHUNK), :, at] = mixed.reshape(
                CHUNK, length, 128
            ).astype(BF16)

        @pl.when(k == 0)
        def _():
            fill(0)
            own.start()

        @pl.when(k > 0)
        def _():
            send_slots(2 * k)

        send_slots(2 * k + 1)
        return carry

    lax.fori_loop(0, chunks, mix_loop, 0)

    def rest_loop(i, carry):
        send_slots(i)
        return carry

    lax.fori_loop(calls // CAP, sources, rest_loop, 0)

    own.wait()
    for table in tables:
        table.sent_all()

    def drain(k, carry):
        for kind in range(4):
            y_copy(kind, y, k, y).wait_send()
        for d in range(1, RING):
            low_copy(y, d, k, y).wait_send()
        return carry

    lax.fori_loop(0, chunks, drain, 0)

    def drain_out(i, carry):
        out_copy(i, me, me).wait_send()
        out_copy(i, me, lax.rem(me + sources - i, sources)).wait_recv()
        return carry

    lax.fori_loop(1, sources, drain_out, 0)


def routing(routed_group_index, call_adapter_index, holder_table_row, me, sources, calls):
    group = lax.dynamic_slice(routed_group_index, (me * calls,), (calls,))
    named = lax.dynamic_slice(call_adapter_index[:, 0], (me * calls,), (calls,))
    call = jnp.arange(calls, dtype=jnp.int32)
    same = group[:, None] == group[None, :]
    rank = jnp.sum(jnp.where(same & (call[None, :] < call[:, None]), 1, 0), axis=1)
    key = lax.rem(group - me + sources, sources) * CAP + rank
    place = jnp.sum(jnp.where(key[None, :] < key[:, None], 1, 0), axis=1)
    row = jnp.sum(
        jnp.where(
            named[:, None] == jnp.arange(holder_table_row.shape[0], dtype=jnp.int32)[None, :],
            holder_table_row[None, :],
            0,
        ),
        axis=1,
    )
    slot = jnp.arange(sources * CAP, dtype=jnp.int32)
    here = place[None, :] == slot[:, None]
    order = jnp.sum(jnp.where(here, call[None, :], 0), axis=1)
    rows = jnp.sum(jnp.where(here, row[None, :], 0), axis=1)
    taken = jnp.sum(jnp.where(key[None, :] < slot[:, None], 1, 0), axis=1)
    live = jnp.sum(jnp.where(key[None, :] == slot[:, None], 1, 0), axis=1)
    return jnp.stack([order, rows, jnp.minimum(taken, calls - 1), live]).astype(jnp.int32)


def on_device(
    call_token_inputs,
    routed_group_index,
    call_adapter_index,
    holder_table_row,
    channel_input_weight,
    input_state_weight,
    output_state_weight,
    step_size_weight,
    channel_input_taps,
    input_state_taps,
    output_state_taps,
    adapter_down_weight,
    adapter_up_weight,
    decay_logarithm,
    step_size_bias,
    head_skip_factor,
):
    sources = lax.axis_size("adapter")
    me = lax.axis_index("adapter")
    calls, length, width = call_token_inputs.shape
    cols = channel_input_weight.shape[1]
    heads = decay_logarithm.shape[0]
    chunks = calls // CHUNK
    rows = CHUNK * length
    total_cols = cols + 2 * NSTATE
    meta = routing(
        routed_group_index, call_adapter_index, holder_table_row, me, sources, calls
    )
    params = jnp.stack([decay_logarithm, step_size_bias])
    params = jnp.pad(params, ((0, 6), (0, 128 - heads)))
    taps = jnp.concatenate(
        [channel_input_taps, input_state_taps, output_state_taps], axis=1
    ).astype(F32)
    skip = jnp.broadcast_to(head_skip_factor[:, None], (heads, HEAD_DIM)).reshape(1, cols)
    down = jnp.swapaxes(adapter_down_weight, 1, 2)
    per_owner, rank, depth = down.shape
    rank_all = adapter_up_weight.shape[1]
    vmem = pl.BlockSpec(memory_space=pltpu.VMEM)
    anywhere = pl.BlockSpec(memory_space=pl.ANY)
    dma = pltpu.SemaphoreType.DMA
    return pl.pallas_call(
        mixer_kernel,
        out_shape=jax.ShapeDtypeStruct((sources * CAP, length, cols), BF16),
        in_specs=[pl.BlockSpec(memory_space=pltpu.SMEM)] + [vmem] * 4 + [anywhere] * 6,
        out_specs=anywhere,
        scratch_shapes=[
            pltpu.VMEM((calls, length, width), BF16),
            pltpu.VMEM((RING, calls, length, width), BF16),
            pltpu.VMEM((depth, total_cols), BF16),
            pltpu.VMEM((depth, 128), BF16),
            pltpu.VMEM((sources, per_owner, rank, depth), BF16),
            pltpu.VMEM((sources, per_owner, rank_all, cols), BF16),
            pltpu.VMEM((chunks, CHUNK, PAD + length, total_cols), F32),
            pltpu.VMEM((chunks, rows, 128), F32),
            pltpu.VMEM((RING, chunks, rows, 128), BF16),
            pltpu.VMEM((CHUNK * rank, depth), BF16),
            pltpu.VMEM((calls, length, cols), BF16),
            pltpu.VMEM((sources * CAP, length, cols), BF16),
            dma((7,)),
            dma((4, chunks)),
            dma((4, chunks)),
            dma((2, N_TABLE)),
            dma((2, N_TABLE)),
            dma((RING - 1, chunks)),
            dma((RING - 1, chunks)),
            dma((sources,)),
            dma((sources,)),
        ],
        compiler_params=pltpu.CompilerParams(
            collective_id=0, has_side_effects=True, vmem_limit_bytes=60 * 2**20
        ),
        cost_estimate=pl.CostEstimate(
            flops=2 * calls * length * depth * (total_cols + 128),
            bytes_accessed=30 * 2**20,
            transcendentals=calls * length * rows * heads,
        ),
    )(
        meta,
        params,
        taps,
        skip,
        step_size_weight,
        call_token_inputs,
        channel_input_weight,
        input_state_weight,
        output_state_weight,
        down,
        adapter_up_weight,
    )


def solution(mesh):
    placed = (
        P("adapter", None, "head"),
        P(),
        P(),
        P(),
        P(None, "head"),
        P(None, "head"),
        P(None, "head"),
        P(None, "head"),
        P(None, "head"),
        P(None, "head"),
        P(None, "head"),
        P("adapter", None, "head"),
        P("adapter", None, "head"),
        P("head"),
        P("head"),
        P("head"),
    )
    return jax.shard_map(
        on_device, mesh=mesh, in_specs=placed, out_specs=P("adapter", None, "head"), check_vma=False
    )
```

```python
import functools

import jax
import jax.numpy as jnp
from jax import lax
from jax.experimental import pallas as pl
from jax.experimental.pallas import tpu as pltpu
from jax.sharding import PartitionSpec as P

HEAD_DIM = 64
NSTATE = 128
CAP = 2
CHUNK = 4
PAD = 8
RING = 4
MESH = pl.DeviceIdType.MESH
HIGH = lax.Precision.HIGHEST
F32 = jnp.float32
BF16 = jnp.bfloat16

OFFSETS = (0, -1, 1, 2)
N_TABLE = 4 + 16 + 16

CHIP_STEPS = (
    (2, 1), (1, 2), (2, 3), (3, 2), (2, 2), (2, 0), (0, 2), (1, 1),
    (3, 3), (1, 3), (3, 1), (1, 0), (0, 1), (3, 0), (0, 3), (0, 0),
)
STEPS = tuple((dx, dz, dc) for dx, dz in CHIP_STEPS for dc in (0, 1))
TABLES_AT = 5


def nt_dot(a, b):
    return lax.dot_general(a, b, (((1,), (1,)), ((), ())), preferred_element_type=F32)


class Table:
    def __init__(self, buf, send, recv, first, second, core, strides, axes_to_adapter):
        self.buf, self.send, self.recv = buf, send, recv
        self.first, self.second, self.core = first, second, core
        self.strides = strides
        self.to_adapter = axes_to_adapter

    def owner(self, df, ds, core=None):
        core = self.core if core is None else core
        a = lax.rem(self.first + (df + RING), RING)
        b = lax.rem(self.second + (ds + RING), RING)
        return a * self.strides[0] + b * self.strides[1] + core

    def unit(self, df, ds, part=None, core=None):
        ref = self.buf.at[self.owner(df, ds, core)]
        return ref if part is None else ref.at[part]

    def copy(self, ref, index, target):
        return pltpu.make_async_remote_copy(
            src_ref=ref,
            dst_ref=ref,
            send_sem=self.send.at[index],
            recv_sem=self.recv.at[index],
            device_id={"adapter": target},
            device_id_type=MESH,
        )

    def plain(self, df):
        return 0 if df is None else 4 + 4 * OFFSETS.index(df)

    def send_plain(self, df):
        base = self.plain(df)
        if df is None:
            self.copy(self.unit(0, 0), base, self.owner(1, 0)).start()
            self.copy(self.unit(0, 0), base + 1, self.owner(-1, 0)).start()
        else:
            self.copy(self.unit(df, 0), base, self.owner(0, 1)).start()
            self.copy(self.unit(df, 0), base + 1, self.owner(0, -1)).start()

    def got_plain(self, df):
        base = self.plain(df)
        here = self.owner(0, 0)
        if df is None:
            self.copy(self.unit(-1, 0), base, here).wait_recv()
            self.copy(self.unit(1, 0), base + 1, here).wait_recv()
        else:
            self.copy(self.unit(df, -1), base, here).wait_recv()
            self.copy(self.unit(df, 1), base + 1, here).wait_recv()

    def send_relay(self, df):
        base = self.plain(df) + 2
        if df is None:
            self.copy(self.unit(-1, 0, 0), base, self.owner(1, 0)).start()
            self.copy(self.unit(1, 0, 1), base + 1, self.owner(-1, 0)).start()
        else:
            self.copy(self.unit(df, -1, 0), base, self.owner(0, 1)).start()
            self.copy(self.unit(df, 1, 1), base + 1, self.owner(0, -1)).start()

    def got_relay(self, df):
        base = self.plain(df) + 2
        here = self.owner(0, 0)
        at = (2, 0) if df is None else (df, 2)
        self.copy(self.unit(*at, 0), base, here).wait_recv()
        self.copy(self.unit(*at, 1), base + 1, here).wait_recv()

    def twin_index(self, df, ds):
        return 20 + 4 * OFFSETS.index(df) + OFFSETS.index(ds)

    def send_twin(self, df, ds):
        self.copy(
            self.unit(df, ds), self.twin_index(df, ds), self.owner(0, 0, 1 - self.core)
        ).start()

    def got_twins(self):
        here = self.owner(0, 0)
        for df in OFFSETS:
            for ds in OFFSETS:
                self.copy(
                    self.unit(df, ds, core=1 - self.core), self.twin_index(df, ds), here
                ).wait_recv()

    def sent_all(self):
        here = self.owner(0, 0)
        for df in (None, *OFFSETS):
            base = self.plain(df)
            for i in (0, 1):
                self.copy(self.unit(0, 0), base + i, here).wait_send()
                self.copy(self.unit(0, 0, 0), base + 2 + i, here).wait_send()
        for i in range(16):
            self.copy(self.unit(0, 0), 20 + i, here).wait_send()

    def event(self, number):
        if number == 0:
            self.send_plain(None)
            self.send_plain(0)
            self.send_twin(0, 0)
        elif number == 1:
            self.got_plain(None)
            self.send_relay(None)
            self.send_plain(-1)
            self.send_plain(1)
            self.got_plain(0)
            self.send_relay(0)
            for at in ((-1, 0), (1, 0), (0, -1), (0, 1)):
                self.send_twin(*at)
        elif number == 2:
            self.got_relay(None)
            self.send_plain(2)
            self.send_twin(2, 0)
            self.got_relay(0)
            self.send_twin(0, 2)
        elif number == 3:
            for df in (-1, 1):
                self.got_plain(df)
                self.send_relay(df)
                self.send_twin(df, -1)
                self.send_twin(df, 1)
        elif number == 4:
            self.got_plain(2)
            self.send_relay(2)
            self.send_twin(2, -1)
            self.send_twin(2, 1)
            for df in (-1, 1):
                self.got_relay(df)
                self.send_twin(df, 2)
        elif number == 5:
            self.got_relay(2)
            self.send_twin(2, 2)


N_EVENTS = 6


def mixer_kernel(
    meta,
    params,
    taps,
    skip,
    wdt_in,
    x_hbm,
    wx_hbm,
    wb_hbm,
    wc_hbm,
    down_hbm,
    up_hbm,
    out_hbm,
    x_in,
    x_all,
    w_all,
    wdt,
    down,
    up,
    proj,
    between,
    mixing,
    low,
    gathered,
    slots,
    load_sem,
    y_send,
    y_recv,
    table_send,
    table_recv,
    low_send,
    low_recv,
    out_send,
    out_recv,
):
    sources = lax.axis_size("adapter")
    me = lax.axis_index("adapter")
    y = lax.axis_index("head")
    calls, length, width = x_in.shape
    chunks = calls // CHUNK
    rows = CHUNK * length
    cols = wx_hbm.shape[1]
    half = CHUNK // 2
    right, left = lax.rem(y + 1, RING), lax.rem(y + RING - 1, RING)
    across = lax.rem(y + 2, RING)
    core = lax.rem(me, 2)
    pos_z = lax.rem(lax.div(me, 2), RING)
    pos_x = lax.div(me, 2 * RING)

    loads = [
        pltpu.make_async_copy(x_hbm, x_in, load_sem.at[0]),
        pltpu.make_async_copy(down_hbm, down.at[me], load_sem.at[1]),
        pltpu.make_async_copy(up_hbm, up.at[me], load_sem.at[2]),
        pltpu.make_async_copy(wx_hbm, w_all.at[:, pl.ds(0, cols)], load_sem.at[3]),
        pltpu.make_async_copy(wb_hbm, w_all.at[:, pl.ds(cols, NSTATE)], load_sem.at[4]),
        pltpu.make_async_copy(
            wc_hbm, w_all.at[:, pl.ds(cols + NSTATE, NSTATE)], load_sem.at[5]
        ),
    ]
    for load in loads:
        load.start()

    barrier = pltpu.get_barrier_semaphore()

    def greet(i, carry):
        pl.semaphore_signal(
            barrier,
            inc=1,
            device_id={"adapter": lax.rem(me + i, sources)},
            device_id_type=MESH,
        )
        return carry

    lax.fori_loop(1, sources, greet, 0)
    for d in range(1, RING):
        pl.semaphore_signal(
            barrier,
            inc=1,
            device_id={"head": lax.rem(y + d, RING)},
            device_id_type=MESH,
        )
    pl.semaphore_wait(barrier, sources - 1 + RING - 1)

    table_down = Table(
        down, table_send.at[0], table_recv.at[0], pos_x, pos_z, core, (2 * RING, 2), None
    )
    table_up = Table(
        up, table_send.at[1], table_recv.at[1], pos_z, pos_x, core, (2, 2 * RING), None
    )
    tables = (table_down, table_up)

    loads[1].wait()
    loads[2].wait()
    for table in tables:
        table.event(0)

    loads[0].wait()

    def arrange(j, carry):
        x_all[y, j] = x_in[meta[0, j]]
        return carry

    lax.fori_loop(0, calls, arrange, 0)

    def y_copy(kind, owner, k, target):
        if kind < 2:
            ref = x_all.at[owner, pl.ds(k * CHUNK, CHUNK)]
        else:
            ref = x_all.at[owner, pl.ds(k * CHUNK + (kind - 2) * half, half)]
        return pltpu.make_async_remote_copy(
            src_ref=ref,
            dst_ref=ref,
            send_sem=y_send.at[kind, k],
            recv_sem=y_recv.at[kind, k],
            device_id={"head": target},
            device_id_type=MESH,
        )

    def send_own(k):
        y_copy(0, y, k, right).start()
        y_copy(1, y, k, left).start()

    send_own(0)
    send_own(1)

    for c in range(CHUNK):
        between[c, pl.ds(0, PAD), :] = jnp.zeros((PAD, 2 * NSTATE), F32)
        for k in range(chunks):
            proj[k, c, pl.ds(0, PAD), :] = jnp.zeros((PAD, cols), F32)
    wdt[...] = jnp.zeros(wdt.shape, BF16)
    wdt[:, pl.ds(0, wdt_in.shape[1])] = wdt_in[...]
    loads[3].wait()
    loads[4].wait()
    loads[5].wait()

    done = x_in
    rank = down.shape[2]
    rank_all = up.shape[2]
    decay_rate = -jnp.exp(params[0:1, :])
    bias = params[1:2, :]

    def chunk_tokens(owner, k):
        return x_all[owner, pl.ds(k * CHUNK, CHUNK)].reshape(rows, width)

    def project(k, weight, at):
        total = None
        for owner in range(RING):
            term = jnp.dot(
                chunk_tokens(owner, k),
                weight[pl.ds(owner * width, width), at],
                preferred_element_type=F32,
            )
            total = term if total is None else total + term
        return total

    def conv(series, at, taps_at):
        total = jnp.zeros((CHUNK, length, 128), F32)
        for i in range(4):
            total = total + taps[pl.ds(i, 1), taps_at].reshape(1, 1, 128) * series[
                :, pl.ds(PAD - 3 + i, length), at
            ]
        total = total.reshape(rows, 128)
        return total / (1.0 + jnp.exp(-total))

    def before_adapters(k):
        tile = 256 if cols % 256 == 0 else 128

        @pl.loop(0, cols // tile)
        def _(n):
            at = pl.ds(pl.multiple_of(n * tile, tile), tile)
            proj[k, :, pl.ds(PAD, length), at] = project(k, w_all, at).reshape(
                CHUNK, length, tile
            )

        between[:, pl.ds(PAD, length), :] = project(
            k, w_all, pl.ds(cols, 2 * NSTATE)
        ).reshape(CHUNK, length, 2 * NSTATE)
        raw = project(k, wdt, slice(None)) + bias
        t_iota = lax.broadcasted_iota(jnp.int32, (rows, rows), 0)
        j_iota = lax.broadcasted_iota(jnp.int32, (rows, rows), 1)
        causal = (t_iota // length == j_iota // length) & (j_iota <= t_iota)
        dt = jnp.maximum(raw, 0.0) + jnp.log1p(jnp.exp(-jnp.abs(raw)))
        cum = jnp.dot(
            jnp.where(causal, 1.0, 0.0),
            decay_rate * dt,
            preferred_element_type=F32,
            precision=HIGH,
        )
        cum_t = cum.T
        dt_t = dt.T
        b_conv = conv(between, pl.ds(0, NSTATE), pl.ds(cols, NSTATE))
        c_conv = conv(between, pl.ds(NSTATE, NSTATE), pl.ds(cols + NSTATE, NSTATE))
        marks = lax.dot_general(
            c_conv,
            b_conv,
            (((1,), (1,)), ((), ())),
            preferred_element_type=F32,
            precision=HIGH,
        )
        for h in range(cols // HEAD_DIM):
            segment = cum[:, h : h + 1] - cum_t[h : h + 1, :]
            decay = jnp.exp(jnp.where(causal, segment, -1e30))
            mixing[k, h // 2, :, pl.ds((h % 2) * rows, rows)] = (
                marks * decay * dt_t[h : h + 1, :]
            ).astype(BF16)

    def low_copy(owner, d, k, target):
        ref = low.at[owner, k]
        return pltpu.make_async_remote_copy(
            src_ref=ref,
            dst_ref=ref,
            send_sem=low_send.at[d - 1, k],
            recv_sem=low_recv.at[d - 1, k],
            device_id={"head": target},
            device_id_type=MESH,
        )

    def reduce_chunk(k, carry):
        for c in range(CHUNK):
            row = meta[1, k * CHUNK + c]
            gathered[pl.ds(c * rank, rank), :] = down[lax.div(row, 2), lax.rem(row, 2)]
        total = jnp.zeros((rows, CHUNK * rank), F32)
        for owner in range(RING):
            total = total + nt_dot(
                chunk_tokens(owner, k), gathered[:, pl.ds(owner * width, width)]
            )
        row_call = lax.broadcasted_iota(jnp.int32, total.shape, 0) // length
        lane_call = lax.broadcasted_iota(jnp.int32, total.shape, 1) // rank
        kept = jnp.where(row_call == lane_call, total, 0.0).astype(BF16)
        shape = (CHUNK * rank, low.shape[3])
        from_rank = lax.broadcasted_iota(jnp.int32, shape, 0) % rank + y * rank
        fold = jnp.where(
            from_rank == lax.broadcasted_iota(jnp.int32, shape, 1), 1.0, 0.0
        ).astype(BF16)
        low[y, k] = jnp.dot(kept, fold, preferred_element_type=F32).astype(BF16)
        for d in range(1, RING):
            low_copy(y, d, k, lax.rem(y + d, RING)).start()
        return carry

    def at_step(i, sign):
        dx, dz, dc = STEPS[i]
        return (
            lax.rem(pos_x + (sign * dx) % RING, RING) * (2 * RING)
            + lax.rem(pos_z + (sign * dz) % RING, RING) * 2
            + lax.rem(core + dc, 2)
        )

    def out_copy(i, target, source):
        return pltpu.make_async_remote_copy(
            src_ref=slots.at[pl.ds(i * CAP, CAP)],
            dst_ref=out_hbm.at[pl.ds(source * CAP, CAP)],
            send_sem=out_send.at[i],
            recv_sem=out_recv.at[i],
            device_id={"adapter": target},
            device_id_type=MESH,
        )

    at_home = STEPS.index((0, 0, 0))
    own = pltpu.make_async_copy(
        slots.at[pl.ds(at_home * CAP, CAP)],
        out_hbm.at[pl.ds(me * CAP, CAP)],
        load_sem.at[6],
    )

    def send_slots(i):
        for r in range(CAP):
            at = i * CAP + r
            block = done[meta[2, at]].astype(F32)
            slots[at] = jnp.where(meta[3, at] > 0, block, 0.0).astype(BF16)
        if i == at_home:
            own.start()
        else:
            out_copy(i, at_step(i, 1), me).start()

    def after_adapters(k, carry):
        for d in range(1, RING):
            low_copy(lax.rem(y + RING - d, RING), d, k, y).wait_recv()
        low_rank = (
            low[0, k].astype(F32)
            + low[1, k].astype(F32)
            + low[2, k].astype(F32)
            + low[3, k].astype(F32)
        ).astype(BF16)
        for c in range(CHUNK):
            row = meta[1, k * CHUNK + c]
            weight = up[lax.div(row, 2), lax.rem(row, 2)]
            delta = jnp.dot(
                low_rank[c * length : (c + 1) * length, :rank_all],
                weight,
                preferred_element_type=F32,
            )
            proj[k, c, pl.ds(PAD, length), :] = proj[k, c, pl.ds(PAD, length), :] + delta
        lane = lax.broadcasted_iota(jnp.int32, (rows, 128), 1)
        for pair in range(cols // 128):
            at = pl.ds(pair * 128, 128)
            x_conv = conv(proj.at[k], at, at)
            x_high = x_conv.astype(BF16)
            mixed = skip[0:1, at] * x_conv
            for part in (x_high.astype(F32), x_conv - x_high.astype(F32)):
                first = jnp.where(lane < HEAD_DIM, part, 0.0).astype(BF16)
                second = jnp.where(lane < HEAD_DIM, 0.0, part).astype(BF16)
                mixed = mixed + jnp.dot(
                    mixing[k, pair],
                    jnp.concatenate([first, second], axis=0),
                    preferred_element_type=F32,
                )
            done[pl.ds(k * CHUNK, CHUNK), :, at] = mixed.reshape(
                CHUNK, length, 128
            ).astype(BF16)
        for number in range(chunks):

            @pl.when(k == number)
            def _(number=number):
                for i in range(CHUNK // CAP):
                    send_slots(number * (CHUNK // CAP) + i)

        return carry

    last = chunks - 1

    def step(k, carry):
        y_copy(0, left, k, y).wait_recv()
        y_copy(2, left, k, right).start()
        y_copy(1, right, k, y).wait_recv()
        y_copy(3, right, k, left).start()

        @pl.when(k + 2 < chunks)
        def _():
            send_own(k + 2)

        for number in range(1, N_EVENTS):

            @pl.when(k == number)
            def _(number=number):
                for table in tables:
                    table.event(number)

        lax.fori_loop(4, jnp.where(k == last, last - 1, 4), after_adapters, 0)
        y_copy(2, across, k, y).wait_recv()
        y_copy(3, across, k, y).wait_recv()
        before_adapters(k)

        @pl.when(k == TABLES_AT)
        def _():
            for table in tables:
                table.got_twins()

        lax.fori_loop(
            jnp.where(k == TABLES_AT, 0, k), jnp.where(k >= TABLES_AT, k + 1, k), reduce_chunk, 0
        )
        lax.fori_loop(
            jnp.where(k == last, last - 1, 0),
            jnp.where(k == last, chunks, jnp.where(k == last - 1, 4, 0)),
            after_adapters,
            0,
        )
        return carry

    lax.fori_loop(0, chunks, step, 0)

    for i in range(calls // CAP, sources):
        send_slots(i)

    own.wait()
    for table in tables:
        table.sent_all()

    def drain(k, carry):
        for kind in range(4):
            y_copy(kind, y, k, y).wait_send()
        for d in range(1, RING):
            low_copy(y, d, k, y).wait_send()
        return carry

    lax.fori_loop(0, chunks, drain, 0)
    for i in range(sources):
        if i != at_home:
            out_copy(i, me, me).wait_send()
            out_copy(i, me, at_step(i, -1)).wait_recv()


def routing(routed_group_index, call_adapter_index, holder_table_row, me, sources, calls):
    group = lax.dynamic_slice(routed_group_index, (me * calls,), (calls,))
    named = lax.dynamic_slice(call_adapter_index[:, 0], (me * calls,), (calls,))
    call = jnp.arange(calls, dtype=jnp.int32)
    same = group[:, None] == group[None, :]
    rank = jnp.sum(jnp.where(same & (call[None, :] < call[:, None]), 1, 0), axis=1)
    way = (
        lax.rem(group // (2 * RING) - me // (2 * RING) + RING, RING) * (2 * RING)
        + lax.rem((group // 2) % RING - (me // 2) % RING + RING, RING) * 2
        + lax.rem(group % 2 + me % 2, 2)
    )
    step_ways = jnp.array([dx * 2 * RING + dz * 2 + dc for dx, dz, dc in STEPS], jnp.int32)
    step = jnp.sum(
        jnp.where(
            way[:, None] == step_ways[None, :], jnp.arange(sources, dtype=jnp.int32)[None, :], 0
        ),
        axis=1,
    )
    key = step * CAP + rank
    place = jnp.sum(jnp.where(key[None, :] < key[:, None], 1, 0), axis=1)
    row = jnp.sum(
        jnp.where(
            named[:, None] == jnp.arange(holder_table_row.shape[0], dtype=jnp.int32)[None, :],
            holder_table_row[None, :],
            0,
        ),
        axis=1,
    )
    slot = jnp.arange(sources * CAP, dtype=jnp.int32)
    here = place[None, :] == slot[:, None]
    order = jnp.sum(jnp.where(here, call[None, :], 0), axis=1)
    rows = jnp.sum(jnp.where(here, row[None, :], 0), axis=1)
    taken = jnp.sum(jnp.where(key[None, :] < slot[:, None], 1, 0), axis=1)
    live = jnp.sum(jnp.where(key[None, :] == slot[:, None], 1, 0), axis=1)
    return jnp.stack([order, rows, jnp.minimum(taken, calls - 1), live]).astype(jnp.int32)


def on_device(
    call_token_inputs,
    routed_group_index,
    call_adapter_index,
    holder_table_row,
    channel_input_weight,
    input_state_weight,
    output_state_weight,
    step_size_weight,
    channel_input_taps,
    input_state_taps,
    output_state_taps,
    adapter_down_weight,
    adapter_up_weight,
    decay_logarithm,
    step_size_bias,
    head_skip_factor,
):
    sources = lax.axis_size("adapter")
    me = lax.axis_index("adapter")
    calls, length, width = call_token_inputs.shape
    cols = channel_input_weight.shape[1]
    heads = decay_logarithm.shape[0]
    chunks = calls // CHUNK
    rows = CHUNK * length
    total_cols = cols + 2 * NSTATE
    meta = routing(
        routed_group_index, call_adapter_index, holder_table_row, me, sources, calls
    )
    params = jnp.stack([decay_logarithm, step_size_bias])
    params = jnp.pad(params, ((0, 6), (0, 128 - heads)))
    taps = jnp.concatenate(
        [channel_input_taps, input_state_taps, output_state_taps], axis=1
    ).astype(F32)
    skip = jnp.broadcast_to(head_skip_factor[:, None], (heads, HEAD_DIM)).reshape(1, cols)
    down = jnp.swapaxes(adapter_down_weight, 1, 2)
    per_owner, rank, depth = down.shape
    rank_all = adapter_up_weight.shape[1]
    vmem = pl.BlockSpec(memory_space=pltpu.VMEM)
    anywhere = pl.BlockSpec(memory_space=pl.ANY)
    dma = pltpu.SemaphoreType.DMA
    return pl.pallas_call(
        mixer_kernel,
        out_shape=jax.ShapeDtypeStruct((sources * CAP, length, cols), BF16),
        in_specs=[pl.BlockSpec(memory_space=pltpu.SMEM)] + [vmem] * 4 + [anywhere] * 6,
        out_specs=anywhere,
        scratch_shapes=[
            pltpu.VMEM((calls, length, width), BF16),
            pltpu.VMEM((RING, calls, length, width), BF16),
            pltpu.VMEM((depth, total_cols), BF16),
            pltpu.VMEM((depth, 128), BF16),
            pltpu.VMEM((sources, per_owner, rank, depth), BF16),
            pltpu.VMEM((sources, per_owner, rank_all, cols), BF16),
            pltpu.VMEM((chunks, CHUNK, PAD + length, cols), F32),
            pltpu.VMEM((CHUNK, PAD + length, 2 * NSTATE), F32),
            pltpu.VMEM((chunks, cols // 128, rows, 2 * rows), BF16),
            pltpu.VMEM((RING, chunks, rows, 128), BF16),
            pltpu.VMEM((CHUNK * rank, depth), BF16),
            pltpu.VMEM((sources * CAP, length, cols), BF16),
            dma((7,)),
            dma((4, chunks)),
            dma((4, chunks)),
            dma((2, N_TABLE)),
            dma((2, N_TABLE)),
            dma((RING - 1, chunks)),
            dma((RING - 1, chunks)),
            dma((sources,)),
            dma((sources,)),
        ],
        compiler_params=pltpu.CompilerParams(
            collective_id=0, has_side_effects=True, vmem_limit_bytes=60 * 2**20
        ),
        cost_estimate=pl.CostEstimate(
            flops=2 * calls * length * depth * (total_cols + 128),
            bytes_accessed=30 * 2**20,
            transcendentals=calls * length * rows * heads,
        ),
    )(
        meta,
        params,
        taps,
        skip,
        step_size_weight,
        call_token_inputs,
        channel_input_weight,
        input_state_weight,
        output_state_weight,
        down,
        adapter_up_weight,
    )


def solution(mesh):
    placed = (
        P("adapter", None, "head"),
        P(),
        P(),
        P(),
        P(None, "head"),
        P(None, "head"),
        P(None, "head"),
        P(None, "head"),
        P(None, "head"),
        P(None, "head"),
        P(None, "head"),
        P("adapter", None, "head"),
        P("adapter", None, "head"),
        P("head"),
        P("head"),
        P("head"),
    )
    return jax.shard_map(
        on_device, mesh=mesh, in_specs=placed, out_specs=P("adapter", None, "head"), check_vma=False
    )
```

```python
import functools

import jax
import jax.numpy as jnp
from jax import lax
from jax.experimental import pallas as pl
from jax.experimental.pallas import tpu as pltpu
from jax.sharding import PartitionSpec as P

HEAD_DIM = 64
NSTATE = 128
CAP = 2
CHUNK = 4
PAD = 8
RING = 4
MESH = pl.DeviceIdType.MESH
HIGH = lax.Precision.HIGHEST
F32 = jnp.float32
BF16 = jnp.bfloat16

OFFSETS = (0, -1, 1, 2)
N_TABLE = 4 + 16 + 16

CHIP_STEPS = (
    ((2, 1), (2, 3), (1, 2), (3, 2)),
    ((2, 2), (2, 0), (0, 2)),
    ((1, 1), (3, 3), (1, 3), (3, 1)),
    ((1, 0), (3, 0), (0, 1), (0, 3)),
    ((0, 0),),
)
STEPS = tuple((dx, dz, dc) for group in CHIP_STEPS for dc in (1, 0) for dx, dz in group)
TABLES_AT = 6


def nt_dot(a, b):
    return lax.dot_general(a, b, (((1,), (1,)), ((), ())), preferred_element_type=F32)


class Table:
    def __init__(self, buf, send, recv, first, second, core, strides, axes_to_adapter):
        self.buf, self.send, self.recv = buf, send, recv
        self.first, self.second, self.core = first, second, core
        self.strides = strides
        self.to_adapter = axes_to_adapter

    def owner(self, df, ds, core=None):
        core = self.core if core is None else core
        a = lax.rem(self.first + (df + RING), RING)
        b = lax.rem(self.second + (ds + RING), RING)
        return a * self.strides[0] + b * self.strides[1] + core

    def unit(self, df, ds, part=None, core=None):
        ref = self.buf.at[self.owner(df, ds, core)]
        return ref if part is None else ref.at[part]

    def copy(self, ref, index, target):
        return pltpu.make_async_remote_copy(
            src_ref=ref,
            dst_ref=ref,
            send_sem=self.send.at[index],
            recv_sem=self.recv.at[index],
            device_id={"adapter": target},
            device_id_type=MESH,
        )

    def plain(self, df):
        return 0 if df is None else 4 + 4 * OFFSETS.index(df)

    def send_plain(self, df):
        base = self.plain(df)
        if df is None:
            self.copy(self.unit(0, 0), base, self.owner(1, 0)).start()
            self.copy(self.unit(0, 0), base + 1, self.owner(-1, 0)).start()
        else:
            self.copy(self.unit(df, 0), base, self.owner(0, 1)).start()
            self.copy(self.unit(df, 0), base + 1, self.owner(0, -1)).start()

    def got_plain(self, df):
        base = self.plain(df)
        here = self.owner(0, 0)
        if df is None:
            self.copy(self.unit(-1, 0), base, here).wait_recv()
            self.copy(self.unit(1, 0), base + 1, here).wait_recv()
        else:
            self.copy(self.unit(df, -1), base, here).wait_recv()
            self.copy(self.unit(df, 1), base + 1, here).wait_recv()

    def send_relay(self, df):
        base = self.plain(df) + 2
        if df is None:
            self.copy(self.unit(-1, 0, 0), base, self.owner(1, 0)).start()
            self.copy(self.unit(1, 0, 1), base + 1, self.owner(-1, 0)).start()
        else:
            self.copy(self.unit(df, -1, 0), base, self.owner(0, 1)).start()
            self.copy(self.unit(df, 1, 1), base + 1, self.owner(0, -1)).start()

    def got_relay(self, df):
        base = self.plain(df) + 2
        here = self.owner(0, 0)
        at = (2, 0) if df is None else (df, 2)
        self.copy(self.unit(*at, 0), base, here).wait_recv()
        self.copy(self.unit(*at, 1), base + 1, here).wait_recv()

    def twin_index(self, df, ds):
        return 20 + 4 * OFFSETS.index(df) + OFFSETS.index(ds)

    def send_twin(self, df, ds):
        self.copy(
            self.unit(df, ds), self.twin_index(df, ds), self.owner(0, 0, 1 - self.core)
        ).start()

    def got_twins(self):
        here = self.owner(0, 0)
        for df in OFFSETS:
            for ds in OFFSETS:
                self.copy(
                    self.unit(df, ds, core=1 - self.core), self.twin_index(df, ds), here
                ).wait_recv()

    def sent_all(self):
        here = self.owner(0, 0)
        for df in (None, *OFFSETS):
            base = self.plain(df)
            for i in (0, 1):
                self.copy(self.unit(0, 0), base + i, here).wait_send()
                self.copy(self.unit(0, 0, 0), base + 2 + i, here).wait_send()
        for i in range(16):
            self.copy(self.unit(0, 0), 20 + i, here).wait_send()

    def event(self, number):
        if number == 0:
            self.send_plain(None)
            self.send_plain(0)
            self.send_twin(0, 0)
        elif number == 1:
            self.got_plain(None)
            self.send_relay(None)
            self.send_plain(-1)
            self.send_plain(1)
            self.got_plain(0)
            self.send_relay(0)
            for at in ((-1, 0), (1, 0), (0, -1), (0, 1)):
                self.send_twin(*at)
        elif number == 2:
            self.got_relay(None)
            self.send_plain(2)
            self.send_twin(2, 0)
            self.got_relay(0)
            self.send_twin(0, 2)
        elif number == 3:
            for df in (-1, 1):
                self.got_plain(df)
                self.send_relay(df)
                self.send_twin(df, -1)
                self.send_twin(df, 1)
        elif number == 4:
            self.got_plain(2)
            self.send_relay(2)
            self.send_twin(2, -1)
            self.send_twin(2, 1)
            for df in (-1, 1):
                self.got_relay(df)
                self.send_twin(df, 2)
        elif number == 5:
            self.got_relay(2)
            self.send_twin(2, 2)


N_EVENTS = 6


def mixer_kernel(
    meta,
    params,
    taps,
    skip,
    wdt_in,
    x_hbm,
    wx_hbm,
    wb_hbm,
    wc_hbm,
    down_hbm,
    up_hbm,
    out_hbm,
    x_in,
    x_all,
    w_all,
    wdt,
    down,
    up,
    proj,
    between,
    mixing,
    low,
    gathered,
    slots,
    load_sem,
    y_send,
    y_recv,
    table_send,
    table_recv,
    low_send,
    low_recv,
    out_send,
    out_recv,
):
    sources = lax.axis_size("adapter")
    me = lax.axis_index("adapter")
    y = lax.axis_index("head")
    calls, length, width = x_in.shape
    chunks = calls // CHUNK
    rows = CHUNK * length
    cols = wx_hbm.shape[1]
    half = CHUNK // 2
    right, left = lax.rem(y + 1, RING), lax.rem(y + RING - 1, RING)
    across = lax.rem(y + 2, RING)
    core = lax.rem(me, 2)
    pos_z = lax.rem(lax.div(me, 2), RING)
    pos_x = lax.div(me, 2 * RING)

    loads = [
        pltpu.make_async_copy(x_hbm, x_in, load_sem.at[0]),
        pltpu.make_async_copy(down_hbm, down.at[me], load_sem.at[1]),
        pltpu.make_async_copy(up_hbm, up.at[me], load_sem.at[2]),
        pltpu.make_async_copy(wx_hbm, w_all.at[:, pl.ds(0, cols)], load_sem.at[3]),
        pltpu.make_async_copy(wb_hbm, w_all.at[:, pl.ds(cols, NSTATE)], load_sem.at[4]),
        pltpu.make_async_copy(
            wc_hbm, w_all.at[:, pl.ds(cols + NSTATE, NSTATE)], load_sem.at[5]
        ),
    ]
    for load in loads:
        load.start()

    barrier = pltpu.get_barrier_semaphore()

    def greet(i, carry):
        pl.semaphore_signal(
            barrier,
            inc=1,
            device_id={"adapter": lax.rem(me + i, sources)},
            device_id_type=MESH,
        )
        return carry

    lax.fori_loop(1, sources, greet, 0)
    for d in range(1, RING):
        pl.semaphore_signal(
            barrier,
            inc=1,
            device_id={"head": lax.rem(y + d, RING)},
            device_id_type=MESH,
        )
    pl.semaphore_wait(barrier, sources - 1 + RING - 1)

    table_down = Table(
        down, table_send.at[0], table_recv.at[0], pos_x, pos_z, core, (2 * RING, 2), None
    )
    table_up = Table(
        up, table_send.at[1], table_recv.at[1], pos_z, pos_x, core, (2, 2 * RING), None
    )
    tables = (table_down, table_up)

    loads[1].wait()
    loads[2].wait()
    for table in tables:
        table.event(0)

    loads[0].wait()

    def arrange(j, carry):
        x_all[y, j] = x_in[meta[0, j]]
        return carry

    lax.fori_loop(0, calls, arrange, 0)

    def y_copy(kind, owner, k, target):
        if kind < 2:
            ref = x_all.at[owner, pl.ds(k * CHUNK, CHUNK)]
        else:
            ref = x_all.at[owner, pl.ds(k * CHUNK + (kind - 2) * half, half)]
        return pltpu.make_async_remote_copy(
            src_ref=ref,
            dst_ref=ref,
            send_sem=y_send.at[kind, k],
            recv_sem=y_recv.at[kind, k],
            device_id={"head": target},
            device_id_type=MESH,
        )

    def send_own(k):
        y_copy(0, y, k, right).start()
        y_copy(1, y, k, left).start()

    send_own(0)
    send_own(1)

    for c in range(CHUNK):
        between[c, pl.ds(0, PAD), :] = jnp.zeros((PAD, 2 * NSTATE), F32)
        for k in range(chunks):
            proj[k, c, pl.ds(0, PAD), :] = jnp.zeros((PAD, cols), F32)
    wdt[...] = jnp.zeros(wdt.shape, BF16)
    wdt[:, pl.ds(0, wdt_in.shape[1])] = wdt_in[...]
    loads[3].wait()
    loads[4].wait()
    loads[5].wait()

    done = x_in
    rank = down.shape[2]
    rank_all = up.shape[2]
    decay_rate = -jnp.exp(params[0:1, :])
    bias = params[1:2, :]

    def chunk_tokens(owner, k):
        return x_all[owner, pl.ds(k * CHUNK, CHUNK)].reshape(rows, width)

    def project(k, weight, at):
        total = None
        for owner in range(RING):
            term = jnp.dot(
                chunk_tokens(owner, k),
                weight[pl.ds(owner * width, width), at],
                preferred_element_type=F32,
            )
            total = term if total is None else total + term
        return total

    def conv(series, at, taps_at):
        total = jnp.zeros((CHUNK, length, 128), F32)
        for i in range(4):
            total = total + taps[pl.ds(i, 1), taps_at].reshape(1, 1, 128) * series[
                :, pl.ds(PAD - 3 + i, length), at
            ]
        total = total.reshape(rows, 128)
        return total / (1.0 + jnp.exp(-total))

    def before_adapters(k):
        tile = 256 if cols % 256 == 0 else 128

        @pl.loop(0, cols // tile)
        def _(n):
            at = pl.ds(pl.multiple_of(n * tile, tile), tile)
            proj[k, :, pl.ds(PAD, length), at] = project(k, w_all, at).reshape(
                CHUNK, length, tile
            )

        between[:, pl.ds(PAD, length), :] = project(
            k, w_all, pl.ds(cols, 2 * NSTATE)
        ).reshape(CHUNK, length, 2 * NSTATE)
        raw = project(k, wdt, slice(None)) + bias
        t_iota = lax.broadcasted_iota(jnp.int32, (rows, rows), 0)
        j_iota = lax.broadcasted_iota(jnp.int32, (rows, rows), 1)
        causal = (t_iota // length == j_iota // length) & (j_iota <= t_iota)
        dt = jnp.maximum(raw, 0.0) + jnp.log1p(jnp.exp(-jnp.abs(raw)))
        cum = jnp.dot(
            jnp.where(causal, 1.0, 0.0),
            decay_rate * dt,
            preferred_element_type=F32,
            precision=HIGH,
        )
        cum_t = cum.T
        dt_t = dt.T
        b_conv = conv(between, pl.ds(0, NSTATE), pl.ds(cols, NSTATE))
        c_conv = conv(between, pl.ds(NSTATE, NSTATE), pl.ds(cols + NSTATE, NSTATE))
        marks = lax.dot_general(
            c_conv,
            b_conv,
            (((1,), (1,)), ((), ())),
            preferred_element_type=F32,
            precision=HIGH,
        )
        for h in range(cols // HEAD_DIM):
            segment = cum[:, h : h + 1] - cum_t[h : h + 1, :]
            decay = jnp.exp(jnp.where(causal, segment, -1e30))
            mixing[k, h // 2, :, pl.ds((h % 2) * rows, rows)] = (
                marks * decay * dt_t[h : h + 1, :]
            ).astype(BF16)

    def low_copy(owner, d, k, target):
        ref = low.at[owner, k]
        return pltpu.make_async_remote_copy(
            src_ref=ref,
            dst_ref=ref,
            send_sem=low_send.at[d - 1, k],
            recv_sem=low_recv.at[d - 1, k],
            device_id={"head": target},
            device_id_type=MESH,
        )

    def reduce_chunk(k, carry):
        for c in range(CHUNK):
            row = meta[1, k * CHUNK + c]
            gathered[pl.ds(c * rank, rank), :] = down[lax.div(row, 2), lax.rem(row, 2)]
        total = jnp.zeros((rows, CHUNK * rank), F32)
        for owner in range(RING):
            total = total + nt_dot(
                chunk_tokens(owner, k), gathered[:, pl.ds(owner * width, width)]
            )
        row_call = lax.broadcasted_iota(jnp.int32, total.shape, 0) // length
        lane_call = lax.broadcasted_iota(jnp.int32, total.shape, 1) // rank
        kept = jnp.where(row_call == lane_call, total, 0.0).astype(BF16)
        shape = (CHUNK * rank, low.shape[3])
        from_rank = lax.broadcasted_iota(jnp.int32, shape, 0) % rank + y * rank
        fold = jnp.where(
            from_rank == lax.broadcasted_iota(jnp.int32, shape, 1), 1.0, 0.0
        ).astype(BF16)
        low[y, k] = jnp.dot(kept, fold, preferred_element_type=F32).astype(BF16)
        for d in range(1, RING):
            low_copy(y, d, k, lax.rem(y + d, RING)).start()
        return carry

    def at_step(i, sign):
        dx, dz, dc = STEPS[i]
        other = lax.rem(core + dc, 2)
        side = sign * (1 - 2 * (core if sign == 1 else other))
        return (
            lax.rem(pos_x + side * dx + RING, RING) * (2 * RING)
            + lax.rem(pos_z + side * dz + RING, RING) * 2
            + other
        )

    def out_copy(i, target, source):
        return pltpu.make_async_remote_copy(
            src_ref=slots.at[pl.ds(i * CAP, CAP)],
            dst_ref=out_hbm.at[pl.ds(source * CAP, CAP)],
            send_sem=out_send.at[i],
            recv_sem=out_recv.at[i],
            device_id={"adapter": target},
            device_id_type=MESH,
        )

    at_home = STEPS.index((0, 0, 0))
    own = pltpu.make_async_copy(
        slots.at[pl.ds(at_home * CAP, CAP)],
        out_hbm.at[pl.ds(me * CAP, CAP)],
        load_sem.at[6],
    )

    def send_slots(i):
        for r in range(CAP):
            at = i * CAP + r
            block = done[meta[2, at]].astype(F32)
            slots[at] = jnp.where(meta[3, at] > 0, block, 0.0).astype(BF16)
        if i == at_home:
            own.start()
        else:
            out_copy(i, at_step(i, 1), me).start()

    def after_adapters(k, carry):
        for d in range(1, RING):
            low_copy(lax.rem(y + RING - d, RING), d, k, y).wait_recv()
        low_rank = (
            low[0, k].astype(F32)
            + low[1, k].astype(F32)
            + low[2, k].astype(F32)
            + low[3, k].astype(F32)
        ).astype(BF16)
        for c in range(CHUNK):
            row = meta[1, k * CHUNK + c]
            weight = up[lax.div(row, 2), lax.rem(row, 2)]
            delta = jnp.dot(
                low_rank[c * length : (c + 1) * length, :rank_all],
                weight,
                preferred_element_type=F32,
            )
            proj[k, c, pl.ds(PAD, length), :] = proj[k, c, pl.ds(PAD, length), :] + delta
        lane = lax.broadcasted_iota(jnp.int32, (rows, 128), 1)
        for pair in range(cols // 128):
            at = pl.ds(pair * 128, 128)
            x_conv = conv(proj.at[k], at, at)
            x_high = x_conv.astype(BF16)
            mixed = skip[0:1, at] * x_conv
            for part in (x_high.astype(F32), x_conv - x_high.astype(F32)):
                first = jnp.where(lane < HEAD_DIM, part, 0.0).astype(BF16)
                second = jnp.where(lane < HEAD_DIM, 0.0, part).astype(BF16)
                mixed = mixed + jnp.dot(
                    mixing[k, pair],
                    jnp.concatenate([first, second], axis=0),
                    preferred_element_type=F32,
                )
            done[pl.ds(k * CHUNK, CHUNK), :, at] = mixed.reshape(
                CHUNK, length, 128
            ).astype(BF16)
        for number in range(chunks):

            @pl.when(k == number)
            def _(number=number):
                for i in range(CHUNK // CAP):
                    send_slots(number * (CHUNK // CAP) + i)

        return carry

    last = chunks - 1

    def step(t, carry):
        @pl.when(t < chunks)
        def _():
            y_copy(0, left, t, y).wait_recv()
            y_copy(2, left, t, right).start()
            y_copy(1, right, t, y).wait_recv()
            y_copy(3, right, t, left).start()

        @pl.when(t + 2 < chunks)
        def _():
            send_own(t + 2)

        for number in range(1, N_EVENTS):

            @pl.when(t == number)
            def _(number=number):
                for table in tables:
                    table.event(number)

        @pl.when(t > 0)
        def _():
            k = t - 1
            y_copy(2, across, k, y).wait_recv()
            y_copy(3, across, k, y).wait_recv()
            before_adapters(k)

        @pl.when(t == TABLES_AT)
        def _():
            for table in tables:
                table.got_twins()

        lax.fori_loop(
            jnp.where(t == TABLES_AT, 0, t - 1), jnp.where(t >= TABLES_AT, t, t - 1), reduce_chunk, 0
        )
        lax.fori_loop(
            jnp.where(t == chunks, 4, 0),
            jnp.where(t == chunks, chunks, jnp.where(t == last, 4, 0)),
            after_adapters,
            0,
        )
        return carry

    lax.fori_loop(0, chunks + 1, step, 0)

    for i in range(calls // CAP, sources):
        send_slots(i)

    own.wait()
    for table in tables:
        table.sent_all()

    def drain(k, carry):
        for kind in range(4):
            y_copy(kind, y, k, y).wait_send()
        for d in range(1, RING):
            low_copy(y, d, k, y).wait_send()
        return carry

    lax.fori_loop(0, chunks, drain, 0)
    for i in range(sources):
        if i != at_home:
            out_copy(i, me, me).wait_send()
            out_copy(i, me, at_step(i, -1)).wait_recv()


def routing(routed_group_index, call_adapter_index, holder_table_row, me, sources, calls):
    group = lax.dynamic_slice(routed_group_index, (me * calls,), (calls,))
    named = lax.dynamic_slice(call_adapter_index[:, 0], (me * calls,), (calls,))
    call = jnp.arange(calls, dtype=jnp.int32)
    same = group[:, None] == group[None, :]
    rank = jnp.sum(jnp.where(same & (call[None, :] < call[:, None]), 1, 0), axis=1)
    side = 1 - 2 * (me % 2)
    way = (
        lax.rem(side * (group // (2 * RING) - me // (2 * RING)) + RING, RING) * (2 * RING)
        + lax.rem(side * ((group // 2) % RING - (me // 2) % RING) + RING, RING) * 2
        + lax.rem(group % 2 + me % 2, 2)
    )
    step_ways = jnp.array([dx * 2 * RING + dz * 2 + dc for dx, dz, dc in STEPS], jnp.int32)
    step = jnp.sum(
        jnp.where(
            way[:, None] == step_ways[None, :], jnp.arange(sources, dtype=jnp.int32)[None, :], 0
        ),
        axis=1,
    )
    key = step * CAP + rank
    place = jnp.sum(jnp.where(key[None, :] < key[:, None], 1, 0), axis=1)
    row = jnp.sum(
        jnp.where(
            named[:, None] == jnp.arange(holder_table_row.shape[0], dtype=jnp.int32)[None, :],
            holder_table_row[None, :],
            0,
        ),
        axis=1,
    )
    slot = jnp.arange(sources * CAP, dtype=jnp.int32)
    here = place[None, :] == slot[:, None]
    order = jnp.sum(jnp.where(here, call[None, :], 0), axis=1)
    rows = jnp.sum(jnp.where(here, row[None, :], 0), axis=1)
    taken = jnp.sum(jnp.where(key[None, :] < slot[:, None], 1, 0), axis=1)
    live = jnp.sum(jnp.where(key[None, :] == slot[:, None], 1, 0), axis=1)
    return jnp.stack([order, rows, jnp.minimum(taken, calls - 1), live]).astype(jnp.int32)


def on_device(
    call_token_inputs,
    routed_group_index,
    call_adapter_index,
    holder_table_row,
    channel_input_weight,
    input_state_weight,
    output_state_weight,
    step_size_weight,
    channel_input_taps,
    input_state_taps,
    output_state_taps,
    adapter_down_weight,
    adapter_up_weight,
    decay_logarithm,
    step_size_bias,
    head_skip_factor,
):
    sources = lax.axis_size("adapter")
    me = lax.axis_index("adapter")
    calls, length, width = call_token_inputs.shape
    cols = channel_input_weight.shape[1]
    heads = decay_logarithm.shape[0]
    chunks = calls // CHUNK
    rows = CHUNK * length
    total_cols = cols + 2 * NSTATE
    meta = routing(
        routed_group_index, call_adapter_index, holder_table_row, me, sources, calls
    )
    params = jnp.stack([decay_logarithm, step_size_bias])
    params = jnp.pad(params, ((0, 6), (0, 128 - heads)))
    taps = jnp.concatenate(
        [channel_input_taps, input_state_taps, output_state_taps], axis=1
    ).astype(F32)
    skip = jnp.broadcast_to(head_skip_factor[:, None], (heads, HEAD_DIM)).reshape(1, cols)
    down = jnp.swapaxes(adapter_down_weight, 1, 2)
    per_owner, rank, depth = down.shape
    rank_all = adapter_up_weight.shape[1]
    vmem = pl.BlockSpec(memory_space=pltpu.VMEM)
    anywhere = pl.BlockSpec(memory_space=pl.ANY)
    dma = pltpu.SemaphoreType.DMA
    return pl.pallas_call(
        mixer_kernel,
        out_shape=jax.ShapeDtypeStruct((sources * CAP, length, cols), BF16),
        in_specs=[pl.BlockSpec(memory_space=pltpu.SMEM)] + [vmem] * 4 + [anywhere] * 6,
        out_specs=anywhere,
        scratch_shapes=[
            pltpu.VMEM((calls, length, width), BF16),
            pltpu.VMEM((RING, calls, length, width), BF16),
            pltpu.VMEM((depth, total_cols), BF16),
            pltpu.VMEM((depth, 128), BF16),
            pltpu.VMEM((sources, per_owner, rank, depth), BF16),
            pltpu.VMEM((sources, per_owner, rank_all, cols), BF16),
            pltpu.VMEM((chunks, CHUNK, PAD + length, cols), F32),
            pltpu.VMEM((CHUNK, PAD + length, 2 * NSTATE), F32),
            pltpu.VMEM((chunks, cols // 128, rows, 2 * rows), BF16),
            pltpu.VMEM((RING, chunks, rows, 128), BF16),
            pltpu.VMEM((CHUNK * rank, depth), BF16),
            pltpu.VMEM((sources * CAP, length, cols), BF16),
            dma((7,)),
            dma((4, chunks)),
            dma((4, chunks)),
            dma((2, N_TABLE)),
            dma((2, N_TABLE)),
            dma((RING - 1, chunks)),
            dma((RING - 1, chunks)),
            dma((sources,)),
            dma((sources,)),
        ],
        compiler_params=pltpu.CompilerParams(
            collective_id=0, has_side_effects=True, vmem_limit_bytes=60 * 2**20
        ),
        cost_estimate=pl.CostEstimate(
            flops=2 * calls * length * depth * (total_cols + 128),
            bytes_accessed=30 * 2**20,
            transcendentals=calls * length * rows * heads,
        ),
    )(
        meta,
        params,
        taps,
        skip,
        step_size_weight,
        call_token_inputs,
        channel_input_weight,
        input_state_weight,
        output_state_weight,
        down,
        adapter_up_weight,
    )


def solution(mesh):
    placed = (
        P("adapter", None, "head"),
        P(),
        P(),
        P(),
        P(None, "head"),
        P(None, "head"),
        P(None, "head"),
        P(None, "head"),
        P(None, "head"),
        P(None, "head"),
        P(None, "head"),
        P("adapter", None, "head"),
        P("adapter", None, "head"),
        P("head"),
        P("head"),
        P("head"),
    )
    return jax.shard_map(
        on_device, mesh=mesh, in_specs=placed, out_specs=P("adapter", None, "head"), check_vma=False
    )
```

```python
import functools

import jax
import jax.numpy as jnp
from jax import lax
from jax.experimental import pallas as pl
from jax.experimental.pallas import tpu as pltpu
from jax.sharding import PartitionSpec as P

HEAD_DIM = 64
NSTATE = 128
CAP = 2
CHUNK = 4
PAD = 8
RING = 4
MESH = pl.DeviceIdType.MESH
HIGH = lax.Precision.HIGHEST
F32 = jnp.float32
BF16 = jnp.bfloat16

OFFSETS = (0, -1, 1, 2)
N_TABLE = 4 + 16 + 16

CHIP_STEPS = (
    ((2, 1), (2, 3), (1, 2), (3, 2)),
    ((2, 2), (2, 0), (0, 2)),
    ((1, 1), (3, 3), (1, 3), (3, 1)),
    ((1, 0), (3, 0), (0, 1), (0, 3)),
    ((0, 0),),
)
STEPS = tuple((dx, dz, dc) for group in CHIP_STEPS for dc in (1, 0) for dx, dz in group)
TABLES_AT = 5
FINISH = ((5, 0, 2), (6, 2, 5), (7, 5, 6), (8, 6, 8))


def nt_dot(a, b):
    return lax.dot_general(a, b, (((1,), (1,)), ((), ())), preferred_element_type=F32)


class Table:
    def __init__(self, buf, send, recv, first, second, core, strides, axes_to_adapter):
        self.buf, self.send, self.recv = buf, send, recv
        self.first, self.second, self.core = first, second, core
        self.strides = strides
        self.to_adapter = axes_to_adapter

    def owner(self, df, ds, core=None):
        core = self.core if core is None else core
        a = lax.rem(self.first + (df + RING), RING)
        b = lax.rem(self.second + (ds + RING), RING)
        return a * self.strides[0] + b * self.strides[1] + core

    def unit(self, df, ds, part=None, core=None):
        ref = self.buf.at[self.owner(df, ds, core)]
        return ref if part is None else ref.at[part]

    def copy(self, ref, index, target):
        return pltpu.make_async_remote_copy(
            src_ref=ref,
            dst_ref=ref,
            send_sem=self.send.at[index],
            recv_sem=self.recv.at[index],
            device_id={"adapter": target},
            device_id_type=MESH,
        )

    def plain(self, df):
        return 0 if df is None else 4 + 4 * OFFSETS.index(df)

    def send_plain(self, df):
        base = self.plain(df)
        if df is None:
            self.copy(self.unit(0, 0), base, self.owner(1, 0)).start()
            self.copy(self.unit(0, 0), base + 1, self.owner(-1, 0)).start()
        else:
            self.copy(self.unit(df, 0), base, self.owner(0, 1)).start()
            self.copy(self.unit(df, 0), base + 1, self.owner(0, -1)).start()

    def got_plain(self, df):
        base = self.plain(df)
        here = self.owner(0, 0)
        if df is None:
            self.copy(self.unit(-1, 0), base, here).wait_recv()
            self.copy(self.unit(1, 0), base + 1, here).wait_recv()
        else:
            self.copy(self.unit(df, -1), base, here).wait_recv()
            self.copy(self.unit(df, 1), base + 1, here).wait_recv()

    def send_relay(self, df):
        base = self.plain(df) + 2
        if df is None:
            self.copy(self.unit(-1, 0, 0), base, self.owner(1, 0)).start()
            self.copy(self.unit(1, 0, 1), base + 1, self.owner(-1, 0)).start()
        else:
            self.copy(self.unit(df, -1, 0), base, self.owner(0, 1)).start()
            self.copy(self.unit(df, 1, 1), base + 1, self.owner(0, -1)).start()

    def got_relay(self, df):
        base = self.plain(df) + 2
        here = self.owner(0, 0)
        at = (2, 0) if df is None else (df, 2)
        self.copy(self.unit(*at, 0), base, here).wait_recv()
        self.copy(self.unit(*at, 1), base + 1, here).wait_recv()

    def twin_index(self, df, ds):
        return 20 + 4 * OFFSETS.index(df) + OFFSETS.index(ds)

    def send_twin(self, df, ds):
        self.copy(
            self.unit(df, ds), self.twin_index(df, ds), self.owner(0, 0, 1 - self.core)
        ).start()

    def got_twins(self):
        here = self.owner(0, 0)
        for df in OFFSETS:
            for ds in OFFSETS:
                self.copy(
                    self.unit(df, ds, core=1 - self.core), self.twin_index(df, ds), here
                ).wait_recv()

    def sent_all(self):
        here = self.owner(0, 0)
        for df in (None, *OFFSETS):
            base = self.plain(df)
            for i in (0, 1):
                self.copy(self.unit(0, 0), base + i, here).wait_send()
                self.copy(self.unit(0, 0, 0), base + 2 + i, here).wait_send()
        for i in range(16):
            self.copy(self.unit(0, 0), 20 + i, here).wait_send()

    def event(self, number):
        if number == 0:
            self.send_plain(None)
            self.send_plain(0)
            self.send_twin(0, 0)
        elif number == 1:
            self.got_plain(None)
            self.send_relay(None)
            self.send_plain(-1)
            self.send_plain(1)
            self.got_plain(0)
            self.send_relay(0)
            for at in ((-1, 0), (1, 0), (0, -1), (0, 1)):
                self.send_twin(*at)
        elif number == 2:
            self.got_relay(None)
            self.send_plain(2)
            self.send_twin(2, 0)
            self.got_relay(0)
            self.send_twin(0, 2)
        elif number == 3:
            for df in (-1, 1):
                self.got_plain(df)
                self.send_relay(df)
                self.send_twin(df, -1)
                self.send_twin(df, 1)
        elif number == 4:
            self.got_plain(2)
            self.send_relay(2)
            self.send_twin(2, -1)
            self.send_twin(2, 1)
            for df in (-1, 1):
                self.got_relay(df)
                self.send_twin(df, 2)
        elif number == 5:
            self.got_relay(2)
            self.send_twin(2, 2)


N_EVENTS = 6


def mixer_kernel(
    meta,
    skip,
    decay_in,
    bias_in,
    x_taps,
    b_taps,
    c_taps,
    wdt_in,
    x_hbm,
    wx_hbm,
    wb_hbm,
    wc_hbm,
    down_hbm,
    up_hbm,
    out_hbm,
    x_in,
    x_all,
    w_all,
    wdt,
    down,
    up,
    proj,
    between,
    mixing,
    low,
    gathered,
    slots,
    params,
    taps,
    load_sem,
    y_send,
    y_recv,
    table_send,
    table_recv,
    low_send,
    low_recv,
    out_send,
    out_recv,
):
    sources = lax.axis_size("adapter")
    me = lax.axis_index("adapter")
    y = lax.axis_index("head")
    calls, length, width = x_in.shape
    chunks = calls // CHUNK
    rows = CHUNK * length
    cols = wx_hbm.shape[1]
    half = CHUNK // 2
    right, left = lax.rem(y + 1, RING), lax.rem(y + RING - 1, RING)
    across = lax.rem(y + 2, RING)
    core = lax.rem(me, 2)
    pos_z = lax.rem(lax.div(me, 2), RING)
    pos_x = lax.div(me, 2 * RING)

    loads = [
        pltpu.make_async_copy(x_hbm, x_in, load_sem.at[0]),
        pltpu.make_async_copy(down_hbm, down.at[me], load_sem.at[1]),
        pltpu.make_async_copy(up_hbm, up.at[me], load_sem.at[2]),
        pltpu.make_async_copy(wx_hbm, w_all.at[:, pl.ds(0, cols)], load_sem.at[3]),
        pltpu.make_async_copy(wb_hbm, w_all.at[:, pl.ds(cols, NSTATE)], load_sem.at[4]),
        pltpu.make_async_copy(
            wc_hbm, w_all.at[:, pl.ds(cols + NSTATE, NSTATE)], load_sem.at[5]
        ),
    ]
    for load in loads:
        load.start()

    barrier = pltpu.get_barrier_semaphore()

    def greet(i, carry):
        pl.semaphore_signal(
            barrier,
            inc=1,
            device_id={"adapter": lax.rem(me + i, sources)},
            device_id_type=MESH,
        )
        return carry

    lax.fori_loop(1, sources, greet, 0)
    for d in range(1, RING):
        pl.semaphore_signal(
            barrier,
            inc=1,
            device_id={"head": lax.rem(y + d, RING)},
            device_id_type=MESH,
        )

    def arrange(j, carry):
        x_all[y, j] = x_in[meta[0, j]]
        return carry

    loads[0].wait()
    lax.fori_loop(0, 2 * CHUNK, arrange, 0)
    pl.semaphore_wait(barrier, sources - 1 + RING - 1)

    def y_copy(kind, owner, k, target):
        if kind < 2:
            ref = x_all.at[owner, pl.ds(k * CHUNK, CHUNK)]
        else:
            ref = x_all.at[owner, pl.ds(k * CHUNK + (kind - 2) * half, half)]
        return pltpu.make_async_remote_copy(
            src_ref=ref,
            dst_ref=ref,
            send_sem=y_send.at[kind, k],
            recv_sem=y_recv.at[kind, k],
            device_id={"head": target},
            device_id_type=MESH,
        )

    def send_own(k):
        y_copy(0, y, k, right).start()
        y_copy(1, y, k, left).start()

    send_own(0)
    send_own(1)

    table_down = Table(
        down, table_send.at[0], table_recv.at[0], pos_x, pos_z, core, (2 * RING, 2), None
    )
    table_up = Table(
        up, table_send.at[1], table_recv.at[1], pos_z, pos_x, core, (2, 2 * RING), None
    )
    tables = (table_down, table_up)
    loads[1].wait()
    loads[2].wait()
    for table in tables:
        table.event(0)
    lax.fori_loop(2 * CHUNK, calls, arrange, 0)


    for c in range(CHUNK):
        between[c, pl.ds(0, PAD), :] = jnp.zeros((PAD, 2 * NSTATE), F32)
        for k in range(chunks):
            proj[k, c, pl.ds(0, PAD), :] = jnp.zeros((PAD, cols), F32)
    wdt[...] = jnp.zeros(wdt.shape, BF16)
    heads = wdt_in.shape[0]
    wdt[pl.ds(0, heads), :] = wdt_in[...]
    params[...] = jnp.zeros(params.shape, F32)
    params[0:1, pl.ds(0, heads)] = decay_in[...]
    params[1:2, pl.ds(0, heads)] = bias_in[...]
    taps[:, pl.ds(0, cols)] = x_taps[...].astype(F32)
    taps[:, pl.ds(cols, NSTATE)] = b_taps[...].astype(F32)
    taps[:, pl.ds(cols + NSTATE, NSTATE)] = c_taps[...].astype(F32)
    loads[3].wait()
    loads[4].wait()
    loads[5].wait()

    done = x_in
    rank = down.shape[2]
    rank_all = up.shape[2]
    decay_rate = -jnp.exp(params[0:1, :])
    bias = params[1:2, :]

    def chunk_tokens(owner, k):
        return x_all[owner, pl.ds(k * CHUNK, CHUNK)].reshape(rows, width)

    def project(k, weight, at):
        total = None
        for owner in range(RING):
            term = jnp.dot(
                chunk_tokens(owner, k),
                weight[pl.ds(owner * width, width), at],
                preferred_element_type=F32,
            )
            total = term if total is None else total + term
        return total

    def conv(series, at, taps_at):
        total = jnp.zeros((CHUNK, length, 128), F32)
        for i in range(4):
            total = total + taps[pl.ds(i, 1), taps_at].reshape(1, 1, 128) * series[
                :, pl.ds(PAD - 3 + i, length), at
            ]
        total = total.reshape(rows, 128)
        return total / (1.0 + jnp.exp(-total))

    def before_adapters(k):
        tile = 256 if cols % 256 == 0 else 128

        @pl.loop(0, cols // tile)
        def _(n):
            at = pl.ds(pl.multiple_of(n * tile, tile), tile)
            proj[k, :, pl.ds(PAD, length), at] = project(k, w_all, at).reshape(
                CHUNK, length, tile
            )

        between[:, pl.ds(PAD, length), :] = project(
            k, w_all, pl.ds(cols, 2 * NSTATE)
        ).reshape(CHUNK, length, 2 * NSTATE)
        raw = bias
        for owner in range(RING):
            raw = raw + nt_dot(chunk_tokens(owner, k), wdt[:, pl.ds(owner * width, width)])
        t_iota = lax.broadcasted_iota(jnp.int32, (rows, rows), 0)
        j_iota = lax.broadcasted_iota(jnp.int32, (rows, rows), 1)
        causal = (t_iota // length == j_iota // length) & (j_iota <= t_iota)
        dt = jnp.maximum(raw, 0.0) + jnp.log1p(jnp.exp(-jnp.abs(raw)))
        cum = jnp.dot(
            jnp.where(causal, 1.0, 0.0),
            decay_rate * dt,
            preferred_element_type=F32,
            precision=HIGH,
        )
        cum_t = cum.T
        dt_t = dt.T
        b_conv = conv(between, pl.ds(0, NSTATE), pl.ds(cols, NSTATE))
        c_conv = conv(between, pl.ds(NSTATE, NSTATE), pl.ds(cols + NSTATE, NSTATE))
        marks = lax.dot_general(
            c_conv,
            b_conv,
            (((1,), (1,)), ((), ())),
            preferred_element_type=F32,
            precision=HIGH,
        )
        for h in range(cols // HEAD_DIM):
            segment = cum[:, h : h + 1] - cum_t[h : h + 1, :]
            decay = jnp.exp(jnp.where(causal, segment, -1e30))
            mixing[k, h // 2, :, pl.ds((h % 2) * rows, rows)] = (
                marks * decay * dt_t[h : h + 1, :]
            ).astype(BF16)

    def low_copy(owner, d, k, target):
        ref = low.at[owner, k]
        return pltpu.make_async_remote_copy(
            src_ref=ref,
            dst_ref=ref,
            send_sem=low_send.at[d - 1, k],
            recv_sem=low_recv.at[d - 1, k],
            device_id={"head": target},
            device_id_type=MESH,
        )

    def reduce_chunk(k, carry):
        for c in range(CHUNK):
            row = meta[1, k * CHUNK + c]
            gathered[pl.ds(c * rank, rank), :] = down[lax.div(row, 2), lax.rem(row, 2)]
        total = jnp.zeros((rows, CHUNK * rank), F32)
        for owner in range(RING):
            total = total + nt_dot(
                chunk_tokens(owner, k), gathered[:, pl.ds(owner * width, width)]
            )
        row_call = lax.broadcasted_iota(jnp.int32, total.shape, 0) // length
        lane_call = lax.broadcasted_iota(jnp.int32, total.shape, 1) // rank
        kept = jnp.where(row_call == lane_call, total, 0.0).astype(BF16)
        shape = (CHUNK * rank, low.shape[3])
        from_rank = lax.broadcasted_iota(jnp.int32, shape, 0) % rank + y * rank
        fold = jnp.where(
            from_rank == lax.broadcasted_iota(jnp.int32, shape, 1), 1.0, 0.0
        ).astype(BF16)
        low[y, k] = jnp.dot(kept, fold, preferred_element_type=F32).astype(BF16)
        for d in range(1, RING):
            low_copy(y, d, k, lax.rem(y + d, RING)).start()
        return carry

    def at_step(i, sign):
        dx, dz, dc = STEPS[i]
        other = lax.rem(core + dc, 2)
        side = sign * (1 - 2 * (core if sign == 1 else other))
        return (
            lax.rem(pos_x + side * dx + RING, RING) * (2 * RING)
            + lax.rem(pos_z + side * dz + RING, RING) * 2
            + other
        )

    def out_copy(i, target, source):
        return pltpu.make_async_remote_copy(
            src_ref=slots.at[pl.ds(i * CAP, CAP)],
            dst_ref=out_hbm.at[pl.ds(source * CAP, CAP)],
            send_sem=out_send.at[i],
            recv_sem=out_recv.at[i],
            device_id={"adapter": target},
            device_id_type=MESH,
        )

    at_home = STEPS.index((0, 0, 0))
    own = pltpu.make_async_copy(
        slots.at[pl.ds(at_home * CAP, CAP)],
        out_hbm.at[pl.ds(me * CAP, CAP)],
        load_sem.at[6],
    )

    def send_slots(i):
        for r in range(CAP):
            at = i * CAP + r
            block = done[meta[2, at]].astype(F32)
            slots[at] = jnp.where(meta[3, at] > 0, block, 0.0).astype(BF16)
        if i == at_home:
            own.start()
        else:
            out_copy(i, at_step(i, 1), me).start()

    def after_adapters(k, carry):
        for d in range(1, RING):
            low_copy(lax.rem(y + RING - d, RING), d, k, y).wait_recv()
        low_rank = (
            low[0, k].astype(F32)
            + low[1, k].astype(F32)
            + low[2, k].astype(F32)
            + low[3, k].astype(F32)
        ).astype(BF16)
        for c in range(CHUNK):
            row = meta[1, k * CHUNK + c]
            weight = up[lax.div(row, 2), lax.rem(row, 2)]
            delta = jnp.dot(
                low_rank[c * length : (c + 1) * length, :rank_all],
                weight,
                preferred_element_type=F32,
            )
            proj[k, c, pl.ds(PAD, length), :] = proj[k, c, pl.ds(PAD, length), :] + delta
        lane = lax.broadcasted_iota(jnp.int32, (rows, 128), 1)
        for pair in range(cols // 128):
            at = pl.ds(pair * 128, 128)
            x_conv = conv(proj.at[k], at, at)
            x_high = x_conv.astype(BF16)
            mixed = jnp.where(lane < HEAD_DIM, skip[2 * pair], skip[2 * pair + 1]) * x_conv
            for part in (x_high.astype(F32), x_conv - x_high.astype(F32)):
                first = jnp.where(lane < HEAD_DIM, part, 0.0).astype(BF16)
                second = jnp.where(lane < HEAD_DIM, 0.0, part).astype(BF16)
                mixed = mixed + jnp.dot(
                    mixing[k, pair],
                    jnp.concatenate([first, second], axis=0),
                    preferred_element_type=F32,
                )
            done[pl.ds(k * CHUNK, CHUNK), :, at] = mixed.reshape(
                CHUNK, length, 128
            ).astype(BF16)
        for number in range(chunks):

            @pl.when(k == number)
            def _(number=number):
                for i in range(CHUNK // CAP):
                    send_slots(number * (CHUNK // CAP) + i)

        return carry

    last = chunks - 1

    def step(t, carry):
        @pl.when(t < chunks)
        def _():
            y_copy(0, left, t, y).wait_recv()
            y_copy(2, left, t, right).start()
            y_copy(1, right, t, y).wait_recv()
            y_copy(3, right, t, left).start()

        @pl.when(t + 2 < chunks)
        def _():
            send_own(t + 2)

        for number in range(1, N_EVENTS):

            @pl.when(t == number)
            def _(number=number):
                for table in tables:
                    table.event(number)

        @pl.when(t > 0)
        def _():
            k = t - 1
            y_copy(2, across, k, y).wait_recv()
            y_copy(3, across, k, y).wait_recv()
            before_adapters(k)

        @pl.when(t == TABLES_AT)
        def _():
            for table in tables:
                table.got_twins()

        lax.fori_loop(
            jnp.where(t == TABLES_AT, 0, t - 1), jnp.where(t >= TABLES_AT, t, t - 1), reduce_chunk, 0
        )
        first, end = 0, 0
        for at, begin, until in FINISH:
            first = jnp.where(t == at, begin, first)
            end = jnp.where(t == at, until, end)
        lax.fori_loop(first, end, after_adapters, 0)
        return carry

    lax.fori_loop(0, chunks + 1, step, 0)

    for i in range(calls // CAP, sources):
        send_slots(i)

    own.wait()
    for table in tables:
        table.sent_all()

    def drain(k, carry):
        for kind in range(4):
            y_copy(kind, y, k, y).wait_send()
        for d in range(1, RING):
            low_copy(y, d, k, y).wait_send()
        return carry

    lax.fori_loop(0, chunks, drain, 0)
    for i in range(sources):
        if i != at_home:
            out_copy(i, me, me).wait_send()
            out_copy(i, me, at_step(i, -1)).wait_recv()


def routing(routed_group_index, call_adapter_index, holder_table_row, me, sources, calls):
    group = lax.dynamic_slice(routed_group_index, (me * calls,), (calls,))
    named = lax.dynamic_slice(call_adapter_index[:, 0], (me * calls,), (calls,))
    call = jnp.arange(calls, dtype=jnp.int32)
    same = group[:, None] == group[None, :]
    rank = jnp.sum(jnp.where(same & (call[None, :] < call[:, None]), 1, 0), axis=1)
    side = 1 - 2 * (me % 2)
    way = (
        lax.rem(side * (group // (2 * RING) - me // (2 * RING)) + RING, RING) * (2 * RING)
        + lax.rem(side * ((group // 2) % RING - (me // 2) % RING) + RING, RING) * 2
        + lax.rem(group % 2 + me % 2, 2)
    )
    step_ways = jnp.array([dx * 2 * RING + dz * 2 + dc for dx, dz, dc in STEPS], jnp.int32)
    step = jnp.sum(
        jnp.where(
            way[:, None] == step_ways[None, :], jnp.arange(sources, dtype=jnp.int32)[None, :], 0
        ),
        axis=1,
    )
    key = step * CAP + rank
    place = jnp.sum(jnp.where(key[None, :] < key[:, None], 1, 0), axis=1)
    row = jnp.sum(
        jnp.where(
            named[:, None] == jnp.arange(holder_table_row.shape[0], dtype=jnp.int32)[None, :],
            holder_table_row[None, :],
            0,
        ),
        axis=1,
    )
    slot = jnp.arange(sources * CAP, dtype=jnp.int32)
    here = place[None, :] == slot[:, None]
    order = jnp.sum(jnp.where(here, call[None, :], 0), axis=1)
    rows = jnp.sum(jnp.where(here, row[None, :], 0), axis=1)
    taken = jnp.sum(jnp.where(key[None, :] < slot[:, None], 1, 0), axis=1)
    live = jnp.sum(jnp.where(key[None, :] == slot[:, None], 1, 0), axis=1)
    return jnp.stack([order, rows, jnp.minimum(taken, calls - 1), live]).astype(jnp.int32)


def on_device(
    call_token_inputs,
    routed_group_index,
    call_adapter_index,
    holder_table_row,
    channel_input_weight,
    input_state_weight,
    output_state_weight,
    step_size_weight,
    channel_input_taps,
    input_state_taps,
    output_state_taps,
    adapter_down_weight,
    adapter_up_weight,
    decay_logarithm,
    step_size_bias,
    head_skip_factor,
):
    sources = lax.axis_size("adapter")
    me = lax.axis_index("adapter")
    calls, length, width = call_token_inputs.shape
    cols = channel_input_weight.shape[1]
    heads = decay_logarithm.shape[0]
    chunks = calls // CHUNK
    rows = CHUNK * length
    total_cols = cols + 2 * NSTATE
    meta = routing(
        routed_group_index, call_adapter_index, holder_table_row, me, sources, calls
    )
    down = jnp.swapaxes(adapter_down_weight, 1, 2)
    per_owner, rank, depth = down.shape
    rank_all = adapter_up_weight.shape[1]
    vmem = pl.BlockSpec(memory_space=pltpu.VMEM)
    anywhere = pl.BlockSpec(memory_space=pl.ANY)
    dma = pltpu.SemaphoreType.DMA
    return pl.pallas_call(
        mixer_kernel,
        out_shape=jax.ShapeDtypeStruct((sources * CAP, length, cols), BF16),
        in_specs=[pl.BlockSpec(memory_space=pltpu.SMEM)] * 2 + [vmem] * 6 + [anywhere] * 6,
        out_specs=anywhere,
        scratch_shapes=[
            pltpu.VMEM((calls, length, width), BF16),
            pltpu.VMEM((RING, calls, length, width), BF16),
            pltpu.VMEM((depth, total_cols), BF16),
            pltpu.VMEM((128, depth), BF16),
            pltpu.VMEM((sources, per_owner, rank, depth), BF16),
            pltpu.VMEM((sources, per_owner, rank_all, cols), BF16),
            pltpu.VMEM((chunks, CHUNK, PAD + length, cols), F32),
            pltpu.VMEM((CHUNK, PAD + length, 2 * NSTATE), F32),
            pltpu.VMEM((chunks, cols // 128, rows, 2 * rows), BF16),
            pltpu.VMEM((RING, chunks, rows, 128), BF16),
            pltpu.VMEM((CHUNK * rank, depth), BF16),
            pltpu.VMEM((sources * CAP, length, cols), BF16),
            pltpu.VMEM((8, 128), F32),
            pltpu.VMEM((4, total_cols), F32),
            dma((7,)),
            dma((4, chunks)),
            dma((4, chunks)),
            dma((2, N_TABLE)),
            dma((2, N_TABLE)),
            dma((RING - 1, chunks)),
            dma((RING - 1, chunks)),
            dma((sources,)),
            dma((sources,)),
        ],
        compiler_params=pltpu.CompilerParams(
            collective_id=0, has_side_effects=True, vmem_limit_bytes=60 * 2**20
        ),
        cost_estimate=pl.CostEstimate(
            flops=2 * calls * length * depth * (total_cols + 128),
            bytes_accessed=30 * 2**20,
            transcendentals=calls * length * rows * heads,
        ),
    )(
        meta,
        head_skip_factor,
        decay_logarithm[None, :],
        step_size_bias[None, :],
        channel_input_taps,
        input_state_taps,
        output_state_taps,
        step_size_weight.T,
        call_token_inputs,
        channel_input_weight,
        input_state_weight,
        output_state_weight,
        down,
        adapter_up_weight,
    )


def solution(mesh):
    placed = (
        P("adapter", None, "head"),
        P(),
        P(),
        P(),
        P(None, "head"),
        P(None, "head"),
        P(None, "head"),
        P(None, "head"),
        P(None, "head"),
        P(None, "head"),
        P(None, "head"),
        P("adapter", None, "head"),
        P("adapter", None, "head"),
        P("head"),
        P("head"),
        P("head"),
    )
    return jax.shard_map(
        on_device, mesh=mesh, in_specs=placed, out_specs=P("adapter", None, "head"), check_vma=False
    )
```

```python
import functools

import jax
import jax.numpy as jnp
from jax import lax
from jax.experimental import pallas as pl
from jax.experimental.pallas import tpu as pltpu
from jax.sharding import PartitionSpec as P

HEAD_DIM = 64
NSTATE = 128
CAP = 2
CHUNK = 4
PAD = 8
RING = 4
MESH = pl.DeviceIdType.MESH
HIGH = lax.Precision.HIGHEST
F32 = jnp.float32
BF16 = jnp.bfloat16

OFFSETS = (0, -1, 1, 2)
N_TABLE = 4 + 16 + 16

CHIP_STEPS = (
    ((2, 1), (2, 3), (1, 2), (3, 2)),
    ((2, 2), (2, 0), (0, 2)),
    ((1, 1), (3, 3), (1, 3), (3, 1)),
    ((1, 0), (3, 0), (0, 1), (0, 3)),
    ((0, 0),),
)
STEPS = tuple((dx, dz, dc) for group in CHIP_STEPS for dc in (1, 0) for dx, dz in group)
TABLES_AT = 4
FINISH = ((4, 0, 2), (5, 2, 4), (6, 4, 5), (7, 5, 6), (8, 6, 8))


def nt_dot(a, b):
    return lax.dot_general(a, b, (((1,), (1,)), ((), ())), preferred_element_type=F32)


class Table:
    def __init__(self, buf, send, recv, first, second, core, strides, axes_to_adapter):
        self.buf, self.send, self.recv = buf, send, recv
        self.first, self.second, self.core = first, second, core
        self.strides = strides
        self.to_adapter = axes_to_adapter

    def owner(self, df, ds, core=None):
        core = self.core if core is None else core
        a = lax.rem(self.first + (df + RING), RING)
        b = lax.rem(self.second + (ds + RING), RING)
        return a * self.strides[0] + b * self.strides[1] + core

    def unit(self, df, ds, part=None, core=None):
        ref = self.buf.at[self.owner(df, ds, core)]
        return ref if part is None else ref.at[part]

    def copy(self, ref, index, target):
        return pltpu.make_async_remote_copy(
            src_ref=ref,
            dst_ref=ref,
            send_sem=self.send.at[index],
            recv_sem=self.recv.at[index],
            device_id={"adapter": target},
            device_id_type=MESH,
        )

    def plain(self, df):
        return 0 if df is None else 4 + 4 * OFFSETS.index(df)

    def send_plain(self, df):
        base = self.plain(df)
        if df is None:
            self.copy(self.unit(0, 0), base, self.owner(1, 0)).start()
            self.copy(self.unit(0, 0), base + 1, self.owner(-1, 0)).start()
        else:
            self.copy(self.unit(df, 0), base, self.owner(0, 1)).start()
            self.copy(self.unit(df, 0), base + 1, self.owner(0, -1)).start()

    def got_plain(self, df):
        base = self.plain(df)
        here = self.owner(0, 0)
        if df is None:
            self.copy(self.unit(-1, 0), base, here).wait_recv()
            self.copy(self.unit(1, 0), base + 1, here).wait_recv()
        else:
            self.copy(self.unit(df, -1), base, here).wait_recv()
            self.copy(self.unit(df, 1), base + 1, here).wait_recv()

    def send_relay(self, df):
        base = self.plain(df) + 2
        if df is None:
            self.copy(self.unit(-1, 0, 0), base, self.owner(1, 0)).start()
            self.copy(self.unit(1, 0, 1), base + 1, self.owner(-1, 0)).start()
        else:
            self.copy(self.unit(df, -1, 0), base, self.owner(0, 1)).start()
            self.copy(self.unit(df, 1, 1), base + 1, self.owner(0, -1)).start()

    def got_relay(self, df):
        base = self.plain(df) + 2
        here = self.owner(0, 0)
        at = (2, 0) if df is None else (df, 2)
        self.copy(self.unit(*at, 0), base, here).wait_recv()
        self.copy(self.unit(*at, 1), base + 1, here).wait_recv()

    def twin_index(self, df, ds):
        return 20 + 4 * OFFSETS.index(df) + OFFSETS.index(ds)

    def send_twin(self, df, ds):
        self.copy(
            self.unit(df, ds), self.twin_index(df, ds), self.owner(0, 0, 1 - self.core)
        ).start()

    def got_twins(self):
        here = self.owner(0, 0)
        for df in OFFSETS:
            for ds in OFFSETS:
                self.copy(
                    self.unit(df, ds, core=1 - self.core), self.twin_index(df, ds), here
                ).wait_recv()

    def sent_all(self):
        here = self.owner(0, 0)
        for df in (None, *OFFSETS):
            base = self.plain(df)
            for i in (0, 1):
                self.copy(self.unit(0, 0), base + i, here).wait_send()
                self.copy(self.unit(0, 0, 0), base + 2 + i, here).wait_send()
        for i in range(16):
            self.copy(self.unit(0, 0), 20 + i, here).wait_send()

    def event(self, number):
        if number == 0:
            self.send_plain(None)
            self.send_plain(0)
            self.send_twin(0, 0)
        elif number == 1:
            self.got_plain(None)
            self.send_relay(None)
            self.send_plain(-1)
            self.send_plain(1)
            self.got_plain(0)
            self.send_relay(0)
            for at in ((-1, 0), (1, 0), (0, -1), (0, 1)):
                self.send_twin(*at)
        elif number == 2:
            self.got_relay(None)
            self.send_plain(2)
            self.send_twin(2, 0)
            self.got_relay(0)
            self.send_twin(0, 2)
        elif number == 3:
            for df in (-1, 1):
                self.got_plain(df)
                self.send_relay(df)
                self.send_twin(df, -1)
                self.send_twin(df, 1)
        elif number == 4:
            self.got_plain(2)
            self.send_relay(2)
            self.send_twin(2, -1)
            self.send_twin(2, 1)
            for df in (-1, 1):
                self.got_relay(df)
                self.send_twin(df, 2)
        elif number == 5:
            self.got_relay(2)
            self.send_twin(2, 2)


N_EVENTS = 6


def mixer_kernel(
    meta,
    skip,
    decay_in,
    bias_in,
    x_taps,
    b_taps,
    c_taps,
    wdt_in,
    x_hbm,
    wx_hbm,
    wb_hbm,
    wc_hbm,
    down_hbm,
    up_hbm,
    out_hbm,
    x_in,
    x_all,
    w_all,
    wdt,
    down,
    up,
    proj,
    between,
    mixing,
    low,
    gathered,
    slots,
    params,
    taps,
    load_sem,
    y_send,
    y_recv,
    table_send,
    table_recv,
    low_send,
    low_recv,
    out_send,
    out_recv,
):
    sources = lax.axis_size("adapter")
    me = lax.axis_index("adapter")
    y = lax.axis_index("head")
    calls, length, width = x_in.shape
    chunks = calls // CHUNK
    rows = CHUNK * length
    cols = wx_hbm.shape[1]
    half = CHUNK // 2
    right, left = lax.rem(y + 1, RING), lax.rem(y + RING - 1, RING)
    across = lax.rem(y + 2, RING)
    core = lax.rem(me, 2)
    pos_z = lax.rem(lax.div(me, 2), RING)
    pos_x = lax.div(me, 2 * RING)

    loads = [
        pltpu.make_async_copy(x_hbm, x_in, load_sem.at[0]),
        pltpu.make_async_copy(down_hbm, down.at[me], load_sem.at[1]),
        pltpu.make_async_copy(up_hbm, up.at[me], load_sem.at[2]),
        pltpu.make_async_copy(wx_hbm, w_all.at[:, pl.ds(0, cols)], load_sem.at[3]),
        pltpu.make_async_copy(wb_hbm, w_all.at[:, pl.ds(cols, NSTATE)], load_sem.at[4]),
        pltpu.make_async_copy(
            wc_hbm, w_all.at[:, pl.ds(cols + NSTATE, NSTATE)], load_sem.at[5]
        ),
    ]
    for load in loads:
        load.start()

    barrier = pltpu.get_barrier_semaphore()

    def greet(i, carry):
        pl.semaphore_signal(
            barrier,
            inc=1,
            device_id={"adapter": lax.rem(me + i, sources)},
            device_id_type=MESH,
        )
        return carry

    lax.fori_loop(1, sources, greet, 0)
    for d in range(1, RING):
        pl.semaphore_signal(
            barrier,
            inc=1,
            device_id={"head": lax.rem(y + d, RING)},
            device_id_type=MESH,
        )

    def arrange(j, carry):
        x_all[y, j] = x_in[meta[0, j]]
        return carry

    loads[0].wait()
    lax.fori_loop(0, 2 * CHUNK, arrange, 0)
    pl.semaphore_wait(barrier, sources - 1 + RING - 1)

    def y_copy(kind, owner, k, target):
        if kind < 2:
            ref = x_all.at[owner, pl.ds(k * CHUNK, CHUNK)]
        else:
            ref = x_all.at[owner, pl.ds(k * CHUNK + (kind - 2) * half, half)]
        return pltpu.make_async_remote_copy(
            src_ref=ref,
            dst_ref=ref,
            send_sem=y_send.at[kind, k],
            recv_sem=y_recv.at[kind, k],
            device_id={"head": target},
            device_id_type=MESH,
        )

    def send_own(k):
        y_copy(0, y, k, right).start()
        y_copy(1, y, k, left).start()

    send_own(0)
    send_own(1)

    table_down = Table(
        down, table_send.at[0], table_recv.at[0], pos_x, pos_z, core, (2 * RING, 2), None
    )
    table_up = Table(
        up, table_send.at[1], table_recv.at[1], pos_z, pos_x, core, (2, 2 * RING), None
    )
    tables = (table_down, table_up)
    loads[1].wait()
    loads[2].wait()
    for table in tables:
        table.event(0)
    lax.fori_loop(2 * CHUNK, calls, arrange, 0)


    for c in range(CHUNK):
        between[c, pl.ds(0, PAD), :] = jnp.zeros((PAD, 2 * NSTATE), F32)
        for k in range(chunks):
            proj[k, c, pl.ds(0, PAD), :] = jnp.zeros((PAD, cols), F32)
    wdt[...] = jnp.zeros(wdt.shape, BF16)
    heads = wdt_in.shape[0]
    wdt[pl.ds(0, heads), :] = wdt_in[...]
    params[...] = jnp.zeros(params.shape, F32)
    params[0:1, pl.ds(0, heads)] = decay_in[...]
    params[1:2, pl.ds(0, heads)] = bias_in[...]
    taps[:, pl.ds(0, cols)] = x_taps[...].astype(F32)
    taps[:, pl.ds(cols, NSTATE)] = b_taps[...].astype(F32)
    taps[:, pl.ds(cols + NSTATE, NSTATE)] = c_taps[...].astype(F32)
    loads[3].wait()
    loads[4].wait()
    loads[5].wait()

    done = x_in
    rank = down.shape[2]
    rank_all = up.shape[2]
    decay_rate = -jnp.exp(params[0:1, :])
    bias = params[1:2, :]

    def chunk_tokens(owner, k):
        return x_all[owner, pl.ds(k * CHUNK, CHUNK)].reshape(rows, width)

    def project(k, weight, at):
        total = None
        for owner in range(RING):
            term = jnp.dot(
                chunk_tokens(owner, k),
                weight[pl.ds(owner * width, width), at],
                preferred_element_type=F32,
            )
            total = term if total is None else total + term
        return total

    def conv(series, at, taps_at):
        total = jnp.zeros((CHUNK, length, 128), F32)
        for i in range(4):
            total = total + taps[pl.ds(i, 1), taps_at].reshape(1, 1, 128) * series[
                :, pl.ds(PAD - 3 + i, length), at
            ]
        total = total.reshape(rows, 128)
        return total / (1.0 + jnp.exp(-total))

    def before_adapters(k):
        tile = 256 if cols % 256 == 0 else 128

        @pl.loop(0, cols // tile)
        def _(n):
            at = pl.ds(pl.multiple_of(n * tile, tile), tile)
            proj[k, :, pl.ds(PAD, length), at] = project(k, w_all, at).reshape(
                CHUNK, length, tile
            )

        between[:, pl.ds(PAD, length), :] = project(
            k, w_all, pl.ds(cols, 2 * NSTATE)
        ).reshape(CHUNK, length, 2 * NSTATE)
        raw = bias
        for owner in range(RING):
            raw = raw + nt_dot(chunk_tokens(owner, k), wdt[:, pl.ds(owner * width, width)])
        t_iota = lax.broadcasted_iota(jnp.int32, (rows, rows), 0)
        j_iota = lax.broadcasted_iota(jnp.int32, (rows, rows), 1)
        causal = (t_iota // length == j_iota // length) & (j_iota <= t_iota)
        dt = jnp.maximum(raw, 0.0) + jnp.log1p(jnp.exp(-jnp.abs(raw)))
        cum = jnp.dot(
            jnp.where(causal, 1.0, 0.0),
            decay_rate * dt,
            preferred_element_type=F32,
            precision=HIGH,
        )
        cum_t = cum.T
        dt_t = dt.T
        b_conv = conv(between, pl.ds(0, NSTATE), pl.ds(cols, NSTATE))
        c_conv = conv(between, pl.ds(NSTATE, NSTATE), pl.ds(cols + NSTATE, NSTATE))
        marks = lax.dot_general(
            c_conv,
            b_conv,
            (((1,), (1,)), ((), ())),
            preferred_element_type=F32,
            precision=HIGH,
        )
        for h in range(cols // HEAD_DIM):
            segment = cum[:, h : h + 1] - cum_t[h : h + 1, :]
            decay = jnp.exp(jnp.where(causal, segment, -1e30))
            mixing[k, h // 2, :, pl.ds((h % 2) * rows, rows)] = (
                marks * decay * dt_t[h : h + 1, :]
            ).astype(BF16)

    def low_copy(owner, d, k, target):
        ref = low.at[owner, k]
        return pltpu.make_async_remote_copy(
            src_ref=ref,
            dst_ref=ref,
            send_sem=low_send.at[d - 1, k],
            recv_sem=low_recv.at[d - 1, k],
            device_id={"head": target},
            device_id_type=MESH,
        )

    def reduce_chunk(k, carry):
        for c in range(CHUNK):
            row = meta[1, k * CHUNK + c]
            gathered[pl.ds(c * rank, rank), :] = down[lax.div(row, 2), lax.rem(row, 2)]
        total = jnp.zeros((rows, CHUNK * rank), F32)
        for owner in range(RING):
            total = total + nt_dot(
                chunk_tokens(owner, k), gathered[:, pl.ds(owner * width, width)]
            )
        row_call = lax.broadcasted_iota(jnp.int32, total.shape, 0) // length
        lane_call = lax.broadcasted_iota(jnp.int32, total.shape, 1) // rank
        kept = jnp.where(row_call == lane_call, total, 0.0).astype(BF16)
        shape = (CHUNK * rank, low.shape[3])
        from_rank = lax.broadcasted_iota(jnp.int32, shape, 0) % rank + y * rank
        fold = jnp.where(
            from_rank == lax.broadcasted_iota(jnp.int32, shape, 1), 1.0, 0.0
        ).astype(BF16)
        low[y, k] = jnp.dot(kept, fold, preferred_element_type=F32).astype(BF16)
        for d in range(1, RING):
            low_copy(y, d, k, lax.rem(y + d, RING)).start()
        return carry

    def at_step(i, sign):
        dx, dz, dc = STEPS[i]
        other = lax.rem(core + dc, 2)
        side = sign * (1 - 2 * (core if sign == 1 else other))
        return (
            lax.rem(pos_x + side * dx + RING, RING) * (2 * RING)
            + lax.rem(pos_z + side * dz + RING, RING) * 2
            + other
        )

    def out_copy(i, target, source):
        return pltpu.make_async_remote_copy(
            src_ref=slots.at[pl.ds(i * CAP, CAP)],
            dst_ref=out_hbm.at[pl.ds(source * CAP, CAP)],
            send_sem=out_send.at[i],
            recv_sem=out_recv.at[i],
            device_id={"adapter": target},
            device_id_type=MESH,
        )

    at_home = STEPS.index((0, 0, 0))
    own = pltpu.make_async_copy(
        slots.at[pl.ds(at_home * CAP, CAP)],
        out_hbm.at[pl.ds(me * CAP, CAP)],
        load_sem.at[6],
    )

    def send_slots(i):
        for r in range(CAP):
            at = i * CAP + r
            block = done[meta[2, at]].astype(F32)
            slots[at] = jnp.where(meta[3, at] > 0, block, 0.0).astype(BF16)
        if i == at_home:
            own.start()
        else:
            out_copy(i, at_step(i, 1), me).start()

    def after_adapters(k, carry):
        for d in range(1, RING):
            low_copy(lax.rem(y + RING - d, RING), d, k, y).wait_recv()
        low_rank = (
            low[0, k].astype(F32)
            + low[1, k].astype(F32)
            + low[2, k].astype(F32)
            + low[3, k].astype(F32)
        ).astype(BF16)
        for c in range(CHUNK):
            row = meta[1, k * CHUNK + c]
            weight = up[lax.div(row, 2), lax.rem(row, 2)]
            delta = jnp.dot(
                low_rank[c * length : (c + 1) * length, :rank_all],
                weight,
                preferred_element_type=F32,
            )
            proj[k, c, pl.ds(PAD, length), :] = proj[k, c, pl.ds(PAD, length), :] + delta
        lane = lax.broadcasted_iota(jnp.int32, (rows, 128), 1)
        for pair in range(cols // 128):
            at = pl.ds(pair * 128, 128)
            x_conv = conv(proj.at[k], at, at)
            x_high = x_conv.astype(BF16)
            mixed = jnp.where(lane < HEAD_DIM, skip[2 * pair], skip[2 * pair + 1]) * x_conv
            for part in (x_high.astype(F32), x_conv - x_high.astype(F32)):
                first = jnp.where(lane < HEAD_DIM, part, 0.0).astype(BF16)
                second = jnp.where(lane < HEAD_DIM, 0.0, part).astype(BF16)
                mixed = mixed + jnp.dot(
                    mixing[k, pair],
                    jnp.concatenate([first, second], axis=0),
                    preferred_element_type=F32,
                )
            done[pl.ds(k * CHUNK, CHUNK), :, at] = mixed.reshape(
                CHUNK, length, 128
            ).astype(BF16)
        for number in range(chunks):

            @pl.when(k == number)
            def _(number=number):
                for i in range(CHUNK // CAP):
                    send_slots(number * (CHUNK // CAP) + i)

        return carry

    last = chunks - 1

    def step(t, carry):
        @pl.when(t < chunks)
        def _():
            y_copy(0, left, t, y).wait_recv()
            y_copy(2, left, t, right).start()
            y_copy(1, right, t, y).wait_recv()
            y_copy(3, right, t, left).start()

        @pl.when(t + 2 < chunks)
        def _():
            send_own(t + 2)

        for number in range(1, TABLES_AT + 1):

            @pl.when(t == number)
            def _(number=number):
                for table in tables:
                    table.event(number)

        @pl.when(t > 0)
        def _():
            k = t - 1
            y_copy(2, across, k, y).wait_recv()
            y_copy(3, across, k, y).wait_recv()
            before_adapters(k)

        @pl.when(t == TABLES_AT)
        def _():
            for number in range(TABLES_AT + 1, N_EVENTS):
                for table in tables:
                    table.event(number)
            for table in tables:
                table.got_twins()

        lax.fori_loop(
            jnp.where(t == TABLES_AT, 0, t - 1), jnp.where(t >= TABLES_AT, t, t - 1), reduce_chunk, 0
        )
        first, end = 0, 0
        for at, begin, until in FINISH:
            first = jnp.where(t == at, begin, first)
            end = jnp.where(t == at, until, end)
        lax.fori_loop(first, end, after_adapters, 0)
        return carry

    lax.fori_loop(0, chunks + 1, step, 0)

    for i in range(calls // CAP, sources):
        send_slots(i)

    own.wait()
    for table in tables:
        table.sent_all()

    def drain(k, carry):
        for kind in range(4):
            y_copy(kind, y, k, y).wait_send()
        for d in range(1, RING):
            low_copy(y, d, k, y).wait_send()
        return carry

    lax.fori_loop(0, chunks, drain, 0)
    for i in range(sources):
        if i != at_home:
            out_copy(i, me, me).wait_send()
            out_copy(i, me, at_step(i, -1)).wait_recv()


def routing(routed_group_index, call_adapter_index, holder_table_row, me, sources, calls):
    group = lax.dynamic_slice(routed_group_index, (me * calls,), (calls,))
    named = lax.dynamic_slice(call_adapter_index[:, 0], (me * calls,), (calls,))
    call = jnp.arange(calls, dtype=jnp.int32)
    same = group[:, None] == group[None, :]
    rank = jnp.sum(jnp.where(same & (call[None, :] < call[:, None]), 1, 0), axis=1)
    side = 1 - 2 * (me % 2)
    way = (
        lax.rem(side * (group // (2 * RING) - me // (2 * RING)) + RING, RING) * (2 * RING)
        + lax.rem(side * ((group // 2) % RING - (me // 2) % RING) + RING, RING) * 2
        + lax.rem(group % 2 + me % 2, 2)
    )
    step_ways = jnp.array([dx * 2 * RING + dz * 2 + dc for dx, dz, dc in STEPS], jnp.int32)
    step = jnp.sum(
        jnp.where(
            way[:, None] == step_ways[None, :], jnp.arange(sources, dtype=jnp.int32)[None, :], 0
        ),
        axis=1,
    )
    key = step * CAP + rank
    place = jnp.sum(jnp.where(key[None, :] < key[:, None], 1, 0), axis=1)
    row = jnp.sum(
        jnp.where(
            named[:, None] == jnp.arange(holder_table_row.shape[0], dtype=jnp.int32)[None, :],
            holder_table_row[None, :],
            0,
        ),
        axis=1,
    )
    slot = jnp.arange(sources * CAP, dtype=jnp.int32)
    here = place[None, :] == slot[:, None]
    order = jnp.sum(jnp.where(here, call[None, :], 0), axis=1)
    rows = jnp.sum(jnp.where(here, row[None, :], 0), axis=1)
    taken = jnp.sum(jnp.where(key[None, :] < slot[:, None], 1, 0), axis=1)
    live = jnp.sum(jnp.where(key[None, :] == slot[:, None], 1, 0), axis=1)
    return jnp.stack([order, rows, jnp.minimum(taken, calls - 1), live]).astype(jnp.int32)


def on_device(
    call_token_inputs,
    routed_group_index,
    call_adapter_index,
    holder_table_row,
    channel_input_weight,
    input_state_weight,
    output_state_weight,
    step_size_weight,
    channel_input_taps,
    input_state_taps,
    output_state_taps,
    adapter_down_weight,
    adapter_up_weight,
    decay_logarithm,
    step_size_bias,
    head_skip_factor,
):
    sources = lax.axis_size("adapter")
    me = lax.axis_index("adapter")
    calls, length, width = call_token_inputs.shape
    cols = channel_input_weight.shape[1]
    heads = decay_logarithm.shape[0]
    chunks = calls // CHUNK
    rows = CHUNK * length
    total_cols = cols + 2 * NSTATE
    meta = routing(
        routed_group_index, call_adapter_index, holder_table_row, me, sources, calls
    )
    down = jnp.swapaxes(adapter_down_weight, 1, 2)
    per_owner, rank, depth = down.shape
    rank_all = adapter_up_weight.shape[1]
    vmem = pl.BlockSpec(memory_space=pltpu.VMEM)
    anywhere = pl.BlockSpec(memory_space=pl.ANY)
    dma = pltpu.SemaphoreType.DMA
    return pl.pallas_call(
        mixer_kernel,
        out_shape=jax.ShapeDtypeStruct((sources * CAP, length, cols), BF16),
        in_specs=[pl.BlockSpec(memory_space=pltpu.SMEM)] * 2 + [vmem] * 6 + [anywhere] * 6,
        out_specs=anywhere,
        scratch_shapes=[
            pltpu.VMEM((calls, length, width), BF16),
            pltpu.VMEM((RING, calls, length, width), BF16),
            pltpu.VMEM((depth, total_cols), BF16),
            pltpu.VMEM((128, depth), BF16),
            pltpu.VMEM((sources, per_owner, rank, depth), BF16),
            pltpu.VMEM((sources, per_owner, rank_all, cols), BF16),
            pltpu.VMEM((chunks, CHUNK, PAD + length, cols), F32),
            pltpu.VMEM((CHUNK, PAD + length, 2 * NSTATE), F32),
            pltpu.VMEM((chunks, cols // 128, rows, 2 * rows), BF16),
            pltpu.VMEM((RING, chunks, rows, 128), BF16),
            pltpu.VMEM((CHUNK * rank, depth), BF16),
            pltpu.VMEM((sources * CAP, length, cols), BF16),
            pltpu.VMEM((8, 128), F32),
            pltpu.VMEM((4, total_cols), F32),
            dma((7,)),
            dma((4, chunks)),
            dma((4, chunks)),
            dma((2, N_TABLE)),
            dma((2, N_TABLE)),
            dma((RING - 1, chunks)),
            dma((RING - 1, chunks)),
            dma((sources,)),
            dma((sources,)),
        ],
        compiler_params=pltpu.CompilerParams(
            collective_id=0, has_side_effects=True, vmem_limit_bytes=60 * 2**20
        ),
        cost_estimate=pl.CostEstimate(
            flops=2 * calls * length * depth * (total_cols + 128),
            bytes_accessed=30 * 2**20,
            transcendentals=calls * length * rows * heads,
        ),
    )(
        meta,
        head_skip_factor,
        decay_logarithm[None, :],
        step_size_bias[None, :],
        channel_input_taps,
        input_state_taps,
        output_state_taps,
        step_size_weight.T,
        call_token_inputs,
        channel_input_weight,
        input_state_weight,
        output_state_weight,
        down,
        adapter_up_weight,
    )


def solution(mesh):
    placed = (
        P("adapter", None, "head"),
        P(),
        P(),
        P(),
        P(None, "head"),
        P(None, "head"),
        P(None, "head"),
        P(None, "head"),
        P(None, "head"),
        P(None, "head"),
        P(None, "head"),
        P("adapter", None, "head"),
        P("adapter", None, "head"),
        P("head"),
        P("head"),
        P("head"),
    )
    return jax.shard_map(
        on_device, mesh=mesh, in_specs=placed, out_specs=P("adapter", None, "head"), check_vma=False
    )
```

```python
import functools

import jax
import jax.numpy as jnp
from jax import lax
from jax.experimental import pallas as pl
from jax.experimental.pallas import tpu as pltpu
from jax.sharding import PartitionSpec as P

HEAD_DIM = 64
NSTATE = 128
CAP = 2
CHUNK = 4
PAD = 8
RING = 4
MESH = pl.DeviceIdType.MESH
HIGH = lax.Precision.HIGHEST
F32 = jnp.float32
BF16 = jnp.bfloat16

OFFSETS = (0, -1, 1, 2)
N_TABLE = 4 + 16 + 16

CHIP_STEPS = (
    ((2, 1), (2, 3), (1, 2), (3, 2)),
    ((2, 2), (2, 0), (0, 2)),
    ((1, 1), (3, 3), (1, 3), (3, 1)),
    ((1, 0), (3, 0), (0, 1), (0, 3)),
    ((0, 0),),
)
STEPS = tuple((dx, dz, dc) for group in CHIP_STEPS for dc in (1, 0) for dx, dz in group)
TABLES_AT = 4
FINISH = ((4, 0, 2), (5, 2, 4), (6, 4, 5), (7, 5, 6), (8, 6, 8))


def nt_dot(a, b):
    return lax.dot_general(a, b, (((1,), (1,)), ((), ())), preferred_element_type=F32)


class Table:
    def __init__(self, buf, send, recv, first, second, core, strides, axes_to_adapter):
        self.buf, self.send, self.recv = buf, send, recv
        self.first, self.second, self.core = first, second, core
        self.strides = strides
        self.to_adapter = axes_to_adapter

    def owner(self, df, ds, core=None):
        core = self.core if core is None else core
        a = lax.rem(self.first + (df + RING), RING)
        b = lax.rem(self.second + (ds + RING), RING)
        return a * self.strides[0] + b * self.strides[1] + core

    def unit(self, df, ds, part=None, core=None):
        ref = self.buf.at[self.owner(df, ds, core)]
        return ref if part is None else ref.at[part]

    def copy(self, ref, index, target):
        return pltpu.make_async_remote_copy(
            src_ref=ref,
            dst_ref=ref,
            send_sem=self.send.at[index],
            recv_sem=self.recv.at[index],
            device_id={"adapter": target},
            device_id_type=MESH,
        )

    def plain(self, df):
        return 0 if df is None else 4 + 4 * OFFSETS.index(df)

    def send_plain(self, df):
        base = self.plain(df)
        if df is None:
            self.copy(self.unit(0, 0), base, self.owner(1, 0)).start()
            self.copy(self.unit(0, 0), base + 1, self.owner(-1, 0)).start()
        else:
            self.copy(self.unit(df, 0), base, self.owner(0, 1)).start()
            self.copy(self.unit(df, 0), base + 1, self.owner(0, -1)).start()

    def got_plain(self, df):
        base = self.plain(df)
        here = self.owner(0, 0)
        if df is None:
            self.copy(self.unit(-1, 0), base, here).wait_recv()
            self.copy(self.unit(1, 0), base + 1, here).wait_recv()
        else:
            self.copy(self.unit(df, -1), base, here).wait_recv()
            self.copy(self.unit(df, 1), base + 1, here).wait_recv()

    def send_relay(self, df):
        base = self.plain(df) + 2
        if df is None:
            self.copy(self.unit(-1, 0, 0), base, self.owner(1, 0)).start()
            self.copy(self.unit(1, 0, 1), base + 1, self.owner(-1, 0)).start()
        else:
            self.copy(self.unit(df, -1, 0), base, self.owner(0, 1)).start()
            self.copy(self.unit(df, 1, 1), base + 1, self.owner(0, -1)).start()

    def got_relay(self, df):
        base = self.plain(df) + 2
        here = self.owner(0, 0)
        at = (2, 0) if df is None else (df, 2)
        self.copy(self.unit(*at, 0), base, here).wait_recv()
        self.copy(self.unit(*at, 1), base + 1, here).wait_recv()

    def twin_index(self, df, ds):
        return 20 + 4 * OFFSETS.index(df) + OFFSETS.index(ds)

    def send_twin(self, df, ds):
        self.copy(
            self.unit(df, ds), self.twin_index(df, ds), self.owner(0, 0, 1 - self.core)
        ).start()

    def got_twins(self):
        here = self.owner(0, 0)
        for df in OFFSETS:
            for ds in OFFSETS:
                self.copy(
                    self.unit(df, ds, core=1 - self.core), self.twin_index(df, ds), here
                ).wait_recv()

    def sent_all(self):
        here = self.owner(0, 0)
        for df in (None, *OFFSETS):
            base = self.plain(df)
            for i in (0, 1):
                self.copy(self.unit(0, 0), base + i, here).wait_send()
                self.copy(self.unit(0, 0, 0), base + 2 + i, here).wait_send()
        for i in range(16):
            self.copy(self.unit(0, 0), 20 + i, here).wait_send()

    def event(self, number):
        if number == 0:
            self.send_plain(None)
            self.send_plain(0)
            self.send_twin(0, 0)
        elif number == 1:
            self.got_plain(None)
            self.send_relay(None)
            self.send_plain(-1)
            self.send_plain(1)
            self.got_plain(0)
            self.send_relay(0)
            for at in ((-1, 0), (1, 0), (0, -1), (0, 1)):
                self.send_twin(*at)
        elif number == 2:
            self.got_relay(None)
            self.send_plain(2)
            self.send_twin(2, 0)
            self.got_relay(0)
            self.send_twin(0, 2)
        elif number == 3:
            for df in (-1, 1):
                self.got_plain(df)
                self.send_relay(df)
                self.send_twin(df, -1)
                self.send_twin(df, 1)
        elif number == 4:
            self.got_plain(2)
            self.send_relay(2)
            self.send_twin(2, -1)
            self.send_twin(2, 1)
            for df in (-1, 1):
                self.got_relay(df)
                self.send_twin(df, 2)
        elif number == 5:
            self.got_relay(2)
            self.send_twin(2, 2)


N_EVENTS = 6


def mixer_kernel(
    meta,
    skip,
    decay_in,
    bias_in,
    x_taps,
    b_taps,
    c_taps,
    wdt_in,
    x_hbm,
    wx_hbm,
    wb_hbm,
    wc_hbm,
    down_hbm,
    up_hbm,
    out_hbm,
    x_in,
    x_all,
    w_all,
    wdt,
    down,
    up,
    proj,
    between,
    mixing,
    low,
    gathered,
    slots,
    params,
    taps,
    load_sem,
    y_send,
    y_recv,
    table_send,
    table_recv,
    low_send,
    low_recv,
    out_send,
    out_recv,
):
    sources = lax.axis_size("adapter")
    me = lax.axis_index("adapter")
    y = lax.axis_index("head")
    calls, length, width = x_in.shape
    chunks = calls // CHUNK
    rows = CHUNK * length
    cols = wx_hbm.shape[1]
    half = CHUNK // 2
    right, left = lax.rem(y + 1, RING), lax.rem(y + RING - 1, RING)
    across = lax.rem(y + 2, RING)
    core = lax.rem(me, 2)
    pos_z = lax.rem(lax.div(me, 2), RING)
    pos_x = lax.div(me, 2 * RING)

    loads = [
        pltpu.make_async_copy(x_hbm, x_in, load_sem.at[0]),
        pltpu.make_async_copy(down_hbm, down.at[me], load_sem.at[1]),
        pltpu.make_async_copy(up_hbm, up.at[me], load_sem.at[2]),
        pltpu.make_async_copy(wx_hbm, w_all.at[:, pl.ds(0, cols)], load_sem.at[3]),
        pltpu.make_async_copy(wb_hbm, w_all.at[:, pl.ds(cols, NSTATE)], load_sem.at[4]),
        pltpu.make_async_copy(
            wc_hbm, w_all.at[:, pl.ds(cols + NSTATE, NSTATE)], load_sem.at[5]
        ),
    ]
    for load in loads:
        load.start()

    barrier = pltpu.get_barrier_semaphore()

    def greet(i, carry):
        pl.semaphore_signal(
            barrier,
            inc=1,
            device_id={"adapter": lax.rem(me + i, sources)},
            device_id_type=MESH,
        )
        return carry

    lax.fori_loop(1, sources, greet, 0)
    for d in range(1, RING):
        pl.semaphore_signal(
            barrier,
            inc=1,
            device_id={"head": lax.rem(y + d, RING)},
            device_id_type=MESH,
        )

    def arrange(j, carry):
        x_all[y, j] = x_in[meta[0, j]]
        return carry

    loads[0].wait()
    lax.fori_loop(0, 2 * CHUNK, arrange, 0)
    pl.semaphore_wait(barrier, sources - 1 + RING - 1)

    def y_copy(kind, owner, k, target):
        if kind < 2:
            ref = x_all.at[owner, pl.ds(k * CHUNK, CHUNK)]
        else:
            ref = x_all.at[owner, pl.ds(k * CHUNK + (kind - 2) * half, half)]
        return pltpu.make_async_remote_copy(
            src_ref=ref,
            dst_ref=ref,
            send_sem=y_send.at[kind, k],
            recv_sem=y_recv.at[kind, k],
            device_id={"head": target},
            device_id_type=MESH,
        )

    def send_own(k):
        y_copy(0, y, k, right).start()
        y_copy(1, y, k, left).start()

    send_own(0)
    send_own(1)

    table_down = Table(
        down, table_send.at[0], table_recv.at[0], pos_x, pos_z, core, (2 * RING, 2), None
    )
    table_up = Table(
        up, table_send.at[1], table_recv.at[1], pos_z, pos_x, core, (2, 2 * RING), None
    )
    tables = (table_down, table_up)
    loads[1].wait()
    loads[2].wait()
    for table in tables:
        table.event(0)
    lax.fori_loop(2 * CHUNK, calls, arrange, 0)


    for c in range(CHUNK):
        between[c, pl.ds(0, PAD), :] = jnp.zeros((PAD, 2 * NSTATE), F32)
        for k in range(chunks):
            proj[k, c, pl.ds(0, PAD), :] = jnp.zeros((PAD, cols), F32)
    wdt[...] = jnp.zeros(wdt.shape, BF16)
    heads = wdt_in.shape[0]
    wdt[pl.ds(0, heads), :] = wdt_in[...]
    params[...] = jnp.zeros(params.shape, F32)
    params[0:1, pl.ds(0, heads)] = decay_in[...]
    params[1:2, pl.ds(0, heads)] = bias_in[...]
    taps[:, pl.ds(0, cols)] = x_taps[...].astype(F32)
    taps[:, pl.ds(cols, NSTATE)] = b_taps[...].astype(F32)
    taps[:, pl.ds(cols + NSTATE, NSTATE)] = c_taps[...].astype(F32)
    loads[3].wait()
    loads[4].wait()
    loads[5].wait()

    done = x_in
    rank = down.shape[2]
    rank_all = up.shape[2]
    decay_rate = -jnp.exp(params[0:1, :])
    bias = params[1:2, :]

    def chunk_tokens(owner, k):
        return x_all[owner, pl.ds(k * CHUNK, CHUNK)].reshape(rows, width)

    def project(k, weight, at, owners=(0, 1, 2, 3)):
        total = None
        for owner in owners:
            term = jnp.dot(
                chunk_tokens(owner, k),
                weight[pl.ds(pl.multiple_of(owner * width, width), width), at],
                preferred_element_type=F32,
            )
            total = term if total is None else total + term
        return total

    def conv(series, at, taps_at):
        total = jnp.zeros((CHUNK, length, 128), F32)
        for i in range(4):
            total = total + taps[pl.ds(i, 1), taps_at].reshape(1, 1, 128) * series[
                :, pl.ds(PAD - 3 + i, length), at
            ]
        total = total.reshape(rows, 128)
        return total / (1.0 + jnp.exp(-total))

    tile = 256 if cols % 256 == 0 else 128

    def project_near(k):
        @pl.loop(0, cols // tile)
        def _(n):
            at = pl.ds(pl.multiple_of(n * tile, tile), tile)
            proj[k, :, pl.ds(PAD, length), at] = project(
                k, w_all, at, (y, left, right)
            ).reshape(CHUNK, length, tile)

    def before_adapters(k):
        @pl.loop(0, cols // tile)
        def _(n):
            at = pl.ds(pl.multiple_of(n * tile, tile), tile)
            proj[k, :, pl.ds(PAD, length), at] = proj[
                k, :, pl.ds(PAD, length), at
            ] + project(k, w_all, at, (across,)).reshape(CHUNK, length, tile)

        between[:, pl.ds(PAD, length), :] = project(
            k, w_all, pl.ds(cols, 2 * NSTATE)
        ).reshape(CHUNK, length, 2 * NSTATE)
        raw = bias
        for owner in range(RING):
            raw = raw + nt_dot(chunk_tokens(owner, k), wdt[:, pl.ds(owner * width, width)])
        t_iota = lax.broadcasted_iota(jnp.int32, (rows, rows), 0)
        j_iota = lax.broadcasted_iota(jnp.int32, (rows, rows), 1)
        causal = (t_iota // length == j_iota // length) & (j_iota <= t_iota)
        dt = jnp.maximum(raw, 0.0) + jnp.log1p(jnp.exp(-jnp.abs(raw)))
        cum = jnp.dot(
            jnp.where(causal, 1.0, 0.0),
            decay_rate * dt,
            preferred_element_type=F32,
            precision=HIGH,
        )
        cum_t = cum.T
        dt_t = dt.T
        b_conv = conv(between, pl.ds(0, NSTATE), pl.ds(cols, NSTATE))
        c_conv = conv(between, pl.ds(NSTATE, NSTATE), pl.ds(cols + NSTATE, NSTATE))
        marks = lax.dot_general(
            c_conv,
            b_conv,
            (((1,), (1,)), ((), ())),
            preferred_element_type=F32,
            precision=HIGH,
        )
        for h in range(cols // HEAD_DIM):
            segment = cum[:, h : h + 1] - cum_t[h : h + 1, :]
            decay = jnp.exp(jnp.where(causal, segment, -1e30))
            mixing[k, h // 2, :, pl.ds((h % 2) * rows, rows)] = (
                marks * decay * dt_t[h : h + 1, :]
            ).astype(BF16)

    def low_copy(owner, d, k, target):
        ref = low.at[owner, k]
        return pltpu.make_async_remote_copy(
            src_ref=ref,
            dst_ref=ref,
            send_sem=low_send.at[d - 1, k],
            recv_sem=low_recv.at[d - 1, k],
            device_id={"head": target},
            device_id_type=MESH,
        )

    def reduce_chunk(k, carry):
        for c in range(CHUNK):
            row = meta[1, k * CHUNK + c]
            gathered[pl.ds(c * rank, rank), :] = down[lax.div(row, 2), lax.rem(row, 2)]
        total = jnp.zeros((rows, CHUNK * rank), F32)
        for owner in range(RING):
            total = total + nt_dot(
                chunk_tokens(owner, k), gathered[:, pl.ds(owner * width, width)]
            )
        row_call = lax.broadcasted_iota(jnp.int32, total.shape, 0) // length
        lane_call = lax.broadcasted_iota(jnp.int32, total.shape, 1) // rank
        kept = jnp.where(row_call == lane_call, total, 0.0).astype(BF16)
        shape = (CHUNK * rank, low.shape[3])
        from_rank = lax.broadcasted_iota(jnp.int32, shape, 0) % rank + y * rank
        fold = jnp.where(
            from_rank == lax.broadcasted_iota(jnp.int32, shape, 1), 1.0, 0.0
        ).astype(BF16)
        low[y, k] = jnp.dot(kept, fold, preferred_element_type=F32).astype(BF16)
        for d in range(1, RING):
            low_copy(y, d, k, lax.rem(y + d, RING)).start()
        return carry

    def at_step(i, sign):
        dx, dz, dc = STEPS[i]
        other = lax.rem(core + dc, 2)
        side = sign * (1 - 2 * (core if sign == 1 else other))
        return (
            lax.rem(pos_x + side * dx + RING, RING) * (2 * RING)
            + lax.rem(pos_z + side * dz + RING, RING) * 2
            + other
        )

    def out_copy(i, target, source):
        return pltpu.make_async_remote_copy(
            src_ref=slots.at[pl.ds(i * CAP, CAP)],
            dst_ref=out_hbm.at[pl.ds(source * CAP, CAP)],
            send_sem=out_send.at[i],
            recv_sem=out_recv.at[i],
            device_id={"adapter": target},
            device_id_type=MESH,
        )

    at_home = STEPS.index((0, 0, 0))
    own = pltpu.make_async_copy(
        slots.at[pl.ds(at_home * CAP, CAP)],
        out_hbm.at[pl.ds(me * CAP, CAP)],
        load_sem.at[6],
    )

    def send_slots(i):
        for r in range(CAP):
            at = i * CAP + r
            block = done[meta[2, at]].astype(F32)
            slots[at] = jnp.where(meta[3, at] > 0, block, 0.0).astype(BF16)
        if i == at_home:
            own.start()
        else:
            out_copy(i, at_step(i, 1), me).start()

    def after_adapters(k, carry):
        for d in range(1, RING):
            low_copy(lax.rem(y + RING - d, RING), d, k, y).wait_recv()
        low_rank = (
            low[0, k].astype(F32)
            + low[1, k].astype(F32)
            + low[2, k].astype(F32)
            + low[3, k].astype(F32)
        ).astype(BF16)
        for c in range(CHUNK):
            row = meta[1, k * CHUNK + c]
            weight = up[lax.div(row, 2), lax.rem(row, 2)]
            delta = jnp.dot(
                low_rank[c * length : (c + 1) * length, :rank_all],
                weight,
                preferred_element_type=F32,
            )
            proj[k, c, pl.ds(PAD, length), :] = proj[k, c, pl.ds(PAD, length), :] + delta
        lane = lax.broadcasted_iota(jnp.int32, (rows, 128), 1)
        for pair in range(cols // 128):
            at = pl.ds(pair * 128, 128)
            x_conv = conv(proj.at[k], at, at)
            x_high = x_conv.astype(BF16)
            mixed = jnp.where(lane < HEAD_DIM, skip[2 * pair], skip[2 * pair + 1]) * x_conv
            for part in (x_high.astype(F32), x_conv - x_high.astype(F32)):
                first = jnp.where(lane < HEAD_DIM, part, 0.0).astype(BF16)
                second = jnp.where(lane < HEAD_DIM, 0.0, part).astype(BF16)
                mixed = mixed + jnp.dot(
                    mixing[k, pair],
                    jnp.concatenate([first, second], axis=0),
                    preferred_element_type=F32,
                )
            done[pl.ds(k * CHUNK, CHUNK), :, at] = mixed.reshape(
                CHUNK, length, 128
            ).astype(BF16)
        for number in range(chunks):

            @pl.when(k == number)
            def _(number=number):
                for i in range(CHUNK // CAP):
                    send_slots(number * (CHUNK // CAP) + i)

        return carry

    last = chunks - 1

    def step(t, carry):
        @pl.when(t < chunks)
        def _():
            y_copy(0, left, t, y).wait_recv()
            y_copy(2, left, t, right).start()
            y_copy(1, right, t, y).wait_recv()
            y_copy(3, right, t, left).start()

        for number in range(1, TABLES_AT + 1):

            @pl.when(t == number)
            def _(number=number):
                for table in tables:
                    table.event(number)

        @pl.when(t > 0)
        def _():
            y_copy(2, across, t - 1, y).wait_recv()
            y_copy(3, across, t - 1, y).wait_recv()

        lax.fori_loop(jnp.where(t > TABLES_AT, t - 1, t), t, reduce_chunk, 0)

        @pl.when(t + 2 < chunks)
        def _():
            send_own(t + 2)

        @pl.when(t > 0)
        def _():
            before_adapters(t - 1)

        @pl.when(t == TABLES_AT)
        def _():
            for number in range(TABLES_AT + 1, N_EVENTS):
                for table in tables:
                    table.event(number)
            for table in tables:
                table.got_twins()

        lax.fori_loop(0, jnp.where(t == TABLES_AT, t, 0), reduce_chunk, 0)
        first, end = 0, 0
        for at, begin, until in FINISH:
            first = jnp.where(t == at, begin, first)
            end = jnp.where(t == at, until, end)
        lax.fori_loop(first, end, after_adapters, 0)

        @pl.when(t < chunks)
        def _():
            project_near(t)

        return carry

    lax.fori_loop(0, chunks + 1, step, 0)

    for i in range(calls // CAP, sources):
        send_slots(i)

    own.wait()
    for table in tables:
        table.sent_all()

    def drain(k, carry):
        for kind in range(4):
            y_copy(kind, y, k, y).wait_send()
        for d in range(1, RING):
            low_copy(y, d, k, y).wait_send()
        return carry

    lax.fori_loop(0, chunks, drain, 0)
    for i in range(sources):
        if i != at_home:
            out_copy(i, me, me).wait_send()
            out_copy(i, me, at_step(i, -1)).wait_recv()


def routing(routed_group_index, call_adapter_index, holder_table_row, me, sources, calls):
    group = lax.dynamic_slice(routed_group_index, (me * calls,), (calls,))
    named = lax.dynamic_slice(call_adapter_index[:, 0], (me * calls,), (calls,))
    call = jnp.arange(calls, dtype=jnp.int32)
    same = group[:, None] == group[None, :]
    rank = jnp.sum(jnp.where(same & (call[None, :] < call[:, None]), 1, 0), axis=1)
    side = 1 - 2 * (me % 2)
    way = (
        lax.rem(side * (group // (2 * RING) - me // (2 * RING)) + RING, RING) * (2 * RING)
        + lax.rem(side * ((group // 2) % RING - (me // 2) % RING) + RING, RING) * 2
        + lax.rem(group % 2 + me % 2, 2)
    )
    step_ways = jnp.array([dx * 2 * RING + dz * 2 + dc for dx, dz, dc in STEPS], jnp.int32)
    step = jnp.sum(
        jnp.where(
            way[:, None] == step_ways[None, :], jnp.arange(sources, dtype=jnp.int32)[None, :], 0
        ),
        axis=1,
    )
    key = step * CAP + rank
    place = jnp.sum(jnp.where(key[None, :] < key[:, None], 1, 0), axis=1)
    row = jnp.sum(
        jnp.where(
            named[:, None] == jnp.arange(holder_table_row.shape[0], dtype=jnp.int32)[None, :],
            holder_table_row[None, :],
            0,
        ),
        axis=1,
    )
    slot = jnp.arange(sources * CAP, dtype=jnp.int32)
    here = place[None, :] == slot[:, None]
    order = jnp.sum(jnp.where(here, call[None, :], 0), axis=1)
    rows = jnp.sum(jnp.where(here, row[None, :], 0), axis=1)
    taken = jnp.sum(jnp.where(key[None, :] < slot[:, None], 1, 0), axis=1)
    live = jnp.sum(jnp.where(key[None, :] == slot[:, None], 1, 0), axis=1)
    return jnp.stack([order, rows, jnp.minimum(taken, calls - 1), live]).astype(jnp.int32)


def on_device(
    call_token_inputs,
    routed_group_index,
    call_adapter_index,
    holder_table_row,
    channel_input_weight,
    input_state_weight,
    output_state_weight,
    step_size_weight,
    channel_input_taps,
    input_state_taps,
    output_state_taps,
    adapter_down_weight,
    adapter_up_weight,
    decay_logarithm,
    step_size_bias,
    head_skip_factor,
):
    sources = lax.axis_size("adapter")
    me = lax.axis_index("adapter")
    calls, length, width = call_token_inputs.shape
    cols = channel_input_weight.shape[1]
    heads = decay_logarithm.shape[0]
    chunks = calls // CHUNK
    rows = CHUNK * length
    total_cols = cols + 2 * NSTATE
    meta = routing(
        routed_group_index, call_adapter_index, holder_table_row, me, sources, calls
    )
    down = jnp.swapaxes(adapter_down_weight, 1, 2)
    per_owner, rank, depth = down.shape
    rank_all = adapter_up_weight.shape[1]
    vmem = pl.BlockSpec(memory_space=pltpu.VMEM)
    anywhere = pl.BlockSpec(memory_space=pl.ANY)
    dma = pltpu.SemaphoreType.DMA
    return pl.pallas_call(
        mixer_kernel,
        out_shape=pltpu.VMEM((sources * CAP, length, cols), BF16),
        in_specs=[pl.BlockSpec(memory_space=pltpu.SMEM)] * 2 + [vmem] * 6 + [anywhere] * 6,
        out_specs=pl.BlockSpec(memory_space=pl.ANY),
        scratch_shapes=[
            pltpu.VMEM((calls, length, width), BF16),
            pltpu.VMEM((RING, calls, length, width), BF16),
            pltpu.VMEM((depth, total_cols), BF16),
            pltpu.VMEM((128, depth), BF16),
            pltpu.VMEM((sources, per_owner, rank, depth), BF16),
            pltpu.VMEM((sources, per_owner, rank_all, cols), BF16),
            pltpu.VMEM((chunks, CHUNK, PAD + length, cols), F32),
            pltpu.VMEM((CHUNK, PAD + length, 2 * NSTATE), F32),
            pltpu.VMEM((chunks, cols // 128, rows, 2 * rows), BF16),
            pltpu.VMEM((RING, chunks, rows, 128), BF16),
            pltpu.VMEM((CHUNK * rank, depth), BF16),
            pltpu.VMEM((sources * CAP, length, cols), BF16),
            pltpu.VMEM((8, 128), F32),
            pltpu.VMEM((4, total_cols), F32),
            dma((7,)),
            dma((4, chunks)),
            dma((4, chunks)),
            dma((2, N_TABLE)),
            dma((2, N_TABLE)),
            dma((RING - 1, chunks)),
            dma((RING - 1, chunks)),
            dma((sources,)),
            dma((sources,)),
        ],
        compiler_params=pltpu.CompilerParams(
            collective_id=0, has_side_effects=True, vmem_limit_bytes=56 * 2**20
        ),
        cost_estimate=pl.CostEstimate(
            flops=2 * calls * length * depth * (total_cols + 128),
            bytes_accessed=30 * 2**20,
            transcendentals=calls * length * rows * heads,
        ),
    )(
        meta,
        head_skip_factor,
        decay_logarithm[None, :],
        step_size_bias[None, :],
        channel_input_taps,
        input_state_taps,
        output_state_taps,
        step_size_weight.T,
        call_token_inputs,
        channel_input_weight,
        input_state_weight,
        output_state_weight,
        down,
        adapter_up_weight,
    )


def solution(mesh):
    placed = (
        P("adapter", None, "head"),
        P(),
        P(),
        P(),
        P(None, "head"),
        P(None, "head"),
        P(None, "head"),
        P(None, "head"),
        P(None, "head"),
        P(None, "head"),
        P(None, "head"),
        P("adapter", None, "head"),
        P("adapter", None, "head"),
        P("head"),
        P("head"),
        P("head"),
    )
    return jax.shard_map(
        on_device, mesh=mesh, in_specs=placed, out_specs=P("adapter", None, "head"), check_vma=False
    )
```

```python
import functools

import jax
import jax.numpy as jnp
from jax import lax
from jax.experimental import pallas as pl
from jax.experimental.pallas import tpu as pltpu
from jax.sharding import PartitionSpec as P

HEAD_DIM = 64
NSTATE = 128
CAP = 2
CHUNK = 4
PAD = 8
RING = 4
MESH = pl.DeviceIdType.MESH
HIGH = lax.Precision.HIGHEST
F32 = jnp.float32
BF16 = jnp.bfloat16

OFFSETS = (0, -1, 1, 2)
N_TABLE = 4 + 16 + 16

CHIP_STEPS = (
    ((2, 1), (2, 3), (1, 2), (3, 2)),
    ((2, 2), (2, 0), (0, 2)),
    ((1, 1), (3, 3), (1, 3), (3, 1)),
    ((1, 0), (3, 0), (0, 1), (0, 3)),
    ((0, 0),),
)
STEPS = (
    (2, 1, 1),
    (2, 3, 1),
    (1, 2, 1),
    (3, 2, 1),
    (2, 1, 0),
    (2, 3, 0),
    (1, 2, 0),
    (3, 2, 0),
    (2, 2, 1),
    (2, 0, 1),
    (0, 2, 1),
    (2, 2, 0),
    (2, 0, 0),
    (0, 2, 0),
    (1, 1, 1),
    (3, 3, 1),
    (0, 0, 1),
    (0, 0, 0),
    (1, 0, 1),
    (3, 0, 1),
    (0, 1, 1),
    (0, 3, 1),
    (1, 3, 1),
    (3, 1, 1),
    (1, 1, 0),
    (3, 3, 0),
    (1, 3, 0),
    (3, 1, 0),
    (1, 0, 0),
    (3, 0, 0),
    (0, 1, 0),
    (0, 3, 0),
)
TABLES_AT = 4
FINISH = ((4, 0, 2), (5, 2, 4), (6, 4, 5), (7, 5, 6), (8, 6, 8))


def nt_dot(a, b):
    return lax.dot_general(a, b, (((1,), (1,)), ((), ())), preferred_element_type=F32)


class Table:
    def __init__(self, buf, send, recv, first, second, core, strides, axes_to_adapter):
        self.buf, self.send, self.recv = buf, send, recv
        self.first, self.second, self.core = first, second, core
        self.strides = strides
        self.to_adapter = axes_to_adapter

    def owner(self, df, ds, core=None):
        core = self.core if core is None else core
        a = lax.rem(self.first + (df + RING), RING)
        b = lax.rem(self.second + (ds + RING), RING)
        return a * self.strides[0] + b * self.strides[1] + core

    def unit(self, df, ds, part=None, core=None):
        ref = self.buf.at[self.owner(df, ds, core)]
        return ref if part is None else ref.at[part]

    def copy(self, ref, index, target):
        return pltpu.make_async_remote_copy(
            src_ref=ref,
            dst_ref=ref,
            send_sem=self.send.at[index],
            recv_sem=self.recv.at[index],
            device_id={"adapter": target},
            device_id_type=MESH,
        )

    def plain(self, df):
        return 0 if df is None else 4 + 4 * OFFSETS.index(df)

    def send_plain(self, df):
        base = self.plain(df)
        if df is None:
            self.copy(self.unit(0, 0), base, self.owner(1, 0)).start()
            self.copy(self.unit(0, 0), base + 1, self.owner(-1, 0)).start()
        else:
            self.copy(self.unit(df, 0), base, self.owner(0, 1)).start()
            self.copy(self.unit(df, 0), base + 1, self.owner(0, -1)).start()

    def got_plain(self, df):
        base = self.plain(df)
        here = self.owner(0, 0)
        if df is None:
            self.copy(self.unit(-1, 0), base, here).wait_recv()
            self.copy(self.unit(1, 0), base + 1, here).wait_recv()
        else:
            self.copy(self.unit(df, -1), base, here).wait_recv()
            self.copy(self.unit(df, 1), base + 1, here).wait_recv()

    def send_relay(self, df):
        base = self.plain(df) + 2
        if df is None:
            self.copy(self.unit(-1, 0, 0), base, self.owner(1, 0)).start()
            self.copy(self.unit(1, 0, 1), base + 1, self.owner(-1, 0)).start()
        else:
            self.copy(self.unit(df, -1, 0), base, self.owner(0, 1)).start()
            self.copy(self.unit(df, 1, 1), base + 1, self.owner(0, -1)).start()

    def got_relay(self, df):
        base = self.plain(df) + 2
        here = self.owner(0, 0)
        at = (2, 0) if df is None else (df, 2)
        self.copy(self.unit(*at, 0), base, here).wait_recv()
        self.copy(self.unit(*at, 1), base + 1, here).wait_recv()

    def twin_index(self, df, ds):
        return 20 + 4 * OFFSETS.index(df) + OFFSETS.index(ds)

    def send_twin(self, df, ds):
        self.copy(
            self.unit(df, ds), self.twin_index(df, ds), self.owner(0, 0, 1 - self.core)
        ).start()

    def got_twins(self):
        here = self.owner(0, 0)
        for df in OFFSETS:
            for ds in OFFSETS:
                self.copy(
                    self.unit(df, ds, core=1 - self.core), self.twin_index(df, ds), here
                ).wait_recv()

    def sent_all(self):
        here = self.owner(0, 0)
        for df in (None, *OFFSETS):
            base = self.plain(df)
            for i in (0, 1):
                self.copy(self.unit(0, 0), base + i, here).wait_send()
                self.copy(self.unit(0, 0, 0), base + 2 + i, here).wait_send()
        for i in range(16):
            self.copy(self.unit(0, 0), 20 + i, here).wait_send()

    def event(self, number):
        if number == 0:
            self.send_plain(None)
            self.send_plain(0)
            self.send_twin(0, 0)
        elif number == 1:
            self.got_plain(None)
            self.send_relay(None)
            self.send_plain(-1)
            self.send_plain(1)
            self.got_plain(0)
            self.send_relay(0)
            for at in ((-1, 0), (1, 0), (0, -1), (0, 1)):
                self.send_twin(*at)
        elif number == 2:
            self.got_relay(None)
            self.send_plain(2)
            self.send_twin(2, 0)
            self.got_relay(0)
            self.send_twin(0, 2)
        elif number == 3:
            for df in (-1, 1):
                self.got_plain(df)
                self.send_relay(df)
                self.send_twin(df, -1)
                self.send_twin(df, 1)
        elif number == 4:
            self.got_plain(2)
            self.send_relay(2)
            self.send_twin(2, -1)
            self.send_twin(2, 1)
            for df in (-1, 1):
                self.got_relay(df)
                self.send_twin(df, 2)
        elif number == 5:
            self.got_relay(2)
            self.send_twin(2, 2)


N_EVENTS = 6


def mixer_kernel(
    meta,
    skip,
    decay_in,
    bias_in,
    x_taps,
    b_taps,
    c_taps,
    wdt_in,
    x_hbm,
    wx_hbm,
    wb_hbm,
    wc_hbm,
    down_hbm,
    up_hbm,
    out_hbm,
    x_in,
    x_all,
    w_all,
    wdt,
    down,
    up,
    proj,
    between,
    mixing,
    low,
    gathered,
    slots,
    params,
    taps,
    load_sem,
    y_send,
    y_recv,
    table_send,
    table_recv,
    low_send,
    low_recv,
    out_send,
    out_recv,
):
    sources = lax.axis_size("adapter")
    me = lax.axis_index("adapter")
    y = lax.axis_index("head")
    calls, length, width = x_in.shape
    chunks = calls // CHUNK
    rows = CHUNK * length
    cols = wx_hbm.shape[1]
    half = CHUNK // 2
    right, left = lax.rem(y + 1, RING), lax.rem(y + RING - 1, RING)
    across = lax.rem(y + 2, RING)
    core = lax.rem(me, 2)
    pos_z = lax.rem(lax.div(me, 2), RING)
    pos_x = lax.div(me, 2 * RING)

    loads = [
        pltpu.make_async_copy(x_hbm, x_in, load_sem.at[0]),
        pltpu.make_async_copy(down_hbm, down.at[me], load_sem.at[1]),
        pltpu.make_async_copy(up_hbm, up.at[me], load_sem.at[2]),
        pltpu.make_async_copy(wx_hbm, w_all.at[:, pl.ds(0, cols)], load_sem.at[3]),
        pltpu.make_async_copy(wb_hbm, w_all.at[:, pl.ds(cols, NSTATE)], load_sem.at[4]),
        pltpu.make_async_copy(
            wc_hbm, w_all.at[:, pl.ds(cols + NSTATE, NSTATE)], load_sem.at[5]
        ),
    ]
    for load in loads[:3]:
        load.start()

    barrier = pltpu.get_barrier_semaphore()

    def greet(i, carry):
        pl.semaphore_signal(
            barrier,
            inc=1,
            device_id={"adapter": lax.rem(me + i, sources)},
            device_id_type=MESH,
        )
        return carry

    lax.fori_loop(1, sources, greet, 0)
    for d in range(1, RING):
        pl.semaphore_signal(
            barrier,
            inc=1,
            device_id={"head": lax.rem(y + d, RING)},
            device_id_type=MESH,
        )

    def arrange(j, carry):
        x_all[y, j] = x_in[meta[0, j]]
        return carry

    loads[0].wait()
    lax.fori_loop(0, 2 * CHUNK, arrange, 0)
    pl.semaphore_wait(barrier, sources - 1 + RING - 1)

    def y_copy(kind, owner, k, target):
        if kind < 2:
            ref = x_all.at[owner, pl.ds(k * CHUNK, CHUNK)]
        else:
            ref = x_all.at[owner, pl.ds(k * CHUNK + (kind - 2) * half, half)]
        return pltpu.make_async_remote_copy(
            src_ref=ref,
            dst_ref=ref,
            send_sem=y_send.at[kind, k],
            recv_sem=y_recv.at[kind, k],
            device_id={"head": target},
            device_id_type=MESH,
        )

    def send_own(k):
        y_copy(0, y, k, right).start()
        y_copy(1, y, k, left).start()

    send_own(0)
    send_own(1)

    table_down = Table(
        down, table_send.at[0], table_recv.at[0], pos_x, pos_z, core, (2 * RING, 2), None
    )
    table_up = Table(
        up, table_send.at[1], table_recv.at[1], pos_z, pos_x, core, (2, 2 * RING), None
    )
    tables = (table_down, table_up)
    loads[1].wait()
    loads[2].wait()
    for table in tables:
        table.event(0)
    for load in loads[3:]:
        load.start()
    lax.fori_loop(2 * CHUNK, calls, arrange, 0)


    for c in range(CHUNK):
        between[c, pl.ds(0, PAD), :] = jnp.zeros((PAD, 2 * NSTATE), F32)
        for k in range(chunks):
            proj[k, c, pl.ds(0, PAD), :] = jnp.zeros((PAD, cols), F32)
    wdt[...] = jnp.zeros(wdt.shape, BF16)
    heads = wdt_in.shape[0]
    wdt[pl.ds(0, heads), :] = wdt_in[...]
    params[...] = jnp.zeros(params.shape, F32)
    params[0:1, pl.ds(0, heads)] = decay_in[...]
    params[1:2, pl.ds(0, heads)] = bias_in[...]
    taps[:, pl.ds(0, cols)] = x_taps[...].astype(F32)
    taps[:, pl.ds(cols, NSTATE)] = b_taps[...].astype(F32)
    taps[:, pl.ds(cols + NSTATE, NSTATE)] = c_taps[...].astype(F32)
    loads[3].wait()
    loads[4].wait()
    loads[5].wait()

    done = x_in
    rank = down.shape[2]
    rank_all = up.shape[2]
    decay_rate = -jnp.exp(params[0:1, :])
    bias = params[1:2, :]

    def chunk_tokens(owner, k):
        return x_all[owner, pl.ds(k * CHUNK, CHUNK)].reshape(rows, width)

    def project(k, weight, at, owners=(0, 1, 2, 3)):
        total = None
        for owner in owners:
            term = jnp.dot(
                chunk_tokens(owner, k),
                weight[pl.ds(pl.multiple_of(owner * width, width), width), at],
                preferred_element_type=F32,
            )
            total = term if total is None else total + term
        return total

    def conv(series, at, taps_at):
        total = jnp.zeros((CHUNK, length, 128), F32)
        for i in range(4):
            total = total + taps[pl.ds(i, 1), taps_at].reshape(1, 1, 128) * series[
                :, pl.ds(PAD - 3 + i, length), at
            ]
        total = total.reshape(rows, 128)
        return total / (1.0 + jnp.exp(-total))

    tile = 256 if cols % 256 == 0 else 128

    def project_near(k):
        @pl.loop(0, cols // tile)
        def _(n):
            at = pl.ds(pl.multiple_of(n * tile, tile), tile)
            proj[k, :, pl.ds(PAD, length), at] = project(
                k, w_all, at, (y, left, right)
            ).reshape(CHUNK, length, tile)

    def before_adapters(k):
        @pl.loop(0, cols // tile)
        def _(n):
            at = pl.ds(pl.multiple_of(n * tile, tile), tile)
            proj[k, :, pl.ds(PAD, length), at] = proj[
                k, :, pl.ds(PAD, length), at
            ] + project(k, w_all, at, (across,)).reshape(CHUNK, length, tile)

        between[:, pl.ds(PAD, length), :] = project(
            k, w_all, pl.ds(cols, 2 * NSTATE)
        ).reshape(CHUNK, length, 2 * NSTATE)
        raw = bias
        for owner in range(RING):
            raw = raw + nt_dot(chunk_tokens(owner, k), wdt[:, pl.ds(owner * width, width)])
        t_iota = lax.broadcasted_iota(jnp.int32, (rows, rows), 0)
        j_iota = lax.broadcasted_iota(jnp.int32, (rows, rows), 1)
        causal = (t_iota // length == j_iota // length) & (j_iota <= t_iota)
        dt = jnp.maximum(raw, 0.0) + jnp.log1p(jnp.exp(-jnp.abs(raw)))
        cum = jnp.dot(
            jnp.where(causal, 1.0, 0.0),
            decay_rate * dt,
            preferred_element_type=F32,
            precision=HIGH,
        )
        cum_t = cum.T
        dt_t = dt.T
        b_conv = conv(between, pl.ds(0, NSTATE), pl.ds(cols, NSTATE))
        c_conv = conv(between, pl.ds(NSTATE, NSTATE), pl.ds(cols + NSTATE, NSTATE))
        marks = lax.dot_general(
            c_conv,
            b_conv,
            (((1,), (1,)), ((), ())),
            preferred_element_type=F32,
            precision=HIGH,
        )
        for h in range(cols // HEAD_DIM):
            segment = cum[:, h : h + 1] - cum_t[h : h + 1, :]
            decay = jnp.exp(jnp.where(causal, segment, -1e30))
            mixing[k, h // 2, :, pl.ds((h % 2) * rows, rows)] = (
                marks * decay * dt_t[h : h + 1, :]
            ).astype(BF16)

    def low_copy(owner, d, k, target):
        ref = low.at[owner, k]
        return pltpu.make_async_remote_copy(
            src_ref=ref,
            dst_ref=ref,
            send_sem=low_send.at[d - 1, k],
            recv_sem=low_recv.at[d - 1, k],
            device_id={"head": target},
            device_id_type=MESH,
        )

    def reduce_chunk(k, carry):
        for c in range(CHUNK):
            row = meta[1, k * CHUNK + c]
            gathered[pl.ds(c * rank, rank), :] = down[lax.div(row, 2), lax.rem(row, 2)]
        total = jnp.zeros((rows, CHUNK * rank), F32)
        for owner in range(RING):
            total = total + nt_dot(
                chunk_tokens(owner, k), gathered[:, pl.ds(owner * width, width)]
            )
        row_call = lax.broadcasted_iota(jnp.int32, total.shape, 0) // length
        lane_call = lax.broadcasted_iota(jnp.int32, total.shape, 1) // rank
        kept = jnp.where(row_call == lane_call, total, 0.0).astype(BF16)
        shape = (CHUNK * rank, low.shape[3])
        from_rank = lax.broadcasted_iota(jnp.int32, shape, 0) % rank + y * rank
        fold = jnp.where(
            from_rank == lax.broadcasted_iota(jnp.int32, shape, 1), 1.0, 0.0
        ).astype(BF16)
        low[y, k] = jnp.dot(kept, fold, preferred_element_type=F32).astype(BF16)
        for d in range(1, RING):
            low_copy(y, d, k, lax.rem(y + d, RING)).start()
        return carry

    def at_step(i, sign):
        dx, dz, dc = STEPS[i]
        other = lax.rem(core + dc, 2)
        side = sign * (1 - 2 * (core if sign == 1 else other))
        return (
            lax.rem(pos_x + side * dx + RING, RING) * (2 * RING)
            + lax.rem(pos_z + side * dz + RING, RING) * 2
            + other
        )

    def out_copy(i, target, source):
        return pltpu.make_async_remote_copy(
            src_ref=slots.at[pl.ds(i * CAP, CAP)],
            dst_ref=out_hbm.at[pl.ds(source * CAP, CAP)],
            send_sem=out_send.at[i],
            recv_sem=out_recv.at[i],
            device_id={"adapter": target},
            device_id_type=MESH,
        )

    at_home = STEPS.index((0, 0, 0))
    own = pltpu.make_async_copy(
        slots.at[pl.ds(at_home * CAP, CAP)],
        out_hbm.at[pl.ds(me * CAP, CAP)],
        load_sem.at[6],
    )

    def send_slots(i):
        for r in range(CAP):
            at = i * CAP + r
            block = done[meta[2, at]].astype(F32)
            slots[at] = jnp.where(meta[3, at] > 0, block, 0.0).astype(BF16)
        if i == at_home:
            own.start()
        else:
            out_copy(i, at_step(i, 1), me).start()

    def after_adapters(k, carry):
        for d in range(1, RING):
            low_copy(lax.rem(y + RING - d, RING), d, k, y).wait_recv()
        low_rank = (
            low[0, k].astype(F32)
            + low[1, k].astype(F32)
            + low[2, k].astype(F32)
            + low[3, k].astype(F32)
        ).astype(BF16)
        for c in range(CHUNK):
            row = meta[1, k * CHUNK + c]
            weight = up[lax.div(row, 2), lax.rem(row, 2)]
            delta = jnp.dot(
                low_rank[c * length : (c + 1) * length, :rank_all],
                weight,
                preferred_element_type=F32,
            )
            proj[k, c, pl.ds(PAD, length), :] = proj[k, c, pl.ds(PAD, length), :] + delta
        lane = lax.broadcasted_iota(jnp.int32, (rows, 128), 1)
        for pair in range(cols // 128):
            at = pl.ds(pair * 128, 128)
            x_conv = conv(proj.at[k], at, at)
            x_high = x_conv.astype(BF16)
            mixed = jnp.where(lane < HEAD_DIM, skip[2 * pair], skip[2 * pair + 1]) * x_conv
            for part in (x_high.astype(F32), x_conv - x_high.astype(F32)):
                first = jnp.where(lane < HEAD_DIM, part, 0.0).astype(BF16)
                second = jnp.where(lane < HEAD_DIM, 0.0, part).astype(BF16)
                mixed = mixed + jnp.dot(
                    mixing[k, pair],
                    jnp.concatenate([first, second], axis=0),
                    preferred_element_type=F32,
                )
            done[pl.ds(k * CHUNK, CHUNK), :, at] = mixed.reshape(
                CHUNK, length, 128
            ).astype(BF16)
        for number in range(chunks):

            @pl.when(k == number)
            def _(number=number):
                for i in range(CHUNK // CAP):
                    send_slots(number * (CHUNK // CAP) + i)

        return carry

    last = chunks - 1

    def step(t, carry):
        @pl.when(t < chunks)
        def _():
            y_copy(0, left, t, y).wait_recv()
            y_copy(2, left, t, right).start()
            y_copy(1, right, t, y).wait_recv()
            y_copy(3, right, t, left).start()

        for number in range(1, TABLES_AT + 1):

            @pl.when(t == number)
            def _(number=number):
                for table in tables:
                    table.event(number)

        @pl.when(t > 0)
        def _():
            y_copy(2, across, t - 1, y).wait_recv()
            y_copy(3, across, t - 1, y).wait_recv()

        lax.fori_loop(jnp.where(t > TABLES_AT, t - 1, t), t, reduce_chunk, 0)

        @pl.when(t + 2 < chunks)
        def _():
            send_own(t + 2)

        @pl.when(t > 0)
        def _():
            before_adapters(t - 1)

        @pl.when(t == TABLES_AT)
        def _():
            for number in range(TABLES_AT + 1, N_EVENTS):
                for table in tables:
                    table.event(number)
            for table in tables:
                table.got_twins()

        lax.fori_loop(0, jnp.where(t == TABLES_AT, t, 0), reduce_chunk, 0)
        first, end = 0, 0
        for at, begin, until in FINISH:
            first = jnp.where(t == at, begin, first)
            end = jnp.where(t == at, until, end)
        lax.fori_loop(first, end, after_adapters, 0)

        @pl.when(t < chunks)
        def _():
            project_near(t)

        return carry

    lax.fori_loop(0, chunks + 1, step, 0)

    for i in range(calls // CAP, sources):
        send_slots(i)

    own.wait()
    for table in tables:
        table.sent_all()

    def drain(k, carry):
        for kind in range(4):
            y_copy(kind, y, k, y).wait_send()
        for d in range(1, RING):
            low_copy(y, d, k, y).wait_send()
        return carry

    lax.fori_loop(0, chunks, drain, 0)
    for i in range(sources):
        if i != at_home:
            out_copy(i, me, me).wait_send()
            out_copy(i, me, at_step(i, -1)).wait_recv()


def routing(routed_group_index, call_adapter_index, holder_table_row, me, sources, calls):
    group = lax.dynamic_slice(routed_group_index, (me * calls,), (calls,))
    named = lax.dynamic_slice(call_adapter_index[:, 0], (me * calls,), (calls,))
    call = jnp.arange(calls, dtype=jnp.int32)
    side = 1 - 2 * (me % 2)
    way = (
        lax.rem(side * (lax.shift_right_logical(group, 3) - me // (2 * RING)) + RING, RING)
        * (2 * RING)
        + lax.rem(side * ((lax.shift_right_logical(group, 1) & 3) - (me // 2) % RING) + RING, RING)
        * 2
        + ((group + me) & 1)
    )
    step = jnp.zeros((calls,), jnp.int32)
    for i, (dx, dz, dc) in enumerate(STEPS):
        step = jnp.where(way == dx * 2 * RING + dz * 2 + dc, i, step)
    key = step * calls + call
    place = jnp.sum(jnp.where(key[None, :] < key[:, None], 1, 0), axis=1)
    row = jnp.sum(
        jnp.where(
            named[:, None] == jnp.arange(holder_table_row.shape[0], dtype=jnp.int32)[None, :],
            holder_table_row[None, :],
            0,
        ),
        axis=1,
    )
    slot = jnp.arange(sources * CAP, dtype=jnp.int32)
    here = place[None, :] == slot[:, None]
    order = jnp.sum(jnp.where(here, call[None, :], 0), axis=1)
    rows = jnp.sum(jnp.where(here, row[None, :], 0), axis=1)
    slot_step, slot_rank = slot // CAP, slot % CAP
    ahead = jnp.sum(jnp.where(step[None, :] < slot_step[:, None], 1, 0), axis=1)
    count = jnp.sum(jnp.where(step[None, :] == slot_step[:, None], 1, 0), axis=1)
    taken = ahead + jnp.minimum(slot_rank, count)
    live = jnp.where(count > slot_rank, 1, 0)
    return jnp.stack([order, rows, jnp.minimum(taken, calls - 1), live]).astype(jnp.int32)


def on_device(
    call_token_inputs,
    routed_group_index,
    call_adapter_index,
    holder_table_row,
    channel_input_weight,
    input_state_weight,
    output_state_weight,
    step_size_weight,
    channel_input_taps,
    input_state_taps,
    output_state_taps,
    adapter_down_weight,
    adapter_up_weight,
    decay_logarithm,
    step_size_bias,
    head_skip_factor,
):
    sources = lax.axis_size("adapter")
    me = lax.axis_index("adapter")
    calls, length, width = call_token_inputs.shape
    cols = channel_input_weight.shape[1]
    heads = decay_logarithm.shape[0]
    chunks = calls // CHUNK
    rows = CHUNK * length
    total_cols = cols + 2 * NSTATE
    meta = routing(
        routed_group_index, call_adapter_index, holder_table_row, me, sources, calls
    )
    down = jnp.swapaxes(adapter_down_weight, 1, 2)
    per_owner, rank, depth = down.shape
    rank_all = adapter_up_weight.shape[1]
    vmem = pl.BlockSpec(memory_space=pltpu.VMEM)
    anywhere = pl.BlockSpec(memory_space=pl.ANY)
    dma = pltpu.SemaphoreType.DMA
    return pl.pallas_call(
        mixer_kernel,
        out_shape=pltpu.VMEM((sources * CAP, length, cols), BF16),
        in_specs=[pl.BlockSpec(memory_space=pltpu.SMEM)] * 2 + [vmem] * 6 + [anywhere] * 6,
        out_specs=pl.BlockSpec(memory_space=pl.ANY),
        scratch_shapes=[
            pltpu.VMEM((calls, length, width), BF16),
            pltpu.VMEM((RING, calls, length, width), BF16),
            pltpu.VMEM((depth, total_cols), BF16),
            pltpu.VMEM((128, depth), BF16),
            pltpu.VMEM((sources, per_owner, rank, depth), BF16),
            pltpu.VMEM((sources, per_owner, rank_all, cols), BF16),
            pltpu.VMEM((chunks, CHUNK, PAD + length, cols), F32),
            pltpu.VMEM((CHUNK, PAD + length, 2 * NSTATE), F32),
            pltpu.VMEM((chunks, cols // 128, rows, 2 * rows), BF16),
            pltpu.VMEM((RING, chunks, rows, 128), BF16),
            pltpu.VMEM((CHUNK * rank, depth), BF16),
            pltpu.VMEM((sources * CAP, length, cols), BF16),
            pltpu.VMEM((8, 128), F32),
            pltpu.VMEM((4, total_cols), F32),
            dma((7,)),
            dma((4, chunks)),
            dma((4, chunks)),
            dma((2, N_TABLE)),
            dma((2, N_TABLE)),
            dma((RING - 1, chunks)),
            dma((RING - 1, chunks)),
            dma((sources,)),
            dma((sources,)),
        ],
        compiler_params=pltpu.CompilerParams(
            collective_id=0, has_side_effects=True, vmem_limit_bytes=56 * 2**20
        ),
        cost_estimate=pl.CostEstimate(
            flops=2 * calls * length * depth * (total_cols + 128),
            bytes_accessed=30 * 2**20,
            transcendentals=calls * length * rows * heads,
        ),
    )(
        meta,
        head_skip_factor,
        decay_logarithm[None, :],
        step_size_bias[None, :],
        channel_input_taps,
        input_state_taps,
        output_state_taps,
        step_size_weight.T,
        call_token_inputs,
        channel_input_weight,
        input_state_weight,
        output_state_weight,
        down,
        adapter_up_weight,
    )


def solution(mesh):
    placed = (
        P("adapter", None, "head"),
        P(),
        P(),
        P(),
        P(None, "head"),
        P(None, "head"),
        P(None, "head"),
        P(None, "head"),
        P(None, "head"),
        P(None, "head"),
        P(None, "head"),
        P("adapter", None, "head"),
        P("adapter", None, "head"),
        P("head"),
        P("head"),
        P("head"),
    )
    return jax.shard_map(
        on_device, mesh=mesh, in_specs=placed, out_specs=P("adapter", None, "head"), check_vma=False
    )
```

```python
import functools

import jax
import jax.numpy as jnp
from jax import lax
from jax.experimental import pallas as pl
from jax.experimental.pallas import tpu as pltpu
from jax.sharding import PartitionSpec as P

HEAD_DIM = 64
NSTATE = 128
CAP = 2
CHUNK = 4
PAD = 8
RING = 4
MESH = pl.DeviceIdType.MESH
HIGH = lax.Precision.HIGHEST
F32 = jnp.float32
BF16 = jnp.bfloat16

OFFSETS = (0, -1, 1, 2)
N_TABLE = 4 + 16 + 16

CHIP_STEPS = (
    ((2, 1), (2, 3), (1, 2), (3, 2)),
    ((2, 2), (2, 0), (0, 2)),
    ((1, 1), (3, 3), (1, 3), (3, 1)),
    ((1, 0), (3, 0), (0, 1), (0, 3)),
    ((0, 0),),
)
STEPS = (
    (2, 1, 1),
    (2, 3, 1),
    (1, 2, 1),
    (3, 2, 1),
    (2, 1, 0),
    (2, 3, 0),
    (1, 2, 0),
    (3, 2, 0),
    (2, 2, 1),
    (2, 0, 1),
    (0, 2, 1),
    (2, 2, 0),
    (2, 0, 0),
    (0, 2, 0),
    (1, 1, 1),
    (3, 3, 1),
    (0, 0, 1),
    (0, 0, 0),
    (1, 0, 1),
    (3, 0, 1),
    (0, 1, 1),
    (0, 3, 1),
    (1, 3, 1),
    (3, 1, 1),
    (1, 1, 0),
    (3, 3, 0),
    (1, 3, 0),
    (3, 1, 0),
    (1, 0, 0),
    (3, 0, 0),
    (0, 1, 0),
    (0, 3, 0),
)
TABLES_AT = 4
FINISH = ((4, 0, 2), (5, 2, 4), (6, 4, 5), (7, 5, 6), (8, 6, 8))


def nt_dot(a, b):
    return lax.dot_general(a, b, (((1,), (1,)), ((), ())), preferred_element_type=F32)


class Table:
    def __init__(self, buf, send, recv, first, second, core, strides, axes_to_adapter):
        self.buf, self.send, self.recv = buf, send, recv
        self.first, self.second, self.core = first, second, core
        self.strides = strides
        self.to_adapter = axes_to_adapter

    def owner(self, df, ds, core=None):
        core = self.core if core is None else core
        a = lax.rem(self.first + (df + RING), RING)
        b = lax.rem(self.second + (ds + RING), RING)
        return a * self.strides[0] + b * self.strides[1] + core

    def unit(self, df, ds, part=None, core=None):
        ref = self.buf.at[self.owner(df, ds, core)]
        return ref if part is None else ref.at[part]

    def copy(self, ref, index, target):
        return pltpu.make_async_remote_copy(
            src_ref=ref,
            dst_ref=ref,
            send_sem=self.send.at[index],
            recv_sem=self.recv.at[index],
            device_id={"adapter": target},
            device_id_type=MESH,
        )

    def plain(self, df):
        return 0 if df is None else 4 + 4 * OFFSETS.index(df)

    def send_plain(self, df):
        base = self.plain(df)
        if df is None:
            self.copy(self.unit(0, 0), base, self.owner(1, 0)).start()
            self.copy(self.unit(0, 0), base + 1, self.owner(-1, 0)).start()
        else:
            self.copy(self.unit(df, 0), base, self.owner(0, 1)).start()
            self.copy(self.unit(df, 0), base + 1, self.owner(0, -1)).start()

    def got_plain(self, df):
        base = self.plain(df)
        here = self.owner(0, 0)
        if df is None:
            self.copy(self.unit(-1, 0), base, here).wait_recv()
            self.copy(self.unit(1, 0), base + 1, here).wait_recv()
        else:
            self.copy(self.unit(df, -1), base, here).wait_recv()
            self.copy(self.unit(df, 1), base + 1, here).wait_recv()

    def send_relay(self, df):
        base = self.plain(df) + 2
        if df is None:
            self.copy(self.unit(-1, 0, 0), base, self.owner(1, 0)).start()
            self.copy(self.unit(1, 0, 1), base + 1, self.owner(-1, 0)).start()
        else:
            self.copy(self.unit(df, -1, 0), base, self.owner(0, 1)).start()
            self.copy(self.unit(df, 1, 1), base + 1, self.owner(0, -1)).start()

    def got_relay(self, df):
        base = self.plain(df) + 2
        here = self.owner(0, 0)
        at = (2, 0) if df is None else (df, 2)
        self.copy(self.unit(*at, 0), base, here).wait_recv()
        self.copy(self.unit(*at, 1), base + 1, here).wait_recv()

    def twin_index(self, df, ds):
        return 20 + 4 * OFFSETS.index(df) + OFFSETS.index(ds)

    def send_twin(self, df, ds):
        self.copy(
            self.unit(df, ds), self.twin_index(df, ds), self.owner(0, 0, 1 - self.core)
        ).start()

    def got_twins(self):
        here = self.owner(0, 0)
        for df in OFFSETS:
            for ds in OFFSETS:
                self.copy(
                    self.unit(df, ds, core=1 - self.core), self.twin_index(df, ds), here
                ).wait_recv()

    def sent_all(self):
        here = self.owner(0, 0)
        for df in (None, *OFFSETS):
            base = self.plain(df)
            for i in (0, 1):
                self.copy(self.unit(0, 0), base + i, here).wait_send()
                self.copy(self.unit(0, 0, 0), base + 2 + i, here).wait_send()
        for i in range(16):
            self.copy(self.unit(0, 0), 20 + i, here).wait_send()

    def event(self, number):
        if number == 0:
            self.send_plain(None)
            self.send_plain(0)
            self.send_twin(0, 0)
        elif number == 1:
            self.got_plain(None)
            self.send_relay(None)
            self.send_plain(-1)
            self.send_plain(1)
            self.got_plain(0)
            self.send_relay(0)
            for at in ((-1, 0), (1, 0), (0, -1), (0, 1)):
                self.send_twin(*at)
        elif number == 2:
            self.got_relay(None)
            self.send_plain(2)
            self.send_twin(2, 0)
            self.got_relay(0)
            self.send_twin(0, 2)
        elif number == 3:
            for df in (-1, 1):
                self.got_plain(df)
                self.send_relay(df)
                self.send_twin(df, -1)
                self.send_twin(df, 1)
        elif number == 4:
            self.got_plain(2)
            self.send_relay(2)
            self.send_twin(2, -1)
            self.send_twin(2, 1)
            for df in (-1, 1):
                self.got_relay(df)
                self.send_twin(df, 2)
        elif number == 5:
            self.got_relay(2)
            self.send_twin(2, 2)


N_EVENTS = 6


def mixer_kernel(
    meta,
    skip,
    decay_in,
    bias_in,
    x_taps,
    b_taps,
    c_taps,
    wdt_in,
    x_hbm,
    wx_hbm,
    wb_hbm,
    wc_hbm,
    down_hbm,
    up_hbm,
    out_hbm,
    x_in,
    x_all,
    w_all,
    wdt,
    down,
    up,
    proj,
    between,
    mixing,
    low,
    gathered,
    slots,
    params,
    taps,
    load_sem,
    y_send,
    y_recv,
    table_send,
    table_recv,
    low_send,
    low_recv,
    out_send,
    out_recv,
):
    sources = lax.axis_size("adapter")
    me = lax.axis_index("adapter")
    y = lax.axis_index("head")
    calls, length, width = x_in.shape
    chunks = calls // CHUNK
    rows = CHUNK * length
    cols = wx_hbm.shape[1]
    half = CHUNK // 2
    right, left = lax.rem(y + 1, RING), lax.rem(y + RING - 1, RING)
    across = lax.rem(y + 2, RING)
    core = lax.rem(me, 2)
    pos_z = lax.rem(lax.div(me, 2), RING)
    pos_x = lax.div(me, 2 * RING)

    loads = [
        pltpu.make_async_copy(x_hbm, x_in, load_sem.at[0]),
        pltpu.make_async_copy(down_hbm, down.at[me], load_sem.at[1]),
        pltpu.make_async_copy(up_hbm, up.at[me], load_sem.at[2]),
        pltpu.make_async_copy(wx_hbm, w_all.at[:, pl.ds(0, cols)], load_sem.at[3]),
        pltpu.make_async_copy(wb_hbm, w_all.at[:, pl.ds(cols, NSTATE)], load_sem.at[4]),
        pltpu.make_async_copy(
            wc_hbm, w_all.at[:, pl.ds(cols + NSTATE, NSTATE)], load_sem.at[5]
        ),
    ]
    for load in loads[:3]:
        load.start()

    barrier = pltpu.get_barrier_semaphore()

    def greet(i, carry):
        pl.semaphore_signal(
            barrier,
            inc=1,
            device_id={"adapter": lax.rem(me + i, sources)},
            device_id_type=MESH,
        )
        return carry

    lax.fori_loop(1, sources, greet, 0)
    for d in range(1, RING):
        pl.semaphore_signal(
            barrier,
            inc=1,
            device_id={"head": lax.rem(y + d, RING)},
            device_id_type=MESH,
        )

    def arrange(j, carry):
        x_all[y, j] = x_in[meta[0, j]]
        return carry

    loads[0].wait()
    lax.fori_loop(0, 2 * CHUNK, arrange, 0)
    pl.semaphore_wait(barrier, sources - 1 + RING - 1)

    def y_copy(kind, owner, k, target):
        if kind < 2:
            ref = x_all.at[owner, pl.ds(k * CHUNK, CHUNK)]
        else:
            ref = x_all.at[owner, pl.ds(k * CHUNK + (kind - 2) * half, half)]
        return pltpu.make_async_remote_copy(
            src_ref=ref,
            dst_ref=ref,
            send_sem=y_send.at[kind, k],
            recv_sem=y_recv.at[kind, k],
            device_id={"head": target},
            device_id_type=MESH,
        )

    def send_own(k):
        y_copy(0, y, k, right).start()
        y_copy(1, y, k, left).start()

    send_own(0)
    send_own(1)

    table_down = Table(
        down, table_send.at[0], table_recv.at[0], pos_x, pos_z, core, (2 * RING, 2), None
    )
    table_up = Table(
        up, table_send.at[1], table_recv.at[1], pos_z, pos_x, core, (2, 2 * RING), None
    )
    tables = (table_down, table_up)
    loads[1].wait()
    loads[2].wait()
    for table in tables:
        table.event(0)
    for load in loads[3:]:
        load.start()
    lax.fori_loop(2 * CHUNK, calls, arrange, 0)
    send_own(2)


    for c in range(CHUNK):
        between[c, pl.ds(0, PAD), :] = jnp.zeros((PAD, 2 * NSTATE), F32)
        for k in range(chunks):
            proj[k, c, pl.ds(0, PAD), :] = jnp.zeros((PAD, cols), F32)
    wdt[...] = jnp.zeros(wdt.shape, BF16)
    heads = wdt_in.shape[0]
    wdt[pl.ds(0, heads), :] = wdt_in[...]
    params[...] = jnp.zeros(params.shape, F32)
    params[0:1, pl.ds(0, heads)] = decay_in[...]
    params[1:2, pl.ds(0, heads)] = bias_in[...]
    taps[:, pl.ds(0, cols)] = x_taps[...].astype(F32)
    taps[:, pl.ds(cols, NSTATE)] = b_taps[...].astype(F32)
    taps[:, pl.ds(cols + NSTATE, NSTATE)] = c_taps[...].astype(F32)
    loads[3].wait()
    loads[4].wait()
    loads[5].wait()

    done = x_in
    rank = down.shape[2]
    rank_all = up.shape[2]
    decay_rate = -jnp.exp(params[0:1, :])
    bias = params[1:2, :]

    def chunk_tokens(owner, k):
        return x_all[owner, pl.ds(k * CHUNK, CHUNK)].reshape(rows, width)

    def project(k, weight, at, owners=(0, 1, 2, 3)):
        total = None
        for owner in owners:
            term = jnp.dot(
                chunk_tokens(owner, k),
                weight[pl.ds(pl.multiple_of(owner * width, width), width), at],
                preferred_element_type=F32,
            )
            total = term if total is None else total + term
        return total

    def conv(series, at, taps_at):
        total = jnp.zeros((CHUNK, length, 128), F32)
        for i in range(4):
            total = total + taps[pl.ds(i, 1), taps_at].reshape(1, 1, 128) * series[
                :, pl.ds(PAD - 3 + i, length), at
            ]
        total = total.reshape(rows, 128)
        return total / (1.0 + jnp.exp(-total))

    tile = 256 if cols % 256 == 0 else 128

    def project_near(k):
        @pl.loop(0, cols // tile)
        def _(n):
            at = pl.ds(pl.multiple_of(n * tile, tile), tile)
            proj[k, :, pl.ds(PAD, length), at] = project(
                k, w_all, at, (y, left, right)
            ).reshape(CHUNK, length, tile)

    def before_adapters(k):
        @pl.loop(0, cols // tile)
        def _(n):
            at = pl.ds(pl.multiple_of(n * tile, tile), tile)
            proj[k, :, pl.ds(PAD, length), at] = proj[
                k, :, pl.ds(PAD, length), at
            ] + project(k, w_all, at, (across,)).reshape(CHUNK, length, tile)

        between[:, pl.ds(PAD, length), :] = project(
            k, w_all, pl.ds(cols, 2 * NSTATE)
        ).reshape(CHUNK, length, 2 * NSTATE)
        raw = bias
        for owner in range(RING):
            raw = raw + nt_dot(chunk_tokens(owner, k), wdt[:, pl.ds(owner * width, width)])
        t_iota = lax.broadcasted_iota(jnp.int32, (rows, rows), 0)
        j_iota = lax.broadcasted_iota(jnp.int32, (rows, rows), 1)
        causal = (t_iota // length == j_iota // length) & (j_iota <= t_iota)
        dt = jnp.maximum(raw, 0.0) + jnp.log1p(jnp.exp(-jnp.abs(raw)))
        cum = jnp.dot(
            jnp.where(causal, 1.0, 0.0),
            decay_rate * dt,
            preferred_element_type=F32,
            precision=HIGH,
        )
        cum_t = cum.T
        dt_t = dt.T
        b_conv = conv(between, pl.ds(0, NSTATE), pl.ds(cols, NSTATE))
        c_conv = conv(between, pl.ds(NSTATE, NSTATE), pl.ds(cols + NSTATE, NSTATE))
        marks = lax.dot_general(
            c_conv,
            b_conv,
            (((1,), (1,)), ((), ())),
            preferred_element_type=F32,
            precision=HIGH,
        )
        for h in range(cols // HEAD_DIM):
            segment = cum[:, h : h + 1] - cum_t[h : h + 1, :]
            decay = jnp.exp(jnp.where(causal, segment, -1e30))
            mixing[k, h // 2, :, pl.ds((h % 2) * rows, rows)] = (
                marks * decay * dt_t[h : h + 1, :]
            ).astype(BF16)

    def low_copy(owner, d, k, target):
        ref = low.at[owner, k]
        return pltpu.make_async_remote_copy(
            src_ref=ref,
            dst_ref=ref,
            send_sem=low_send.at[d - 1, k],
            recv_sem=low_recv.at[d - 1, k],
            device_id={"head": target},
            device_id_type=MESH,
        )

    def reduce_chunk(k, carry):
        for c in range(CHUNK):
            row = meta[1, k * CHUNK + c]
            gathered[pl.ds(c * rank, rank), :] = down[lax.div(row, 2), lax.rem(row, 2)]
        total = jnp.zeros((rows, CHUNK * rank), F32)
        for owner in range(RING):
            total = total + nt_dot(
                chunk_tokens(owner, k), gathered[:, pl.ds(owner * width, width)]
            )
        row_call = lax.broadcasted_iota(jnp.int32, total.shape, 0) // length
        lane_call = lax.broadcasted_iota(jnp.int32, total.shape, 1) // rank
        kept = jnp.where(row_call == lane_call, total, 0.0).astype(BF16)
        shape = (CHUNK * rank, low.shape[3])
        from_rank = lax.broadcasted_iota(jnp.int32, shape, 0) % rank + y * rank
        fold = jnp.where(
            from_rank == lax.broadcasted_iota(jnp.int32, shape, 1), 1.0, 0.0
        ).astype(BF16)
        low[y, k] = jnp.dot(kept, fold, preferred_element_type=F32).astype(BF16)
        for d in range(1, RING):
            low_copy(y, d, k, lax.rem(y + d, RING)).start()
        return carry

    def at_step(i, sign):
        dx, dz, dc = STEPS[i]
        other = lax.rem(core + dc, 2)
        side = sign * (1 - 2 * (core if sign == 1 else other))
        return (
            lax.rem(pos_x + side * dx + RING, RING) * (2 * RING)
            + lax.rem(pos_z + side * dz + RING, RING) * 2
            + other
        )

    def out_copy(i, target, source):
        return pltpu.make_async_remote_copy(
            src_ref=slots.at[pl.ds(i * CAP, CAP)],
            dst_ref=out_hbm.at[pl.ds(source * CAP, CAP)],
            send_sem=out_send.at[i],
            recv_sem=out_recv.at[i],
            device_id={"adapter": target},
            device_id_type=MESH,
        )

    at_home = STEPS.index((0, 0, 0))
    own = pltpu.make_async_copy(
        slots.at[pl.ds(at_home * CAP, CAP)],
        out_hbm.at[pl.ds(me * CAP, CAP)],
        load_sem.at[6],
    )

    def send_slots(i):
        for r in range(CAP):
            at = i * CAP + r
            block = done[meta[2, at]].astype(F32)
            slots[at] = jnp.where(meta[3, at] > 0, block, 0.0).astype(BF16)
        if i == at_home:
            own.start()
        else:
            out_copy(i, at_step(i, 1), me).start()

    def after_adapters(k, carry):
        for d in range(1, RING):
            low_copy(lax.rem(y + RING - d, RING), d, k, y).wait_recv()
        low_rank = (
            low[0, k].astype(F32)
            + low[1, k].astype(F32)
            + low[2, k].astype(F32)
            + low[3, k].astype(F32)
        ).astype(BF16)
        for c in range(CHUNK):
            row = meta[1, k * CHUNK + c]
            weight = up[lax.div(row, 2), lax.rem(row, 2)]
            delta = jnp.dot(
                low_rank[c * length : (c + 1) * length, :rank_all],
                weight,
                preferred_element_type=F32,
            )
            proj[k, c, pl.ds(PAD, length), :] = proj[k, c, pl.ds(PAD, length), :] + delta
        lane = lax.broadcasted_iota(jnp.int32, (rows, 128), 1)
        for pair in range(cols // 128):
            at = pl.ds(pair * 128, 128)
            x_conv = conv(proj.at[k], at, at)
            x_high = x_conv.astype(BF16)
            mixed = jnp.where(lane < HEAD_DIM, skip[2 * pair], skip[2 * pair + 1]) * x_conv
            for part in (x_high.astype(F32), x_conv - x_high.astype(F32)):
                first = jnp.where(lane < HEAD_DIM, part, 0.0).astype(BF16)
                second = jnp.where(lane < HEAD_DIM, 0.0, part).astype(BF16)
                mixed = mixed + jnp.dot(
                    mixing[k, pair],
                    jnp.concatenate([first, second], axis=0),
                    preferred_element_type=F32,
                )
            done[pl.ds(k * CHUNK, CHUNK), :, at] = mixed.reshape(
                CHUNK, length, 128
            ).astype(BF16)
        for number in range(chunks):

            @pl.when(k == number)
            def _(number=number):
                for i in range(CHUNK // CAP):
                    send_slots(number * (CHUNK // CAP) + i)

        return carry

    last = chunks - 1

    def step(t, carry):
        @pl.when(t < chunks)
        def _():
            y_copy(0, left, t, y).wait_recv()
            y_copy(2, left, t, right).start()
            y_copy(1, right, t, y).wait_recv()
            y_copy(3, right, t, left).start()

        for number in range(1, TABLES_AT + 1):

            @pl.when(t == number)
            def _(number=number):
                for table in tables:
                    table.event(number)

        @pl.when(t > 0)
        def _():
            y_copy(2, across, t - 1, y).wait_recv()
            y_copy(3, across, t - 1, y).wait_recv()

        lax.fori_loop(jnp.where(t > TABLES_AT, t - 1, t), t, reduce_chunk, 0)

        @pl.when(t + 3 < chunks)
        def _():
            send_own(t + 3)

        @pl.when(t > 0)
        def _():
            before_adapters(t - 1)

        @pl.when(t == TABLES_AT)
        def _():
            for number in range(TABLES_AT + 1, N_EVENTS):
                for table in tables:
                    table.event(number)
            for table in tables:
                table.got_twins()

        lax.fori_loop(0, jnp.where(t == TABLES_AT, t, 0), reduce_chunk, 0)
        first, end = 0, 0
        for at, begin, until in FINISH:
            first = jnp.where(t == at, begin, first)
            end = jnp.where(t == at, until, end)
        lax.fori_loop(first, end, after_adapters, 0)

        @pl.when(t < chunks)
        def _():
            project_near(t)

        return carry

    lax.fori_loop(0, chunks + 1, step, 0)

    for i in range(calls // CAP, sources):
        send_slots(i)

    own.wait()
    for table in tables:
        table.sent_all()

    def drain(k, carry):
        for kind in range(4):
            y_copy(kind, y, k, y).wait_send()
        for d in range(1, RING):
            low_copy(y, d, k, y).wait_send()
        return carry

    lax.fori_loop(0, chunks, drain, 0)
    for i in range(sources):
        if i != at_home:
            out_copy(i, me, me).wait_send()
            out_copy(i, me, at_step(i, -1)).wait_recv()


def routing(routed_group_index, call_adapter_index, holder_table_row, me, sources, calls):
    group = lax.dynamic_slice(routed_group_index, (me * calls,), (calls,))
    named = lax.dynamic_slice(call_adapter_index[:, 0], (me * calls,), (calls,))
    call = jnp.arange(calls, dtype=jnp.int32)
    side = 1 - 2 * (me % 2)
    way = (
        lax.rem(side * (lax.shift_right_logical(group, 3) - me // (2 * RING)) + RING, RING)
        * (2 * RING)
        + lax.rem(side * ((lax.shift_right_logical(group, 1) & 3) - (me // 2) % RING) + RING, RING)
        * 2
        + ((group + me) & 1)
    )
    step = jnp.zeros((calls,), jnp.int32)
    for i, (dx, dz, dc) in enumerate(STEPS):
        step = jnp.where(way == dx * 2 * RING + dz * 2 + dc, i, step)
    key = step * calls + call
    place = jnp.sum(jnp.where(key[None, :] < key[:, None], 1, 0), axis=1)
    row = jnp.sum(
        jnp.where(
            named[:, None] == jnp.arange(holder_table_row.shape[0], dtype=jnp.int32)[None, :],
            holder_table_row[None, :],
            0,
        ),
        axis=1,
    )
    slot = jnp.arange(sources * CAP, dtype=jnp.int32)
    here = place[None, :] == slot[:, None]
    order = jnp.sum(jnp.where(here, call[None, :], 0), axis=1)
    rows = jnp.sum(jnp.where(here, row[None, :], 0), axis=1)
    slot_step, slot_rank = slot // CAP, slot % CAP
    ahead = jnp.sum(jnp.where(step[None, :] < slot_step[:, None], 1, 0), axis=1)
    count = jnp.sum(jnp.where(step[None, :] == slot_step[:, None], 1, 0), axis=1)
    taken = ahead + jnp.minimum(slot_rank, count)
    live = jnp.where(count > slot_rank, 1, 0)
    return jnp.stack([order, rows, jnp.minimum(taken, calls - 1), live]).astype(jnp.int32)


def on_device(
    call_token_inputs,
    routed_group_index,
    call_adapter_index,
    holder_table_row,
    channel_input_weight,
    input_state_weight,
    output_state_weight,
    step_size_weight,
    channel_input_taps,
    input_state_taps,
    output_state_taps,
    adapter_down_weight,
    adapter_up_weight,
    decay_logarithm,
    step_size_bias,
    head_skip_factor,
):
    sources = lax.axis_size("adapter")
    me = lax.axis_index("adapter")
    calls, length, width = call_token_inputs.shape
    cols = channel_input_weight.shape[1]
    heads = decay_logarithm.shape[0]
    chunks = calls // CHUNK
    rows = CHUNK * length
    total_cols = cols + 2 * NSTATE
    meta = routing(
        routed_group_index, call_adapter_index, holder_table_row, me, sources, calls
    )
    down = jnp.swapaxes(adapter_down_weight, 1, 2)
    per_owner, rank, depth = down.shape
    rank_all = adapter_up_weight.shape[1]
    vmem = pl.BlockSpec(memory_space=pltpu.VMEM)
    anywhere = pl.BlockSpec(memory_space=pl.ANY)
    dma = pltpu.SemaphoreType.DMA
    return pl.pallas_call(
        mixer_kernel,
        out_shape=pltpu.VMEM((sources * CAP, length, cols), BF16),
        in_specs=[pl.BlockSpec(memory_space=pltpu.SMEM)] * 2 + [vmem] * 6 + [anywhere] * 6,
        out_specs=pl.BlockSpec(memory_space=pl.ANY),
        scratch_shapes=[
            pltpu.VMEM((calls, length, width), BF16),
            pltpu.VMEM((RING, calls, length, width), BF16),
            pltpu.VMEM((depth, total_cols), BF16),
            pltpu.VMEM((128, depth), BF16),
            pltpu.VMEM((sources, per_owner, rank, depth), BF16),
            pltpu.VMEM((sources, per_owner, rank_all, cols), BF16),
            pltpu.VMEM((chunks, CHUNK, PAD + length, cols), F32),
            pltpu.VMEM((CHUNK, PAD + length, 2 * NSTATE), F32),
            pltpu.VMEM((chunks, cols // 128, rows, 2 * rows), BF16),
            pltpu.VMEM((RING, chunks, rows, 128), BF16),
            pltpu.VMEM((CHUNK * rank, depth), BF16),
            pltpu.VMEM((sources * CAP, length, cols), BF16),
            pltpu.VMEM((8, 128), F32),
            pltpu.VMEM((4, total_cols), F32),
            dma((7,)),
            dma((4, chunks)),
            dma((4, chunks)),
            dma((2, N_TABLE)),
            dma((2, N_TABLE)),
            dma((RING - 1, chunks)),
            dma((RING - 1, chunks)),
            dma((sources,)),
            dma((sources,)),
        ],
        compiler_params=pltpu.CompilerParams(
            collective_id=0, has_side_effects=True, vmem_limit_bytes=56 * 2**20
        ),
        cost_estimate=pl.CostEstimate(
            flops=2 * calls * length * depth * (total_cols + 128),
            bytes_accessed=30 * 2**20,
            transcendentals=calls * length * rows * heads,
        ),
    )(
        meta,
        head_skip_factor,
        decay_logarithm[None, :],
        step_size_bias[None, :],
        channel_input_taps,
        input_state_taps,
        output_state_taps,
        step_size_weight.T,
        call_token_inputs,
        channel_input_weight,
        input_state_weight,
        output_state_weight,
        down,
        adapter_up_weight,
    )


def solution(mesh):
    placed = (
        P("adapter", None, "head"),
        P(),
        P(),
        P(),
        P(None, "head"),
        P(None, "head"),
        P(None, "head"),
        P(None, "head"),
        P(None, "head"),
        P(None, "head"),
        P(None, "head"),
        P("adapter", None, "head"),
        P("adapter", None, "head"),
        P("head"),
        P("head"),
        P("head"),
    )
    return jax.shard_map(
        on_device, mesh=mesh, in_specs=placed, out_specs=P("adapter", None, "head"), check_vma=False
    )
```
